32 devices in a mesh: az: 16 (over z, x, core), rad: 2 (over y).
Axes of the slice: x: 2, y: 2, z: 4, core: 2. Of those that a mesh axis runs over, the one named last changes fastest.
Arguments:
- density: float32 [1024, 64, 512], P('az', 'rad'), may hold values from -10 to 10
Outputs:
- potential: float32 [1024, 64, 512], P('az', 'rad')
The draws below stay inside these ranges and needn't reach their ends.
All inputs are finite; a program needn't handle non-finite values.
Results may differ from the reference program's by a relative error of at most 0.000075.
Values sent between devices are 32-bit elements; how exact they have to be, the bound alone decides.
No kernel may reach another device: no remote copies, remote signals or barrier semaphores. Data moves between devices by JAX's collectives and lax.ppermute only.
A program may use at most 128 MiB of HBM per device.

```python
import jax
import jax.numpy as jnp
from jax import lax

NPHI = 1024
NZ = 512
PRE = 2
POST = 2
COARSE = 6
NR = 64


def draw_density(key, part):
    key = jax.random.fold_in(key, 11)
    rough_key = jax.random.fold_in(key, 0)
    shape = (NPHI, NR, NZ)
    return jnp.clip(jax.random.normal(rough_key, shape, jnp.float32), -6.0, 6.0)


def setup_inputs(seed: int = 0) -> dict:
    splits = jax.random.split(jax.random.key(seed), 2)
    return {
        "density": draw_density(jax.random.fold_in(splits[1], 71), 0),
    }


OMEGA = 0.8


def level_coefficients(first_row, row_count, spacing, mode_numbers):
    row_number = (jnp.arange(row_count, dtype=jnp.int32) + first_row).astype(jnp.float32)
    radius = spacing * (row_number + 0.5)
    outward = (row_number + 1.0) / (spacing * radius)
    inward = row_number / (spacing * radius)
    vertical = 1.0 / (spacing * spacing)
    diagonal = (outward + inward + 2.0 * vertical)[None, :] + (mode_numbers[:, None] / radius[None, :]) ** 2
    return diagonal[:, :, None], outward[None, :, None], inward[None, :, None], vertical


def apply_op(iterate, padded, coefficients):
    diagonal, outward, inward, vertical = coefficients
    return (diagonal * iterate - outward * padded[:, 2:, 1:-1] - inward * padded[:, :-2, 1:-1]
            - vertical * (padded[:, 1:-1, 2:] + padded[:, 1:-1, :-2]))


def relax(iterate, source, coefficients, pad_both):
    return iterate + OMEGA * (source - apply_op(iterate, pad_both(iterate), coefficients)) / coefficients[0]


def restrict(residual):
    k_count, r_count, z_count = residual.shape
    parts = residual.reshape(k_count, r_count // 2, 2, z_count // 2, 2)
    return 0.25 * (parts[:, :, 0, :, 0] + parts[:, :, 1, :, 0] + parts[:, :, 0, :, 1] + parts[:, :, 1, :, 1])


def prolong(correction):
    return jnp.repeat(jnp.repeat(correction, 2, axis=1), 2, axis=2)


def pad_local(field):
    return jnp.pad(field, ((0, 0), (1, 1), (1, 1)))


def vcycle(source, mode_numbers):
    row_total = source.shape[1]
    fine_coef = level_coefficients(0, row_total, 1.0, mode_numbers)
    coarse_coef = level_coefficients(0, row_total // 2, 2.0, mode_numbers)
    iterate = jnp.zeros_like(source)
    for sweep_index in range(PRE):
        iterate = relax(iterate, source, fine_coef, pad_local)
    residual = source - apply_op(iterate, pad_local(iterate), fine_coef)
    coarse_source = restrict(residual)
    correction = jnp.zeros_like(coarse_source)
    for sweep_index in range(COARSE):
        correction = relax(correction, coarse_source, coarse_coef, pad_local)
    iterate = iterate + prolong(correction)
    for sweep_index in range(POST):
        iterate = relax(iterate, source, fine_coef, pad_local)
    return iterate


def reference(density):
    spectrum = jnp.fft.rfft(density, axis=0)
    half_count = NPHI // 2 + 1
    stacked = jnp.concatenate([jnp.real(spectrum), jnp.imag(spectrum)], axis=0).astype(jnp.float32)
    mode_numbers = jnp.concatenate([jnp.arange(half_count), jnp.arange(half_count)]).astype(jnp.float32)

    def solve_plane(inputs):
        mode_plane, mode_number = inputs
        return vcycle(-mode_plane[None], mode_number[None])[0]

    solved = lax.map(solve_plane, (stacked, mode_numbers))
    combined = lax.complex(solved[:half_count], solved[half_count:])
    return jnp.fft.irfft(combined, n=NPHI, axis=0).astype(jnp.float32)
```

```python
import math

import jax
import jax.numpy as jnp
import numpy as np
from jax import lax
from jax.experimental import pallas as pl
from jax.experimental.pallas import tpu as pltpu
from jax.sharding import PartitionSpec as P

PRE = 2
POST = 2
COARSE = 6


OMEGA = 0.8

LANES = 128
TILE = 8
DEEP = 2 * COARSE + 2
NEAR = 3
FAR = COARSE
VMEM_LIMIT = 56 * 1024 * 1024


def with_halo(cells, sides, width):
    for axis, dim in sides:
        count = lax.axis_size(axis)
        ends = count - 1
        head = lax.slice_in_dim(cells, 0, width, axis=dim)
        tail = lax.slice_in_dim(cells, cells.shape[dim] - width, cells.shape[dim], axis=dim)
        cells = jnp.concatenate(
            [
                lax.ppermute(tail, axis, [(i, (i + 1) % count) for i in range(ends)]),
                cells,
                lax.ppermute(head, axis, [((i + 1) % count, i) for i in range(ends)]),
            ],
            axis=dim,
        )
    return cells


def level_coefficients(first_row, row_count, spacing, mode_numbers):
    row_number = (jnp.arange(row_count, dtype=jnp.int32) + first_row).astype(jnp.float32)
    radius = spacing * (row_number + 0.5)
    outward = (row_number + 1.0) / (spacing * radius)
    inward = row_number / (spacing * radius)
    vertical = 1.0 / (spacing * spacing)
    diagonal = (outward + inward + 2.0 * vertical)[None, :] + (
        mode_numbers[:, None] / radius[None, :]
    ) ** 2
    return (diagonal[:, :, None], outward[None, :, None], inward[None, :, None], vertical)


def apply_op(iterate, padded, coefficients):
    diagonal, outward, inward, vertical = coefficients
    return (
        diagonal * iterate
        - outward * padded[:, 2:, 1:-1]
        - inward * padded[:, :-2, 1:-1]
        - vertical * (padded[:, 1:-1, 2:] + padded[:, 1:-1, :-2])
    )


def relax(iterate, source, coefficients, pad_both):
    return (
        iterate
        + OMEGA * (source - apply_op(iterate, pad_both(iterate), coefficients)) / coefficients[0]
    )


def restrict(residual):
    k_count, r_count, z_count = residual.shape
    parts = residual.reshape(k_count, r_count // 2, 2, z_count // 2, 2)
    return 0.25 * (
        parts[:, :, 0, :, 0] + parts[:, :, 1, :, 0] + parts[:, :, 0, :, 1] + parts[:, :, 1, :, 1]
    )


def prolong(correction):
    return jnp.repeat(jnp.repeat(correction, 2, axis=1), 2, axis=2)


def pad_level(field):
    rows = with_halo(field, (("rad", 1),), 1)
    return jnp.pad(rows, ((0, 0), (0, 0), (1, 1)))


def mode_values(mode_index, azimuths):
    return jnp.where(mode_index <= azimuths // 2, mode_index, mode_index - azimuths // 2).astype(
        jnp.float32
    )


def fine_cycle(source, fine_coef, pad_sweep, coarse_solve):
    iterate = OMEGA * source / fine_coef[0]
    for sweep_index in range(PRE - 1):
        iterate = relax(iterate, source, fine_coef, pad_sweep)
    residual = source - apply_op(iterate, pad_sweep(iterate), fine_coef)
    iterate = iterate + prolong(coarse_solve(restrict(residual)))
    for sweep_index in range(POST):
        iterate = relax(iterate, source, fine_coef, pad_sweep)
    return iterate


def general_body(density):
    local_phi, local_rows, vertical_cells = density.shape
    az_count = lax.axis_size("az")
    azimuths = local_phi * az_count
    cell_count = local_rows * vertical_cells // az_count
    numbers = jnp.arange(azimuths, dtype=jnp.int32)
    all_modes = jnp.where(numbers <= azimuths // 2, numbers, numbers - azimuths // 2)
    phase = all_modes[:, None] * numbers[None, :] % azimuths
    phase_angle = phase.astype(jnp.float32) * (2.0 * math.pi / azimuths)
    analysis_table = jnp.where(
        (numbers <= azimuths // 2)[:, None], jnp.cos(phase_angle), jnp.sin(phase_angle)
    )
    synth_weight = jnp.where(
        (numbers == 0) | (numbers == azimuths // 2), 1.0 / azimuths, 2.0 / azimuths
    )
    synthesis_table = analysis_table.T * synth_weight[None, :]

    def transform_with(table, columns):
        width = columns.shape[2]
        matrix = columns.reshape(azimuths, width)
        result = jnp.dot(
            table, matrix, precision=lax.Precision.HIGHEST, preferred_element_type=jnp.float32
        )
        return result.reshape(azimuths, 1, width)

    lines = density.reshape(local_phi, az_count, cell_count)
    spectral = transform_with(
        analysis_table, lax.all_to_all(lines, "az", split_axis=1, concat_axis=0, tiled=True)
    )
    coefficients = lax.all_to_all(spectral, "az", split_axis=0, concat_axis=1, tiled=True)
    source = -coefficients.reshape(local_phi, local_rows, vertical_cells)
    rad_index = lax.axis_index("rad")
    half_rows = local_rows // 2
    mode_index = lax.axis_index("az") * local_phi + jnp.arange(local_phi, dtype=jnp.int32)
    mode_numbers = mode_values(mode_index, azimuths)
    fine_coef = level_coefficients(rad_index * local_rows, local_rows, 1.0, mode_numbers)
    coarse_coef = level_coefficients(rad_index * half_rows, half_rows, 2.0, mode_numbers)

    def coarse_halo(coarse_source):
        correction = OMEGA * coarse_source / coarse_coef[0]
        for sweep_index in range(COARSE - 1):
            correction = relax(correction, coarse_source, coarse_coef, pad_level)
        return correction

    iterate = fine_cycle(source, fine_coef, pad_level, coarse_halo)
    mode_lines = iterate.reshape(local_phi, az_count, cell_count)
    physical = transform_with(
        synthesis_table, lax.all_to_all(mode_lines, "az", split_axis=1, concat_axis=0, tiled=True)
    )
    field = lax.all_to_all(physical, "az", split_axis=0, concat_axis=1, tiled=True)
    return field.reshape(local_phi, local_rows, vertical_cells)


def mode_tables(azimuths):
    half = azimuths // 2
    even = np.concatenate([np.arange(0, half + 1, 2), np.arange(2, half, 2)])
    odd = np.concatenate([np.arange(1, half, 2), np.arange(1, half, 2)])
    even_cos = np.arange(half) <= half // 2
    odd_cos = np.arange(half) < half // 2
    modes = np.concatenate([even, odd])
    is_cos = np.concatenate([even_cos, odd_cos])
    angle = 2.0 * np.pi / azimuths * (np.arange(half)[:, None] * modes[None, :] % azimuths)
    values = np.where(is_cos[None, :], np.cos(angle), np.sin(angle))
    weight = np.where((modes == 0) | (modes == half), 1.0, 2.0) / azimuths
    return modes.astype(np.float32), -values, values * weight[None, :]


def high_low(values):
    values = values.astype(np.float32)
    high = values.astype(jnp.bfloat16)
    low = (values - high.astype(np.float32)).astype(jnp.bfloat16)
    return jnp.asarray(high), jnp.asarray(low)


def split_value(value):
    high = value.astype(jnp.bfloat16)
    return high, (value - high.astype(jnp.float32)).astype(jnp.bfloat16)


def swap_chunks(parts, chunk):
    count = len(parts)
    parts = list(parts)
    lane = lax.broadcasted_iota(jnp.int32, parts[0].shape, parts[0].ndim - 1) // chunk
    span = count // 2
    while span:
        keep = (lane & span) == 0
        for i in range(count):
            if i & span:
                continue
            a, b = parts[i], parts[i + span]
            axis = a.ndim - 1
            parts[i] = jnp.where(keep, a, pltpu.roll(b, span * chunk, axis))
            parts[i + span] = jnp.where(keep, pltpu.roll(a, LANES - span * chunk, axis), b)
        span //= 2
    return parts


def tile_row(pos_ref, row):
    return jnp.where(pos_ref[0] == 0, TILE - 1 - row, row)


def pack_kernel(block, pos_ref, x_ref, o_ref):
    rows = LANES // block
    local_phi = x_ref.shape[0]
    flat = x_ref.reshape(local_phi * TILE, LANES)
    for group in range(TILE // rows):
        parts = [
            flat[pl.ds(tile_row(pos_ref, group * rows + i), local_phi, stride=TILE), :]
            for i in range(rows)
        ]
        for q, part in enumerate(swap_chunks(parts, block)):
            o_ref[q, group] = part


def unpack_kernel(block, pos_ref, x_ref, o_ref):
    rows = LANES // block
    local_phi = o_ref.shape[0]
    flat = o_ref.reshape(local_phi * TILE, LANES)
    for group in range(TILE // rows):
        parts = [x_ref[q, group] for q in range(rows)]
        for i, part in enumerate(swap_chunks(parts, block)):
            flat[pl.ds(tile_row(pos_ref, group * rows + i), local_phi, stride=TILE), :] = part


def analysis_kernel(x_ref, high_ref, low_ref, o_ref, edge_ref=None):
    sources, groups, width, lanes = x_ref.shape
    half = sources // 2 * width
    rows, cells = o_ref.shape[0], o_ref.shape[1]
    for parity in range(2):
        turned = []
        for group in range(groups):
            near, far = x_ref[: sources // 2, group], x_ref[sources // 2 :, group]
            folded = near + far if parity == 0 else near - far
            turned.append(folded.reshape(half, lanes).T)
        high, low = split_value(jnp.concatenate(turned, axis=0))
        columns = slice(parity * half, (parity + 1) * half)
        t_high, t_low = high_ref[:, columns], low_ref[:, columns]
        result = (
            jnp.dot(high, t_high, preferred_element_type=jnp.float32)
            + jnp.dot(high, t_low, preferred_element_type=jnp.float32)
            + jnp.dot(low, t_high, preferred_element_type=jnp.float32)
        )
        for part in range(half // LANES):
            piece = result[:, part * LANES : (part + 1) * LANES]
            o_ref[:, :, parity * (half // LANES) + part, :] = piece.reshape(rows, cells, LANES)
    if edge_ref is not None:
        for step in range(-(-DEEP // rows)):

            @pl.when(pl.program_id(0) == step)
            def _():
                for row in range(rows):
                    if step * rows + row < DEEP:
                        edge_ref[DEEP - 1 - step * rows - row] = o_ref[row]


def synthesis_kernel(u_ref, high_ref, low_ref, o_ref):
    rows, cells = u_ref.shape[0], u_ref.shape[1]
    half = high_ref.shape[0]
    parts = half // LANES
    sums = []
    for parity in range(2):
        field = jnp.concatenate(
            [u_ref[:, :, parity * parts + i, :].reshape(rows * cells, LANES) for i in range(parts)],
            axis=1,
        )
        high, low = split_value(field)
        columns = slice(parity * half, (parity + 1) * half)
        t_high, t_low = high_ref[:, columns], low_ref[:, columns]
        contract = (((1,), (1,)), ((), ()))
        sums.append(
            lax.dot_general(t_high, high, contract, preferred_element_type=jnp.float32)
            + lax.dot_general(t_high, low, contract, preferred_element_type=jnp.float32)
            + lax.dot_general(t_low, high, contract, preferred_element_type=jnp.float32)
        )
    near, far = sums[0] + sums[1], sums[0] - sums[1]
    targets, groups, width, lanes = o_ref.shape
    for group in range(groups):
        columns = slice(group * lanes, (group + 1) * lanes)
        o_ref[: targets // 2, group] = near[:, columns].reshape(targets // 2, width, lanes)
        o_ref[targets // 2 :, group] = far[:, columns].reshape(targets // 2, width, lanes)


def row_weights(upper, boundary, first, count, squares_ref, c_ref, ahead_ref, behind_ref):
    def one(index, carry):
        row = jnp.where(upper, index + (boundary + first), (boundary - 1 - first) - index)
        number = jnp.full(squares_ref.shape, row, jnp.int32).astype(jnp.float32)
        radius = number + 0.5
        outward = (number + 1.0) / radius
        inward = number / radius
        diagonal = outward + inward + 2.0 + squares_ref[...] / (radius * radius)
        c_ref[index] = OMEGA / diagonal
        ahead_ref[index] = jnp.where(upper, outward, inward)
        behind_ref[index] = jnp.where(upper, inward, outward)
        return carry

    lax.fori_loop(0, count, one, 0)


def cell_tiles(first, last, cells, size=16):
    tiles = []
    if first < 0:
        tiles.append((first, -first, -1))
    for start in range(max(first, 0), min(last, cells), size):
        tiles.append((start, min(size, min(last, cells) - start), 0))
    if last > cells:
        tiles.append((cells, last - cells, 1))
    return tiles


def sweep(rows, cells, block, src, source, dst, weights, masks):
    (src_ref, src_t, src_z), (g_ref, g_t, g_z), (dst_ref, dst_t, dst_z) = src, source, dst
    c_ref, ahead_ref, behind_ref, w_t = weights
    low = rows[0]

    def one(step, carry):
        at = step + (low - w_t)
        c_row, ahead, behind = c_ref[at], ahead_ref[at], behind_ref[at]
        for first, count, side in cell_tiles(cells[0], cells[1], block):
            c = c_row if side == 0 else c_row * masks[0 if side < 0 else 1]
            z = first - src_z
            row = low - src_t
            middle = src_ref[step + row, z - 1 : z + count + 1]
            gathered = (
                g_ref[step + (low - g_t), first - g_z : first - g_z + count]
                + ahead * src_ref[step + (row + 1), z : z + count]
                + behind * src_ref[step + (row - 1), z : z + count]
                + (middle[:-2] + middle[2:])
            )
            dst_ref[step + (low - dst_t), first - dst_z : first - dst_z + count] = (
                (1.0 - OMEGA) * middle[1:-1] + c * gathered
            )
        return carry

    lax.fori_loop(0, rows[1] - low, one, 0)


def first_sweep(rows, cells, block, source, dst, weights, masks):
    (g_ref, g_t, g_z), (dst_ref, dst_t, dst_z) = source, dst
    c_ref, w_t = weights[0], weights[3]
    low = rows[0]

    def one(step, carry):
        c_row = c_ref[step + (low - w_t)]
        for first, count, side in cell_tiles(cells[0], cells[1], block):
            c = c_row if side == 0 else c_row * masks[0 if side < 0 else 1]
            dst_ref[step + (low - dst_t), first - dst_z : first - dst_z + count] = (
                c * g_ref[step + (low - g_t), first - g_z : first - g_z + count]
            )
        return carry

    lax.fori_loop(0, rows[1] - low, one, 0)


def side_masks(pos_ref, shape):
    left = jnp.full(shape, pos_ref[1] > 0).astype(jnp.float32)
    right = jnp.full(shape, pos_ref[1] < pos_ref[2] - 1).astype(jnp.float32)
    return left, right


def copies_in(pairs, sems):
    started = []
    for i, (src, dst) in enumerate(pairs):
        copy = pltpu.make_async_copy(src, dst, sems.at[i])
        copy.start()
        started.append(copy)
    return started


def smooth_kernel(
    local_rows, block, pos_ref, squares_ref, deep_ref, near_ref, far_ref, left_ref, right_ref,
    s_ref, s_left_ref, s_right_ref, u_out, g_out,
    g, u1, u2, c_ref, ahead_ref, behind_ref, sems, out_sems,
):
    upper = pos_ref[0] == 1
    part = near_ref.shape[0]
    loads = copies_in(
        [
            (deep_ref, g.at[0:DEEP, NEAR : NEAR + block]),
            (near_ref, g.at[DEEP : DEEP + part, NEAR : NEAR + block]),
            (far_ref, g.at[DEEP + part : DEEP + local_rows, NEAR : NEAR + block]),
            (left_ref, g.at[:, 0:NEAR]),
            (right_ref, g.at[:, NEAR + block : NEAR + block + NEAR]),
        ],
        sems,
    )
    row_weights(upper, local_rows, -DEEP, DEEP + local_rows, squares_ref, c_ref, ahead_ref, behind_ref)
    masks = side_masks(pos_ref, squares_ref.shape)
    weights = (c_ref, ahead_ref, behind_ref, -DEEP)
    g_at = (g, -DEEP, -NEAR)
    u1_at = (u1, -DEEP, -NEAR)
    u2_at = (u2, 1 - DEEP, 1 - NEAR)
    u1[DEEP + local_rows] = jnp.zeros(u1.shape[1:], jnp.float32)
    u2[DEEP - 1 + local_rows] = jnp.zeros(u2.shape[1:], jnp.float32)
    for load in loads:
        load.wait()
    g_copy = pltpu.make_async_copy(
        g.at[DEEP - 1 : DEEP + local_rows, NEAR - 1 : NEAR + block + 1], g_out, out_sems.at[0]
    )
    g_copy.start()
    first_sweep((-DEEP, local_rows), (-NEAR, block + NEAR), block, g_at, u1_at, weights, masks)
    sweep(
        (1 - DEEP, local_rows), (1 - NEAR, block + NEAR - 1), block, u1_at, g_at, u2_at, weights, masks
    )
    u_copy = pltpu.make_async_copy(
        u2.at[DEEP - 3 : DEEP - 1 + local_rows, :], u_out, out_sems.at[1]
    )
    u_copy.start()

    def residual_row(index, first, count):
        z = first - u2_at[2]
        middle = u2[index - 1, z - 1 : z + count + 1]
        return (
            g[index, first + NEAR : first + NEAR + count]
            + ahead_ref[index] * u2[index, z : z + count]
            + behind_ref[index] * u2[index - 2, z : z + count]
            + (middle[:-2] + middle[2:])
            - (OMEGA / c_ref[index]) * middle[1:-1]
        )

    def restrict_row(index, carry):
        at = 2 * index + (DEEP - 2 * FAR)
        for first, count, _ in cell_tiles(0, block, block):
            both = residual_row(at, first, count) + residual_row(at + 1, first, count)
            pairs = both.reshape(count // 2, 2, *both.shape[1:])
            s_ref[index, first // 2 : (first + count) // 2] = pairs[:, 0] + pairs[:, 1]
        s_left_ref[index] = s_ref[index, 0:FAR]
        s_right_ref[index] = s_ref[index, block // 2 - FAR : block // 2]
        return carry

    lax.fori_loop(0, FAR + local_rows // 2, restrict_row, 0)
    g_copy.wait()
    u_copy.wait()


def correct_kernel(
    local_rows, block, pos_ref, squares_ref, s_own, s_left, s_right, u_in, g_in,
    o_ref,
    s, e0, e1, u, v, g, c_ref, ahead_ref, behind_ref, cc_ref, cahead_ref, cbehind_ref, sems,
):
    upper = pos_ref[0] == 1
    half_rows, half = local_rows // 2, block // 2
    loads = copies_in(
        [
            (s_own, s.at[:, FAR : FAR + half]),
            (s_left, s.at[:, 0:FAR]),
            (s_right, s.at[:, FAR + half : FAR + half + FAR]),
            (u_in, u.at[0 : local_rows + 2]),
            (g_in, g),
        ],
        sems,
    )
    masks = side_masks(pos_ref, squares_ref.shape)
    row_weights(upper, half_rows, -FAR, FAR + half_rows, squares_ref, cc_ref, cahead_ref, cbehind_ref)
    row_weights(upper, local_rows, -1, 1 + local_rows, squares_ref, c_ref, ahead_ref, behind_ref)
    coarse = (cc_ref, cahead_ref, cbehind_ref, -FAR)
    fine = (c_ref, ahead_ref, behind_ref, -1)
    for buffer in (e0, e1):
        buffer[FAR + half_rows] = jnp.zeros(buffer.shape[1:], jnp.float32)
    u[2 + local_rows] = jnp.zeros(u.shape[1:], jnp.float32)
    v[1 + local_rows] = jnp.zeros(v.shape[1:], jnp.float32)
    for load in loads[:3]:
        load.wait()
    s_at = (s, -FAR, -FAR)
    here, there = (e0, -FAR, -FAR), (e1, -FAR, -FAR)
    first_sweep((-FAR, half_rows), (-FAR, half + FAR), half, s_at, here, coarse, masks)
    for step in range(1, COARSE):
        sweep(
            (step - FAR, half_rows), (step - FAR, half + FAR - step), half, here, s_at, there, coarse, masks
        )
        here, there = there, here
    e = here[0]
    for load in loads[3:]:
        load.wait()

    def add_correction(index, carry):
        for first, count in ((-1, (half + 2) // 2), (-1 + (half + 2) // 2, half + 2 - (half + 2) // 2)):
            part = e[index + FAR - 1, first + FAR : first + FAR + count]
            twice = jnp.broadcast_to(part[:, None], (count, 2) + part.shape[1:])
            twice = twice.reshape(2 * count, *part.shape[1:])
            cells = slice(2 * first + 2, 2 * first + 2 + 2 * count)
            for offset in range(2):
                u[2 * index + offset, cells] = u[2 * index + offset, cells] + twice
        return carry

    lax.fori_loop(0, half_rows + 1, add_correction, 0)
    u_at, v_at, g_at = (u, -2, -2), (v, -1, -1), (g, -1, -1)
    sweep((-1, local_rows), (-1, block + 1), block, u_at, g_at, v_at, fine, masks)
    sweep((0, local_rows), (0, block), block, v_at, g_at, (o_ref, 0, 0), fine, masks)


def params(*order):
    return pltpu.CompilerParams(dimension_semantics=order or None, vmem_limit_bytes=VMEM_LIMIT)


def cell_body(density):
    local_phi, local_rows, vertical_cells = density.shape
    az_count = lax.axis_size("az")
    azimuths = local_phi * az_count
    block = vertical_cells // az_count
    rows = LANES // block
    tiles = local_rows // TILE
    groups = TILE // rows
    chunks = 2
    chunk_tiles = tiles // chunks
    chunk_rows = local_rows // chunks
    modes, analysis, synthesis = mode_tables(azimuths)
    squares = jnp.asarray((modes * modes).reshape(-1, LANES))
    lines = squares.shape[0]
    point = (lines, LANES)
    f32 = jnp.float32
    a_high, a_low = high_low(analysis)
    s_high, s_low = high_low(synthesis)
    az_index = lax.axis_index("az")
    position = jnp.stack([lax.axis_index("rad"), az_index, jnp.int32(az_count)]).astype(jnp.int32)
    table = pl.BlockSpec((azimuths // 2, azimuths), lambda j, *_: (0, 0))
    product = 2 * 3 * azimuths * azimuths // 2

    def row_tile(tile, pos_ref):
        return jnp.where(pos_ref[0] == 0, tiles - 1 - tile, tile)

    def pack(first_tile):
        return pl.pallas_call(
            lambda *refs: pack_kernel(block, *refs),
            grid_spec=pltpu.PrefetchScalarGridSpec(
                num_scalar_prefetch=1,
                grid=(chunk_tiles, vertical_cells // LANES),
                in_specs=[
                    pl.BlockSpec(
                        (local_phi, TILE, LANES),
                        lambda j, k, pos: (0, row_tile(first_tile + j, pos), k),
                    )
                ],
                out_specs=pl.BlockSpec(
                    (rows, groups, local_phi, LANES), lambda j, k, pos: (k, j, 0, 0)
                ),
            ),
            out_shape=jax.ShapeDtypeStruct(
                (az_count, chunk_tiles * groups, local_phi, LANES), f32
            ),
            compiler_params=params("arbitrary", "arbitrary"),
            name="pack",
        )(position, density)

    def analyse(received, with_edge):
        out_shape = [jax.ShapeDtypeStruct((chunk_rows, block) + point, f32)]
        out_specs = [pl.BlockSpec((TILE, block) + point, lambda j: (j, 0, 0, 0))]
        if with_edge:
            out_shape.append(jax.ShapeDtypeStruct((DEEP, block) + point, f32))
            out_specs.append(pl.BlockSpec((DEEP, block) + point, lambda j: (0, 0, 0, 0)))
        return pl.pallas_call(
            analysis_kernel,
            grid=(chunk_tiles,),
            in_specs=[
                pl.BlockSpec((az_count, groups, local_phi, LANES), lambda j: (0, j, 0, 0)),
                table,
                table,
            ],
            out_specs=out_specs,
            out_shape=out_shape,
            compiler_params=params("arbitrary"),
            cost_estimate=pl.CostEstimate(
                flops=product * chunk_rows * block, bytes_accessed=3 * received.size * 4, transcendentals=0
            ),
            name="analysis",
        )(received, a_high, a_low)

    def exchange(value):
        return lax.all_to_all(value, "az", split_axis=0, concat_axis=0, tiled=True)

    first_received = exchange(pack(0))
    second_received = exchange(pack(chunk_tiles))
    near, edge = analyse(first_received, True)
    deep = lax.ppermute(edge, "rad", [(0, 1), (1, 0)])
    (far,) = analyse(second_received, False)

    to_right = [(i, i + 1) for i in range(az_count - 1)]
    to_left = [(i + 1, i) for i in range(az_count - 1)]

    def side(start):
        return jnp.concatenate([part[:, start : start + NEAR] for part in (deep, near, far)], axis=0)

    left = lax.ppermute(side(block - NEAR), "az", to_right)
    right = lax.ppermute(side(0), "az", to_left)

    anywhere = pl.BlockSpec(memory_space=pl.ANY)
    in_vmem = pl.BlockSpec(memory_space=pltpu.VMEM)
    in_smem = pl.BlockSpec(memory_space=pltpu.SMEM)
    half_rows, half = local_rows // 2, block // 2
    all_rows = DEEP + local_rows
    coarse_rows = FAR + half_rows

    def field(row_count, cell_count):
        return jax.ShapeDtypeStruct((row_count, cell_count) + point, f32)

    def scratch(row_count, *cell_count):
        return pltpu.VMEM((row_count,) + cell_count + point, f32)

    s_own, s_head, s_tail, u_two, g_near = pl.pallas_call(
        lambda *refs: smooth_kernel(local_rows, block, *refs),
        in_specs=[in_smem, in_vmem] + [anywhere] * 5,
        out_specs=[in_vmem] * 3 + [anywhere] * 2,
        out_shape=[
            field(coarse_rows, half),
            field(coarse_rows, FAR),
            field(coarse_rows, FAR),
            field(local_rows + 2, block + 4),
            field(local_rows + 1, block + 2),
        ],
        scratch_shapes=[
            scratch(all_rows, block + 2 * NEAR),
            scratch(all_rows + 1, block + 2 * NEAR),
            scratch(all_rows, block + 2 * NEAR - 2),
            scratch(all_rows),
            scratch(all_rows),
            scratch(all_rows),
            pltpu.SemaphoreType.DMA((5,)),
            pltpu.SemaphoreType.DMA((2,)),
        ],
        compiler_params=params(),
        name="smooth",
    )(position, squares, deep, near, far, left, right)

    s_left = lax.ppermute(s_tail, "az", to_right)
    s_right = lax.ppermute(s_head, "az", to_left)

    solved = pl.pallas_call(
        lambda *refs: correct_kernel(local_rows, block, *refs),
        in_specs=[in_smem, in_vmem] + [anywhere] * 5,
        out_specs=in_vmem,
        out_shape=field(local_rows, block),
        scratch_shapes=[
            scratch(coarse_rows, half + 2 * FAR),
            scratch(coarse_rows + 1, half + 2 * FAR),
            scratch(coarse_rows + 1, half + 2 * FAR),
            scratch(local_rows + 3, block + 4),
            scratch(local_rows + 2, block + 2),
            scratch(local_rows + 1, block + 2),
            scratch(local_rows + 1),
            scratch(local_rows + 1),
            scratch(local_rows + 1),
            scratch(coarse_rows),
            scratch(coarse_rows),
            scratch(coarse_rows),
            pltpu.SemaphoreType.DMA((5,)),
        ],
        compiler_params=params(),
        name="correct",
    )(position, squares, s_own, s_left, s_right, u_two, g_near)

    physical = pl.pallas_call(
        synthesis_kernel,
        grid=(tiles,),
        in_specs=[
            pl.BlockSpec((TILE, block) + point, lambda j: (j, 0, 0, 0)),
            table,
            table,
        ],
        out_specs=pl.BlockSpec((az_count, groups, local_phi, LANES), lambda j: (0, j, 0, 0)),
        out_shape=jax.ShapeDtypeStruct((az_count, tiles * groups, local_phi, LANES), f32),
        compiler_params=params("arbitrary"),
        name="synthesis",
    )(solved, s_high, s_low)

    returned = exchange(physical)
    return pl.pallas_call(
        lambda *refs: unpack_kernel(block, *refs),
        grid_spec=pltpu.PrefetchScalarGridSpec(
            num_scalar_prefetch=1,
            grid=(tiles, vertical_cells // LANES),
            in_specs=[
                pl.BlockSpec((rows, groups, local_phi, LANES), lambda j, k, pos: (k, j, 0, 0))
            ],
            out_specs=pl.BlockSpec(
                (local_phi, TILE, LANES), lambda j, k, pos: (0, row_tile(j, pos), k)
            ),
        ),
        out_shape=jax.ShapeDtypeStruct(density.shape, f32),
        compiler_params=params("arbitrary", "arbitrary"),
        name="unpack",
    )(position, returned)


def fits_cells(density):
    local_phi, local_rows, vertical_cells = density.shape
    az_count, rad_count = lax.axis_size("az"), lax.axis_size("rad")
    block = vertical_cells // az_count
    return (
        rad_count == 2
        and vertical_cells % (az_count * 2) == 0
        and vertical_cells % LANES == 0
        and LANES // TILE <= block <= LANES
        and LANES % block == 0
        and block // 2 >= FAR
        and local_rows % (4 * TILE) == 0
        and local_rows // 2 >= DEEP
        and az_count % 2 == 0
        and local_phi % TILE == 0
        and (az_count * local_phi) % (2 * LANES) == 0
        and az_count * local_phi == TILE * LANES
    )


def body(density):
    return cell_body(density) if fits_cells(density) else general_body(density)


def solution(mesh):
    placed = (P("az", "rad", None),)
    return jax.shard_map(
        body, mesh=mesh, in_specs=placed, out_specs=P("az", "rad", None), check_vma=False
    )
```

```python
import math

import jax
import jax.numpy as jnp
import numpy as np
from jax import lax
from jax.experimental import pallas as pl
from jax.experimental.pallas import tpu as pltpu
from jax.sharding import PartitionSpec as P

PRE = 2
POST = 2
COARSE = 6


OMEGA = 0.8

LANES = 128
TILE = 8
DEEP = 2 * COARSE + 2
NEAR = 3
FAR = COARSE


def with_halo(cells, sides, width):
    for axis, dim in sides:
        count = lax.axis_size(axis)
        ends = count - 1
        head = lax.slice_in_dim(cells, 0, width, axis=dim)
        tail = lax.slice_in_dim(cells, cells.shape[dim] - width, cells.shape[dim], axis=dim)
        cells = jnp.concatenate(
            [
                lax.ppermute(tail, axis, [(i, (i + 1) % count) for i in range(ends)]),
                cells,
                lax.ppermute(head, axis, [((i + 1) % count, i) for i in range(ends)]),
            ],
            axis=dim,
        )
    return cells


def level_coefficients(first_row, row_count, spacing, mode_numbers):
    row_number = (jnp.arange(row_count, dtype=jnp.int32) + first_row).astype(jnp.float32)
    radius = spacing * (row_number + 0.5)
    outward = (row_number + 1.0) / (spacing * radius)
    inward = row_number / (spacing * radius)
    vertical = 1.0 / (spacing * spacing)
    diagonal = (outward + inward + 2.0 * vertical)[None, :] + (
        mode_numbers[:, None] / radius[None, :]
    ) ** 2
    return (diagonal[:, :, None], outward[None, :, None], inward[None, :, None], vertical)


def apply_op(iterate, padded, coefficients):
    diagonal, outward, inward, vertical = coefficients
    return (
        diagonal * iterate
        - outward * padded[:, 2:, 1:-1]
        - inward * padded[:, :-2, 1:-1]
        - vertical * (padded[:, 1:-1, 2:] + padded[:, 1:-1, :-2])
    )


def relax(iterate, source, coefficients, pad_both):
    return (
        iterate
        + OMEGA * (source - apply_op(iterate, pad_both(iterate), coefficients)) / coefficients[0]
    )


def restrict(residual):
    k_count, r_count, z_count = residual.shape
    parts = residual.reshape(k_count, r_count // 2, 2, z_count // 2, 2)
    return 0.25 * (
        parts[:, :, 0, :, 0] + parts[:, :, 1, :, 0] + parts[:, :, 0, :, 1] + parts[:, :, 1, :, 1]
    )


def prolong(correction):
    return jnp.repeat(jnp.repeat(correction, 2, axis=1), 2, axis=2)


def pad_level(field):
    rows = with_halo(field, (("rad", 1),), 1)
    return jnp.pad(rows, ((0, 0), (0, 0), (1, 1)))


def mode_values(mode_index, azimuths):
    return jnp.where(mode_index <= azimuths // 2, mode_index, mode_index - azimuths // 2).astype(
        jnp.float32
    )


def fine_cycle(source, fine_coef, pad_sweep, coarse_solve):
    iterate = OMEGA * source / fine_coef[0]
    for sweep_index in range(PRE - 1):
        iterate = relax(iterate, source, fine_coef, pad_sweep)
    residual = source - apply_op(iterate, pad_sweep(iterate), fine_coef)
    iterate = iterate + prolong(coarse_solve(restrict(residual)))
    for sweep_index in range(POST):
        iterate = relax(iterate, source, fine_coef, pad_sweep)
    return iterate


def general_body(density):
    local_phi, local_rows, vertical_cells = density.shape
    az_count = lax.axis_size("az")
    azimuths = local_phi * az_count
    cell_count = local_rows * vertical_cells // az_count
    numbers = jnp.arange(azimuths, dtype=jnp.int32)
    all_modes = jnp.where(numbers <= azimuths // 2, numbers, numbers - azimuths // 2)
    phase = all_modes[:, None] * numbers[None, :] % azimuths
    phase_angle = phase.astype(jnp.float32) * (2.0 * math.pi / azimuths)
    analysis_table = jnp.where(
        (numbers <= azimuths // 2)[:, None], jnp.cos(phase_angle), jnp.sin(phase_angle)
    )
    synth_weight = jnp.where(
        (numbers == 0) | (numbers == azimuths // 2), 1.0 / azimuths, 2.0 / azimuths
    )
    synthesis_table = analysis_table.T * synth_weight[None, :]

    def transform_with(table, columns):
        width = columns.shape[2]
        matrix = columns.reshape(azimuths, width)
        result = jnp.dot(
            table, matrix, precision=lax.Precision.HIGHEST, preferred_element_type=jnp.float32
        )
        return result.reshape(azimuths, 1, width)

    lines = density.reshape(local_phi, az_count, cell_count)
    spectral = transform_with(
        analysis_table, lax.all_to_all(lines, "az", split_axis=1, concat_axis=0, tiled=True)
    )
    coefficients = lax.all_to_all(spectral, "az", split_axis=0, concat_axis=1, tiled=True)
    source = -coefficients.reshape(local_phi, local_rows, vertical_cells)
    rad_index = lax.axis_index("rad")
    half_rows = local_rows // 2
    mode_index = lax.axis_index("az") * local_phi + jnp.arange(local_phi, dtype=jnp.int32)
    mode_numbers = mode_values(mode_index, azimuths)
    fine_coef = level_coefficients(rad_index * local_rows, local_rows, 1.0, mode_numbers)
    coarse_coef = level_coefficients(rad_index * half_rows, half_rows, 2.0, mode_numbers)

    def coarse_halo(coarse_source):
        correction = OMEGA * coarse_source / coarse_coef[0]
        for sweep_index in range(COARSE - 1):
            correction = relax(correction, coarse_source, coarse_coef, pad_level)
        return correction

    iterate = fine_cycle(source, fine_coef, pad_level, coarse_halo)
    mode_lines = iterate.reshape(local_phi, az_count, cell_count)
    physical = transform_with(
        synthesis_table, lax.all_to_all(mode_lines, "az", split_axis=1, concat_axis=0, tiled=True)
    )
    field = lax.all_to_all(physical, "az", split_axis=0, concat_axis=1, tiled=True)
    return field.reshape(local_phi, local_rows, vertical_cells)


def mode_tables(azimuths):
    half = azimuths // 2
    even = np.concatenate([np.arange(0, half + 1, 2), np.arange(2, half, 2)])
    odd = np.concatenate([np.arange(1, half, 2), np.arange(1, half, 2)])
    even_cos = np.arange(half) <= half // 2
    odd_cos = np.arange(half) < half // 2
    modes = np.concatenate([even, odd])
    is_cos = np.concatenate([even_cos, odd_cos])
    angle = 2.0 * np.pi / azimuths * (np.arange(half)[:, None] * modes[None, :] % azimuths)
    values = np.where(is_cos[None, :], np.cos(angle), np.sin(angle))
    weight = np.where((modes == 0) | (modes == half), 1.0, 2.0) / azimuths
    return modes.astype(np.float32), -values, values * weight[None, :]


def high_low(values):
    values = values.astype(np.float32)
    high = values.astype(jnp.bfloat16)
    low = (values - high.astype(np.float32)).astype(jnp.bfloat16)
    return jnp.asarray(high), jnp.asarray(low)


def split_value(value):
    high = value.astype(jnp.bfloat16)
    return high, (value - high.astype(jnp.float32)).astype(jnp.bfloat16)


def row_tile(pos_ref, local_rows, tile):
    return jnp.where(pos_ref[0] == 0, local_rows // TILE - 1 - tile, tile)


def swap_chunks(parts, chunk):
    count = len(parts)
    parts = list(parts)
    lane = lax.broadcasted_iota(jnp.int32, parts[0].shape, parts[0].ndim - 1) // chunk
    span = count // 2
    while span:
        keep = (lane & span) == 0
        for i in range(count):
            if i & span:
                continue
            a, b = parts[i], parts[i + span]
            axis = a.ndim - 1
            parts[i] = jnp.where(keep, a, pltpu.roll(b, span * chunk, axis))
            parts[i + span] = jnp.where(keep, pltpu.roll(a, LANES - span * chunk, axis), b)
        span //= 2
    return parts


def tile_row(pos_ref, row):
    return jnp.where(pos_ref[0] == 0, TILE - 1 - row, row)


def pack_kernel(block, order, first_tile, pos_ref, x_ref, o_ref, x, o, in_sems, out_sems):
    rows = LANES // block
    local_phi, local_rows, cells = x_ref.shape
    tiles, lane_tiles, groups = x.shape[0], x.shape[1], TILE // rows
    pieces = [(j, k) for j in range(tiles) for k in range(lane_tiles)]
    loads, stores = [], []
    for n, (j, k) in enumerate(pieces):
        start = pl.multiple_of(row_tile(pos_ref, local_rows, first_tile + j) * TILE, TILE)
        source = x_ref.at[:, pl.ds(start, TILE), k * LANES : (k + 1) * LANES]
        loads.append(pltpu.make_async_copy(source, x.at[j, k], in_sems.at[n]))
        loads[-1].start()
    for n, (j, k) in enumerate(pieces):
        loads[n].wait()
        flat = x.at[j, k].reshape(local_phi * TILE, LANES)
        for group in range(groups):
            parts = [
                flat[pl.ds(tile_row(pos_ref, group * rows + i), local_phi, stride=TILE), :]
                for i in range(rows)
            ]
            for q, part in enumerate(swap_chunks(parts, block)):
                o[order[k * rows + q], j * groups + group] = part
        if k == lane_tiles - 1:
            span = slice(j * groups, (j + 1) * groups)
            stores.append(pltpu.make_async_copy(o.at[:, span], o_ref.at[:, span], out_sems.at[j]))
            stores[-1].start()
    for store in stores:
        store.wait()


def unpack_kernel(block, order, pos_ref, x_ref, o_ref, x, o, in_sems, out_sems):
    rows = LANES // block
    local_phi, local_rows, cells = o_ref.shape
    tiles, lane_tiles, groups = o.shape[0], o.shape[1], TILE // rows
    loads, stores = [], []
    for j in range(tiles):
        span = slice(j * groups, (j + 1) * groups)
        loads.append(pltpu.make_async_copy(x_ref.at[:, span], x.at[:, span], in_sems.at[j]))
        loads[-1].start()
    for j in range(tiles):
        loads[j].wait()
        start = pl.multiple_of(row_tile(pos_ref, local_rows, j) * TILE, TILE)
        for k in range(lane_tiles):
            flat = o.at[j, k].reshape(local_phi * TILE, LANES)
            for group in range(groups):
                parts = [x[order[k * rows + q], j * groups + group] for q in range(rows)]
                for i, part in enumerate(swap_chunks(parts, block)):
                    at = tile_row(pos_ref, group * rows + i)
                    flat[pl.ds(at, local_phi, stride=TILE), :] = part
            target = o_ref.at[:, pl.ds(start, TILE), k * LANES : (k + 1) * LANES]
            stores.append(
                pltpu.make_async_copy(o.at[j, k], target, out_sems.at[j * lane_tiles + k])
            )
            stores[-1].start()
    for store in stores:
        store.wait()


def analysis_kernel(x_ref, high_ref, low_ref, o_ref, head_ref, tail_ref, *edge_refs):
    sources, groups, width, lanes = x_ref.shape
    half = sources // 2 * width
    rows, cells = o_ref.shape[0], o_ref.shape[1]
    for parity in range(2):
        turned = []
        for group in range(groups):
            near, far = x_ref[: sources // 2, group], x_ref[sources // 2 :, group]
            folded = near + far if parity == 0 else near - far
            turned.append(folded.reshape(half, lanes).T)
        high, low = split_value(jnp.concatenate(turned, axis=0))
        columns = slice(parity * half, (parity + 1) * half)
        t_high, t_low = high_ref[:, columns], low_ref[:, columns]
        result = (
            jnp.dot(high, t_high, preferred_element_type=jnp.float32)
            + jnp.dot(high, t_low, preferred_element_type=jnp.float32)
            + jnp.dot(low, t_high, preferred_element_type=jnp.float32)
        )
        for part in range(half // LANES):
            piece = result[:, part * LANES : (part + 1) * LANES]
            o_ref[:, :, parity * (half // LANES) + part, :] = piece.reshape(rows, cells, LANES)
    head_ref[...] = o_ref[:, :NEAR]
    tail_ref[...] = o_ref[:, cells - NEAR :]
    if edge_refs:
        edge_ref, edge_head_ref, edge_tail_ref = edge_refs
        for step in range(-(-DEEP // rows)):

            @pl.when(pl.program_id(0) == step)
            def _():
                for row in range(rows):
                    at = DEEP - 1 - step * rows - row
                    if at >= 0:
                        edge_ref[at] = o_ref[row]
                        edge_head_ref[at] = o_ref[row, :NEAR]
                        edge_tail_ref[at] = o_ref[row, cells - NEAR :]


def synthesis_kernel(u_ref, high_ref, low_ref, o_ref):
    rows, cells = u_ref.shape[0], u_ref.shape[1]
    half = high_ref.shape[0]
    parts = half // LANES
    sums = []
    for parity in range(2):
        field = jnp.concatenate(
            [u_ref[:, :, parity * parts + i, :].reshape(rows * cells, LANES) for i in range(parts)],
            axis=1,
        )
        high, low = split_value(field)
        columns = slice(parity * half, (parity + 1) * half)
        t_high, t_low = high_ref[:, columns], low_ref[:, columns]
        contract = (((1,), (1,)), ((), ()))
        sums.append(
            lax.dot_general(t_high, high, contract, preferred_element_type=jnp.float32)
            + lax.dot_general(t_high, low, contract, preferred_element_type=jnp.float32)
            + lax.dot_general(t_low, high, contract, preferred_element_type=jnp.float32)
        )
    near, far = sums[0] + sums[1], sums[0] - sums[1]
    targets, groups, width, lanes = o_ref.shape
    for group in range(groups):
        columns = slice(group * lanes, (group + 1) * lanes)
        o_ref[: targets // 2, group] = near[:, columns].reshape(targets // 2, width, lanes)
        o_ref[targets // 2 :, group] = far[:, columns].reshape(targets // 2, width, lanes)


def row_weights(upper, boundary, first, count, squares_ref, c_ref, ahead_ref, behind_ref):
    def one(index, carry):
        row = jnp.where(upper, index + (boundary + first), (boundary - 1 - first) - index)
        number = jnp.full(squares_ref.shape, row, jnp.int32).astype(jnp.float32)
        radius = number + 0.5
        outward = (number + 1.0) / radius
        inward = number / radius
        diagonal = outward + inward + 2.0 + squares_ref[...] / (radius * radius)
        c_ref[index] = OMEGA / diagonal
        ahead_ref[index] = jnp.where(upper, outward, inward)
        behind_ref[index] = jnp.where(upper, inward, outward)
        return carry

    lax.fori_loop(0, count, one, 0)


def cell_tiles(first, last, cells, size=16):
    tiles = []
    if first < 0:
        tiles.append((first, -first, -1))
    for start in range(max(first, 0), min(last, cells), size):
        tiles.append((start, min(size, min(last, cells) - start), 0))
    if last > cells:
        tiles.append((cells, last - cells, 1))
    return tiles


def sweep(rows, cells, block, src, source, dst, weights, masks):
    (src_ref, src_t, src_z), (g_ref, g_t, g_z), (dst_ref, dst_t, dst_z) = src, source, dst
    c_ref, ahead_ref, behind_ref, w_t = weights
    low = rows[0]

    def one(step, carry):
        at = step + (low - w_t)
        c_row, ahead, behind = c_ref[at], ahead_ref[at], behind_ref[at]
        for first, count, side in cell_tiles(cells[0], cells[1], block):
            c = c_row if side == 0 else c_row * masks[0 if side < 0 else 1]
            z = first - src_z
            row = low - src_t
            middle = src_ref[step + row, z - 1 : z + count + 1]
            gathered = (
                g_ref[step + (low - g_t), first - g_z : first - g_z + count]
                + ahead * src_ref[step + (row + 1), z : z + count]
                + behind * src_ref[step + (row - 1), z : z + count]
                + (middle[:-2] + middle[2:])
            )
            dst_ref[step + (low - dst_t), first - dst_z : first - dst_z + count] = (
                (1.0 - OMEGA) * middle[1:-1] + c * gathered
            )
        return carry

    lax.fori_loop(0, rows[1] - low, one, 0)


def first_sweep(rows, cells, block, source, dst, weights, masks):
    (g_ref, g_t, g_z), (dst_ref, dst_t, dst_z) = source, dst
    c_ref, w_t = weights[0], weights[3]
    low = rows[0]

    def one(step, carry):
        c_row = c_ref[step + (low - w_t)]
        for first, count, side in cell_tiles(cells[0], cells[1], block):
            c = c_row if side == 0 else c_row * masks[0 if side < 0 else 1]
            dst_ref[step + (low - dst_t), first - dst_z : first - dst_z + count] = (
                c * g_ref[step + (low - g_t), first - g_z : first - g_z + count]
            )
        return carry

    lax.fori_loop(0, rows[1] - low, one, 0)


def side_masks(pos_ref, shape):
    left = jnp.full(shape, pos_ref[1] > 0).astype(jnp.float32)
    right = jnp.full(shape, pos_ref[1] < pos_ref[2] - 1).astype(jnp.float32)
    return left, right


def copies_in(pairs, sems):
    started = []
    for i, (src, dst) in enumerate(pairs):
        copy = pltpu.make_async_copy(src, dst, sems.at[i])
        copy.start()
        started.append(copy)
    return started


def smooth_kernel(
    local_rows, block, pos_ref, squares_ref, *refs
):
    field_refs, (
    s_ref, s_left_ref, s_right_ref, u_out, g_out,
    g, u1, u2, c_ref, ahead_ref, behind_ref, sems, out_sems,
    ) = refs[:9], refs[9:]
    upper = pos_ref[0] == 1
    columns = (slice(NEAR, NEAR + block), slice(0, NEAR), slice(NEAR + block, NEAR + block + NEAR))
    pairs, start = [], 0
    for n in range(3):
        count = field_refs[3 * n].shape[0]
        for ref, column in zip(field_refs[3 * n : 3 * n + 3], columns):
            pairs.append((ref, g.at[start : start + count, column]))
        start += count
    loads = copies_in(pairs, sems)
    row_weights(upper, local_rows, -DEEP, DEEP + local_rows, squares_ref, c_ref, ahead_ref, behind_ref)
    masks = side_masks(pos_ref, squares_ref.shape)
    weights = (c_ref, ahead_ref, behind_ref, -DEEP)
    g_at = (g, -DEEP, -NEAR)
    u1_at = (u1, -DEEP, -NEAR)
    u2_at = (u2, 1 - DEEP, 1 - NEAR)
    u1[DEEP + local_rows] = jnp.zeros(u1.shape[1:], jnp.float32)
    u2[DEEP - 1 + local_rows] = jnp.zeros(u2.shape[1:], jnp.float32)
    for load in loads:
        load.wait()
    g_copy = pltpu.make_async_copy(
        g.at[DEEP - 1 : DEEP + local_rows, NEAR - 1 : NEAR + block + 1], g_out, out_sems.at[0]
    )
    g_copy.start()
    first_sweep((-DEEP, local_rows), (-NEAR, block + NEAR), block, g_at, u1_at, weights, masks)
    sweep(
        (1 - DEEP, local_rows), (1 - NEAR, block + NEAR - 1), block, u1_at, g_at, u2_at, weights, masks
    )
    u_copy = pltpu.make_async_copy(
        u2.at[DEEP - 3 : DEEP - 1 + local_rows, :], u_out, out_sems.at[1]
    )
    u_copy.start()

    def residual_row(index, first, count):
        z = first - u2_at[2]
        middle = u2[index - 1, z - 1 : z + count + 1]
        return (
            g[index, first + NEAR : first + NEAR + count]
            + ahead_ref[index] * u2[index, z : z + count]
            + behind_ref[index] * u2[index - 2, z : z + count]
            + (middle[:-2] + middle[2:])
            - (OMEGA / c_ref[index]) * middle[1:-1]
        )

    def restrict_row(index, carry):
        at = 2 * index + (DEEP - 2 * FAR)
        for first, count, _ in cell_tiles(0, block, block):
            both = residual_row(at, first, count) + residual_row(at + 1, first, count)
            pairs = both.reshape(count // 2, 2, *both.shape[1:])
            s_ref[index, first // 2 : (first + count) // 2] = pairs[:, 0] + pairs[:, 1]
        s_left_ref[index] = s_ref[index, 0:FAR]
        s_right_ref[index] = s_ref[index, block // 2 - FAR : block // 2]
        return carry

    lax.fori_loop(0, FAR + local_rows // 2, restrict_row, 0)
    g_copy.wait()
    u_copy.wait()


def correct_kernel(
    local_rows, block, pos_ref, squares_ref, s_own, s_left, s_right, u_in, g_in,
    o_ref,
    s, e0, e1, u, v, g, c_ref, ahead_ref, behind_ref, cc_ref, cahead_ref, cbehind_ref, sems,
):
    upper = pos_ref[0] == 1
    half_rows, half = local_rows // 2, block // 2
    loads = copies_in(
        [
            (s_own, s.at[:, FAR : FAR + half]),
            (s_left, s.at[:, 0:FAR]),
            (s_right, s.at[:, FAR + half : FAR + half + FAR]),
            (u_in, u.at[0 : local_rows + 2]),
            (g_in, g),
        ],
        sems,
    )
    masks = side_masks(pos_ref, squares_ref.shape)
    row_weights(upper, half_rows, -FAR, FAR + half_rows, squares_ref, cc_ref, cahead_ref, cbehind_ref)
    row_weights(upper, local_rows, -1, 1 + local_rows, squares_ref, c_ref, ahead_ref, behind_ref)
    coarse = (cc_ref, cahead_ref, cbehind_ref, -FAR)
    fine = (c_ref, ahead_ref, behind_ref, -1)
    for buffer in (e0, e1):
        buffer[FAR + half_rows] = jnp.zeros(buffer.shape[1:], jnp.float32)
    u[2 + local_rows] = jnp.zeros(u.shape[1:], jnp.float32)
    v[1 + local_rows] = jnp.zeros(v.shape[1:], jnp.float32)
    for load in loads[:3]:
        load.wait()
    s_at = (s, -FAR, -FAR)
    here, there = (e0, -FAR, -FAR), (e1, -FAR, -FAR)
    first_sweep((-FAR, half_rows), (-FAR, half + FAR), half, s_at, here, coarse, masks)
    for step in range(1, COARSE):
        sweep(
            (step - FAR, half_rows), (step - FAR, half + FAR - step), half, here, s_at, there, coarse, masks
        )
        here, there = there, here
    e = here[0]
    for load in loads[3:]:
        load.wait()

    def add_correction(index, carry):
        for first, count in ((-1, (half + 2) // 2), (-1 + (half + 2) // 2, half + 2 - (half + 2) // 2)):
            part = e[index + FAR - 1, first + FAR : first + FAR + count]
            twice = jnp.broadcast_to(part[:, None], (count, 2) + part.shape[1:])
            twice = twice.reshape(2 * count, *part.shape[1:])
            cells = slice(2 * first + 2, 2 * first + 2 + 2 * count)
            for offset in range(2):
                u[2 * index + offset, cells] = u[2 * index + offset, cells] + twice
        return carry

    lax.fori_loop(0, half_rows + 1, add_correction, 0)
    u_at, v_at, g_at = (u, -2, -2), (v, -1, -1), (g, -1, -1)
    sweep((-1, local_rows), (-1, block + 1), block, u_at, g_at, v_at, fine, masks)
    sweep((0, local_rows), (0, block), block, v_at, g_at, (o_ref, 0, 0), fine, masks)


def params(mebibytes, *order):
    return pltpu.CompilerParams(
        dimension_semantics=order or None, vmem_limit_bytes=mebibytes * 1024 * 1024
    )


def cell_body(density):
    local_phi, local_rows, vertical_cells = density.shape
    az_count = lax.axis_size("az")
    azimuths = local_phi * az_count
    block = vertical_cells // az_count
    rows = LANES // block
    tiles = local_rows // TILE
    groups = TILE // rows
    chunks = 2
    chunk_tiles = tiles // chunks
    chunk_rows = local_rows // chunks
    modes, analysis, synthesis = mode_tables(azimuths)
    squares = jnp.asarray((modes * modes).reshape(-1, LANES))
    lines = squares.shape[0]
    point = (lines, LANES)
    f32 = jnp.float32
    a_high, a_low = high_low(analysis)
    s_high, s_low = high_low(synthesis)
    order = block_order(az_count)
    az_index = lax.axis_index("az")
    rad_index = lax.axis_index("rad")
    block_index = jnp.where((az_index // 4) % 2 == 1, az_index ^ 2, az_index)
    position = jnp.stack([rad_index, block_index, jnp.int32(az_count)]).astype(jnp.int32)
    table = pl.BlockSpec((azimuths // 2, azimuths), lambda j, *_: (0, 0))
    product = 2 * 3 * azimuths * azimuths // 2
    lane_tiles = vertical_cells // LANES
    anywhere = pl.BlockSpec(memory_space=pl.ANY)
    in_vmem = pl.BlockSpec(memory_space=pltpu.VMEM)
    in_smem = pl.BlockSpec(memory_space=pltpu.SMEM)

    def pack(first_tile):
        return pl.pallas_call(
            lambda *refs: pack_kernel(block, order, first_tile, *refs),
            in_specs=[in_smem, anywhere],
            out_specs=anywhere,
            out_shape=jax.ShapeDtypeStruct(
                (az_count, chunk_tiles * groups, local_phi, LANES), f32
            ),
            scratch_shapes=[
                pltpu.VMEM((chunk_tiles, lane_tiles, local_phi, TILE, LANES), f32),
                pltpu.VMEM((az_count, chunk_tiles * groups, local_phi, LANES), f32),
                pltpu.SemaphoreType.DMA((chunk_tiles * lane_tiles,)),
                pltpu.SemaphoreType.DMA((chunk_tiles,)),
            ],
            compiler_params=params(8),
            name="pack",
        )(position, density)

    def analyse(received, with_edge):
        def whole(count, cells):
            return pl.BlockSpec((count, cells) + point, lambda j: (0, 0, 0, 0))

        def moving(cells):
            return pl.BlockSpec((TILE, cells) + point, lambda j: (j, 0, 0, 0))

        widths = (block, NEAR, NEAR)
        out_shape = [field(chunk_rows, width) for width in widths]
        out_specs = [moving(width) for width in widths]
        if with_edge:
            out_shape += [field(DEEP, width) for width in widths]
            out_specs += [whole(DEEP, width) for width in widths]
        return pl.pallas_call(
            analysis_kernel,
            grid=(chunk_tiles,),
            in_specs=[
                pl.BlockSpec((az_count, groups, local_phi, LANES), lambda j: (0, j, 0, 0)),
                table,
                table,
            ],
            out_specs=out_specs,
            out_shape=out_shape,
            compiler_params=params(24, "arbitrary"),
            cost_estimate=pl.CostEstimate(
                flops=product * chunk_rows * block, bytes_accessed=3 * received.size * 4, transcendentals=0
            ),
            name="analysis",
        )(received, a_high, a_low)

    def exchange(value):
        return lax.all_to_all(value, "az", split_axis=0, concat_axis=0, tiled=True)

    to_right = [(order[i], order[i + 1]) for i in range(az_count - 1)]
    to_left = [(b, a) for a, b in to_right]

    def from_sides(head, tail):
        return lax.ppermute(tail, "az", to_right), lax.ppermute(head, "az", to_left)

    def across(pairs):
        return [(2 * a + y, 2 * b + 1 - y) for a, b in pairs for y in range(2)]

    def field(row_count, cell_count):
        return jax.ShapeDtypeStruct((row_count, cell_count) + point, f32)

    def scratch(row_count, *cell_count):
        return pltpu.VMEM((row_count,) + cell_count + point, f32)

    first_received = exchange(pack(0))
    second_received = exchange(pack(chunk_tiles))
    near, near_head, near_tail, edge, edge_head, edge_tail = analyse(first_received, True)
    deep = lax.ppermute(edge, "rad", [(0, 1), (1, 0)])
    near_left, near_right = from_sides(near_head, near_tail)
    deep_left = lax.ppermute(edge_tail, ("az", "rad"), across(to_right))
    deep_right = lax.ppermute(edge_head, ("az", "rad"), across(to_left))
    far, far_head, far_tail = analyse(second_received, False)
    far_left, far_right = from_sides(far_head, far_tail)

    half_rows, half = local_rows // 2, block // 2
    all_rows = DEEP + local_rows
    coarse_rows = FAR + half_rows

    s_own, s_head, s_tail, u_two, g_near = pl.pallas_call(
        lambda *refs: smooth_kernel(local_rows, block, *refs),
        in_specs=[in_smem, in_vmem] + [anywhere] * 9,
        out_specs=[in_vmem] * 3 + [anywhere] * 2,
        out_shape=[
            field(coarse_rows, half),
            field(coarse_rows, FAR),
            field(coarse_rows, FAR),
            field(local_rows + 2, block + 4),
            field(local_rows + 1, block + 2),
        ],
        scratch_shapes=[
            scratch(all_rows, block + 2 * NEAR),
            scratch(all_rows + 1, block + 2 * NEAR),
            scratch(all_rows, block + 2 * NEAR - 2),
            scratch(all_rows),
            scratch(all_rows),
            scratch(all_rows),
            pltpu.SemaphoreType.DMA((9,)),
            pltpu.SemaphoreType.DMA((2,)),
        ],
        compiler_params=params(32),
        name="smooth",
    )(
        position, squares, deep, deep_left, deep_right, near, near_left, near_right, far, far_left, far_right
    )

    s_left, s_right = from_sides(s_head, s_tail)

    solved = pl.pallas_call(
        lambda *refs: correct_kernel(local_rows, block, *refs),
        in_specs=[in_smem, in_vmem] + [anywhere] * 5,
        out_specs=in_vmem,
        out_shape=field(local_rows, block),
        scratch_shapes=[
            scratch(coarse_rows, half + 2 * FAR),
            scratch(coarse_rows + 1, half + 2 * FAR),
            scratch(coarse_rows + 1, half + 2 * FAR),
            scratch(local_rows + 3, block + 4),
            scratch(local_rows + 2, block + 2),
            scratch(local_rows + 1, block + 2),
            scratch(local_rows + 1),
            scratch(local_rows + 1),
            scratch(local_rows + 1),
            scratch(coarse_rows),
            scratch(coarse_rows),
            scratch(coarse_rows),
            pltpu.SemaphoreType.DMA((5,)),
        ],
        compiler_params=params(36),
        name="correct",
    )(position, squares, s_own, s_left, s_right, u_two, g_near)

    physical = pl.pallas_call(
        synthesis_kernel,
        grid=(tiles,),
        in_specs=[
            pl.BlockSpec((TILE, block) + point, lambda j: (j, 0, 0, 0)),
            table,
            table,
        ],
        out_specs=pl.BlockSpec((az_count, groups, local_phi, LANES), lambda j: (0, j, 0, 0)),
        out_shape=jax.ShapeDtypeStruct((az_count, tiles * groups, local_phi, LANES), f32),
        compiler_params=params(24, "arbitrary"),
        name="synthesis",
    )(solved, s_high, s_low)

    returned = exchange(physical)
    side = jnp.stack([rad_index, rad_index]).astype(jnp.int32)
    return pl.pallas_call(
        lambda *refs: unpack_kernel(block, order, *refs),
        in_specs=[in_smem, anywhere],
        out_specs=anywhere,
        out_shape=jax.ShapeDtypeStruct(density.shape, f32),
        scratch_shapes=[
            pltpu.VMEM((az_count, tiles * groups, local_phi, LANES), f32),
            pltpu.VMEM((tiles, lane_tiles, local_phi, TILE, LANES), f32),
            pltpu.SemaphoreType.DMA((tiles,)),
            pltpu.SemaphoreType.DMA((tiles * lane_tiles,)),
        ],
        compiler_params=params(12),
        name="unpack",
    )(side, returned)


def block_order(az_count):
    return [i ^ 2 if (i // 4) % 2 else i for i in range(az_count)]


def fits_cells(density):
    local_phi, local_rows, vertical_cells = density.shape
    az_count, rad_count = lax.axis_size("az"), lax.axis_size("rad")
    block = vertical_cells // az_count
    return (
        rad_count == 2
        and vertical_cells % (az_count * 2) == 0
        and vertical_cells % LANES == 0
        and LANES // TILE <= block <= LANES
        and LANES % block == 0
        and block // 2 >= FAR
        and local_rows % (4 * TILE) == 0
        and local_rows // 2 >= DEEP
        and az_count % 4 == 0
        and local_phi % TILE == 0
        and (az_count * local_phi) % (2 * LANES) == 0
        and az_count * local_phi == TILE * LANES
    )


def body(density):
    return cell_body(density) if fits_cells(density) else general_body(density)


def solution(mesh):
    placed = (P("az", "rad", None),)
    return jax.shard_map(
        body, mesh=mesh, in_specs=placed, out_specs=P("az", "rad", None), check_vma=False
    )
```

```python
import math

import jax
import jax.numpy as jnp
import numpy as np
from jax import lax
from jax.experimental import pallas as pl
from jax.experimental.pallas import tpu as pltpu
from jax.sharding import PartitionSpec as P

PRE = 2
POST = 2
COARSE = 6


OMEGA = 0.8

LANES = 128
TILE = 8
DEEP = 2 * COARSE + 2
NEAR = 3
FAR = COARSE


def with_halo(cells, sides, width):
    for axis, dim in sides:
        count = lax.axis_size(axis)
        ends = count - 1
        head = lax.slice_in_dim(cells, 0, width, axis=dim)
        tail = lax.slice_in_dim(cells, cells.shape[dim] - width, cells.shape[dim], axis=dim)
        cells = jnp.concatenate(
            [
                lax.ppermute(tail, axis, [(i, (i + 1) % count) for i in range(ends)]),
                cells,
                lax.ppermute(head, axis, [((i + 1) % count, i) for i in range(ends)]),
            ],
            axis=dim,
        )
    return cells


def level_coefficients(first_row, row_count, spacing, mode_numbers):
    row_number = (jnp.arange(row_count, dtype=jnp.int32) + first_row).astype(jnp.float32)
    radius = spacing * (row_number + 0.5)
    outward = (row_number + 1.0) / (spacing * radius)
    inward = row_number / (spacing * radius)
    vertical = 1.0 / (spacing * spacing)
    diagonal = (outward + inward + 2.0 * vertical)[None, :] + (
        mode_numbers[:, None] / radius[None, :]
    ) ** 2
    return (diagonal[:, :, None], outward[None, :, None], inward[None, :, None], vertical)


def apply_op(iterate, padded, coefficients):
    diagonal, outward, inward, vertical = coefficients
    return (
        diagonal * iterate
        - outward * padded[:, 2:, 1:-1]
        - inward * padded[:, :-2, 1:-1]
        - vertical * (padded[:, 1:-1, 2:] + padded[:, 1:-1, :-2])
    )


def relax(iterate, source, coefficients, pad_both):
    return (
        iterate
        + OMEGA * (source - apply_op(iterate, pad_both(iterate), coefficients)) / coefficients[0]
    )


def restrict(residual):
    k_count, r_count, z_count = residual.shape
    parts = residual.reshape(k_count, r_count // 2, 2, z_count // 2, 2)
    return 0.25 * (
        parts[:, :, 0, :, 0] + parts[:, :, 1, :, 0] + parts[:, :, 0, :, 1] + parts[:, :, 1, :, 1]
    )


def prolong(correction):
    return jnp.repeat(jnp.repeat(correction, 2, axis=1), 2, axis=2)


def pad_level(field):
    rows = with_halo(field, (("rad", 1),), 1)
    return jnp.pad(rows, ((0, 0), (0, 0), (1, 1)))


def mode_values(mode_index, azimuths):
    return jnp.where(mode_index <= azimuths // 2, mode_index, mode_index - azimuths // 2).astype(
        jnp.float32
    )


def fine_cycle(source, fine_coef, pad_sweep, coarse_solve):
    iterate = OMEGA * source / fine_coef[0]
    for sweep_index in range(PRE - 1):
        iterate = relax(iterate, source, fine_coef, pad_sweep)
    residual = source - apply_op(iterate, pad_sweep(iterate), fine_coef)
    iterate = iterate + prolong(coarse_solve(restrict(residual)))
    for sweep_index in range(POST):
        iterate = relax(iterate, source, fine_coef, pad_sweep)
    return iterate


def general_body(density):
    local_phi, local_rows, vertical_cells = density.shape
    az_count = lax.axis_size("az")
    azimuths = local_phi * az_count
    cell_count = local_rows * vertical_cells // az_count
    numbers = jnp.arange(azimuths, dtype=jnp.int32)
    all_modes = jnp.where(numbers <= azimuths // 2, numbers, numbers - azimuths // 2)
    phase = all_modes[:, None] * numbers[None, :] % azimuths
    phase_angle = phase.astype(jnp.float32) * (2.0 * math.pi / azimuths)
    analysis_table = jnp.where(
        (numbers <= azimuths // 2)[:, None], jnp.cos(phase_angle), jnp.sin(phase_angle)
    )
    synth_weight = jnp.where(
        (numbers == 0) | (numbers == azimuths // 2), 1.0 / azimuths, 2.0 / azimuths
    )
    synthesis_table = analysis_table.T * synth_weight[None, :]

    def transform_with(table, columns):
        width = columns.shape[2]
        matrix = columns.reshape(azimuths, width)
        result = jnp.dot(
            table, matrix, precision=lax.Precision.HIGHEST, preferred_element_type=jnp.float32
        )
        return result.reshape(azimuths, 1, width)

    lines = density.reshape(local_phi, az_count, cell_count)
    spectral = transform_with(
        analysis_table, lax.all_to_all(lines, "az", split_axis=1, concat_axis=0, tiled=True)
    )
    coefficients = lax.all_to_all(spectral, "az", split_axis=0, concat_axis=1, tiled=True)
    source = -coefficients.reshape(local_phi, local_rows, vertical_cells)
    rad_index = lax.axis_index("rad")
    half_rows = local_rows // 2
    mode_index = lax.axis_index("az") * local_phi + jnp.arange(local_phi, dtype=jnp.int32)
    mode_numbers = mode_values(mode_index, azimuths)
    fine_coef = level_coefficients(rad_index * local_rows, local_rows, 1.0, mode_numbers)
    coarse_coef = level_coefficients(rad_index * half_rows, half_rows, 2.0, mode_numbers)

    def coarse_halo(coarse_source):
        correction = OMEGA * coarse_source / coarse_coef[0]
        for sweep_index in range(COARSE - 1):
            correction = relax(correction, coarse_source, coarse_coef, pad_level)
        return correction

    iterate = fine_cycle(source, fine_coef, pad_level, coarse_halo)
    mode_lines = iterate.reshape(local_phi, az_count, cell_count)
    physical = transform_with(
        synthesis_table, lax.all_to_all(mode_lines, "az", split_axis=1, concat_axis=0, tiled=True)
    )
    field = lax.all_to_all(physical, "az", split_axis=0, concat_axis=1, tiled=True)
    return field.reshape(local_phi, local_rows, vertical_cells)


def mode_tables(azimuths):
    half = azimuths // 2
    even = np.concatenate([np.arange(0, half + 1, 2), np.arange(2, half, 2)])
    odd = np.concatenate([np.arange(1, half, 2), np.arange(1, half, 2)])
    even_cos = np.arange(half) <= half // 2
    odd_cos = np.arange(half) < half // 2
    modes = np.concatenate([even, odd])
    is_cos = np.concatenate([even_cos, odd_cos])
    angle = 2.0 * np.pi / azimuths * (np.arange(half)[:, None] * modes[None, :] % azimuths)
    values = np.where(is_cos[None, :], np.cos(angle), np.sin(angle))
    weight = np.where((modes == 0) | (modes == half), 1.0, 2.0) / azimuths
    return -values, values * weight[None, :]


def high_low(values):
    values = values.astype(np.float32)
    high = values.astype(jnp.bfloat16)
    low = (values - high.astype(np.float32)).astype(jnp.bfloat16)
    return jnp.asarray(high), jnp.asarray(low)


def split_value(value):
    high = value.astype(jnp.bfloat16)
    return high, (value - high.astype(jnp.float32)).astype(jnp.bfloat16)


def place():
    az = lax.axis_index("az")
    return lax.axis_index("rad"), az ^ (((az >> 2) & 1) << 1), lax.axis_size("az")


def mode_squares(shape):
    half = shape[0] * shape[1] // 2
    index = lax.broadcasted_iota(jnp.int32, shape, 0) * shape[1] + lax.broadcasted_iota(jnp.int32, shape, 1)
    even = 2 * jnp.where(index <= half // 2, index, index - half // 2)
    odd = 2 * (index & (half // 2 - 1)) + 1
    modes = jnp.where(index < half, even, odd)
    return (modes * modes).astype(jnp.float32)


def row_tile(position, local_rows, tile):
    return jnp.where(position[0] == 0, local_rows // TILE - 1 - tile, tile)


def chunk_masks(count, shape):
    lane = lax.broadcasted_iota(jnp.int32, shape, len(shape) - 1) // (LANES // count)
    return [lane == p for p in range(1, count)]


def pick_chunks(parts, masks):
    result = parts[0]
    for part, mask in zip(parts[1:], masks):
        result = jnp.where(mask, part, result)
    return result


def gather_rows(parts, masks):
    count = len(parts)
    chunk = LANES // count
    turned = [pltpu.roll(part, i * chunk, 1) if i else part for i, part in enumerate(parts)]
    return [pick_chunks([turned[(p - q) % count] for p in range(count)], masks) for q in range(count)]


def scatter_rows(parts, masks):
    count = len(parts)
    chunk = LANES // count
    rows = [pick_chunks([parts[(p - i) % count] for p in range(count)], masks) for i in range(count)]
    return [pltpu.roll(row, LANES - i * chunk, 1) if i else row for i, row in enumerate(rows)]


def turned_row(row, turn, rows):
    low = row & (rows - 1)
    return row - low + ((low + turn) & (rows - 1))


def tile_row(position, row):
    return jnp.where(position[0] == 0, TILE - 1 - row, row)


def pack_kernel(block, order, first_tile, x_ref, o_ref, x, o, in_sems, out_sems):
    position = place()
    rows = LANES // block
    local_phi, local_rows, cells = x_ref.shape
    tiles, lane_tiles, groups = x.shape[0], x.shape[1], TILE // rows
    pieces = [(j, k) for j in range(tiles) for k in range(lane_tiles)]
    masks = chunk_masks(rows, (local_phi, LANES))
    loads, stores = [], []
    for n, (j, k) in enumerate(pieces):
        start = pl.multiple_of(row_tile(position, local_rows, first_tile + j) * TILE, TILE)
        source = x_ref.at[:, pl.ds(start, TILE), k * LANES : (k + 1) * LANES]
        loads.append(pltpu.make_async_copy(source, x.at[j, k], in_sems.at[n]))
        loads[-1].start()
    for n, (j, k) in enumerate(pieces):
        loads[n].wait()
        flat = x.at[j, k].reshape(local_phi * TILE, LANES)
        for group in range(groups):
            parts = [
                flat[pl.ds(tile_row(position, group * rows + i), local_phi, stride=TILE), :]
                for i in range(rows)
            ]
            for q, part in enumerate(gather_rows(parts, masks)):
                o[order[k * rows + q], j * groups + group] = part
        if k == lane_tiles - 1:
            span = slice(j * groups, (j + 1) * groups)
            stores.append(pltpu.make_async_copy(o.at[:, span], o_ref.at[:, span], out_sems.at[j]))
            stores[-1].start()
    for store in stores:
        store.wait()


def unpack_kernel(block, order, x_ref, _, o_ref, x, o, in_sems, out_sems):
    position = place()
    rows = LANES // block
    local_phi, local_rows, cells = o_ref.shape
    tiles, lane_tiles, groups = o.shape[0], o.shape[1], TILE // rows
    masks = chunk_masks(rows, (local_phi, LANES))
    loads, stores = [], []
    for j in range(tiles):
        span = slice(j * groups, (j + 1) * groups)
        loads.append(pltpu.make_async_copy(x_ref.at[:, span], x.at[:, span], in_sems.at[j]))
        loads[-1].start()
    for j in range(tiles):
        loads[j].wait()
        start = pl.multiple_of(row_tile(position, local_rows, j) * TILE, TILE)
        for k in range(lane_tiles):
            flat = o.at[j, k].reshape(local_phi * TILE, LANES)
            for group in range(groups):
                parts = [x[order[k * rows + q], j * groups + group] for q in range(rows)]
                for i, part in enumerate(scatter_rows(parts, masks)):
                    at = tile_row(position, group * rows + i)
                    flat[pl.ds(at, local_phi, stride=TILE), :] = part
            target = o_ref.at[:, pl.ds(start, TILE), k * LANES : (k + 1) * LANES]
            stores.append(
                pltpu.make_async_copy(o.at[j, k], target, out_sems.at[j * lane_tiles + k])
            )
            stores[-1].start()
    for store in stores:
        store.wait()


def started(pairs, sems, first=0):
    copies = []
    for n, (src, dst) in enumerate(pairs):
        copies.append(pltpu.make_async_copy(src, dst, sems.at[first + n]))
        copies[-1].start()
    return copies


def finished(copies):
    for copy in copies:
        copy.wait()


def sides_of(field, depth):
    cells = field.shape[1]
    return field, field.at[:, :depth], field.at[:, cells - depth : cells]


def analysis_kernel(tile_groups, *refs):
    position = place()
    x_ref, high_ref, low_ref = refs[:3]
    outs = refs[3:-8]
    x, t_high, t_low, o, edge, in_sems, t_sems, out_sems = refs[-8:]
    if len(outs) == 2:
        held_refs = ()
    else:
        held_refs, outs = outs[:2], outs[2:]
    sources, width, lanes = x.shape[0], x.shape[2], x.shape[3]
    cells = o.shape[1]
    half = sources // 2 * width
    tiles = x.shape[1] // tile_groups
    spans = [slice(n * tile_groups, (n + 1) * tile_groups) for n in range(tiles)]
    pairs = [(x_ref.at[:, span], x.at[:, span]) for span in spans]
    tables = started([(high_ref, t_high), (low_ref, t_low)], t_sems)
    loads = started(pairs, in_sems)
    group_rows = TILE // tile_groups
    turn = position[1] & (group_rows - 1)
    gathers, start = [], 0
    for held in held_refs:
        span = slice(start, start + held.shape[0])
        sides = zip(sides_of(held, NEAR)[1:], (slice(0, NEAR), slice(NEAR, 2 * NEAR)))
        pairs = [(side, edge.at[span, columns]) for side, columns in sides]
        gathers += started(pairs, out_sems, out_sems.shape[0] - 4 + len(gathers))
        start += held.shape[0]
    stores = []
    for n in range(tiles):
        loads[n].wait()
        parts = []
        for parity in range(2):
            turned = []
            for group in range(n * tile_groups, (n + 1) * tile_groups):
                near, far = x[: sources // 2, group], x[sources // 2 :, group]
                folded = near + far if parity == 0 else near - far
                turned.append(folded.reshape(half, lanes).T)
            parts.append(split_value(jnp.concatenate(turned, axis=0)))
        if n == 0:
            finished(tables)
        rows = slice(n * TILE, (n + 1) * TILE)
        for parity, (high, low) in enumerate(parts):
            columns = slice(parity * half, (parity + 1) * half)
            result = (
                jnp.dot(high, t_high[:, columns], preferred_element_type=jnp.float32)
                + jnp.dot(high, t_low[:, columns], preferred_element_type=jnp.float32)
                + jnp.dot(low, t_high[:, columns], preferred_element_type=jnp.float32)
            )
            for part in range(half // LANES):
                piece = result[:, part * LANES : (part + 1) * LANES]
                o[rows, :, parity * (half // LANES) + part, :] = piece.reshape(TILE, cells, LANES)
        pairs = [
            (o.at[turned_row(row, turn, group_rows)], outs[0].at[row])
            for row in range(n * TILE, (n + 1) * TILE)
        ]
        stores += started(pairs, out_sems, len(stores))
    if held_refs:
        finished(gathers)
        for row in range(o.shape[0]):
            at = turned_row(row, turn, group_rows)
            edge[start + row, :NEAR] = o[at, :NEAR]
            edge[start + row, NEAR:] = o[at, cells - NEAR :]
        pairs = [(edge.at[:, :NEAR], outs[1]), (edge.at[:, NEAR:], outs[2])]
        stores += started(pairs, out_sems, len(stores))
    else:
        for row in range(DEEP):
            edge[DEEP - 1 - row] = o[turned_row(row, turn, group_rows)]
        stores += started([(edge, outs[1])], out_sems, len(stores))
    finished(stores)


def synthesis_tile(u, t_high, t_low, o):
    rows, cells = u.shape[0], u.shape[1]
    half = t_high.shape[0]
    parts = half // LANES
    sums = []
    for parity in range(2):
        field = jnp.concatenate(
            [u[:, :, parity * parts + i, :].reshape(rows * cells, LANES) for i in range(parts)],
            axis=1,
        )
        high, low = split_value(field)
        columns = slice(parity * half, (parity + 1) * half)
        contract = (((1,), (1,)), ((), ()))
        sums.append(
            lax.dot_general(t_high[:, columns], high, contract, preferred_element_type=jnp.float32)
            + lax.dot_general(t_high[:, columns], low, contract, preferred_element_type=jnp.float32)
            + lax.dot_general(t_low[:, columns], high, contract, preferred_element_type=jnp.float32)
        )
    near, far = sums[0] + sums[1], sums[0] - sums[1]
    targets, groups, width, lanes = o.shape
    for group in range(groups):
        columns = slice(group * lanes, (group + 1) * lanes)
        o[: targets // 2, group] = near[:, columns].reshape(targets // 2, width, lanes)
        o[targets // 2 :, group] = far[:, columns].reshape(targets // 2, width, lanes)


def row_weights(upper, boundary, first, count, squares, c_ref, ahead_ref, behind_ref):
    def one(index, carry):
        row = jnp.where(upper, index + (boundary + first), (boundary - 1 - first) - index)
        number = jnp.full(squares.shape, row, jnp.int32).astype(jnp.float32)
        radius = number + 0.5
        outward = (number + 1.0) / radius
        inward = number / radius
        diagonal = outward + inward + 2.0 + squares / (radius * radius)
        c_ref[index] = OMEGA / diagonal
        ahead_ref[index] = jnp.where(upper, outward, inward)
        behind_ref[index] = jnp.where(upper, inward, outward)
        return carry

    lax.fori_loop(0, count, one, 0)


def cell_tiles(first, last, cells, size=16):
    tiles = []
    if first < 0:
        tiles.append((first, -first, -1))
    for start in range(max(first, 0), min(last, cells), size):
        tiles.append((start, min(size, min(last, cells) - start), 0))
    if last > cells:
        tiles.append((cells, last - cells, 1))
    return tiles


def sweep(rows, cells, block, src, source, dst, weights, masks, turn=None):
    (src_ref, src_t, src_z), (dst_ref, dst_t, dst_z) = src, dst
    keep = 1.0 - OMEGA if source else 2.0 - OMEGA
    c_ref, ahead_ref, behind_ref, w_t = weights
    low = rows[0]

    def one(step, carry):
        at = step + (low - w_t)
        target = step + (low - dst_t)
        if turn:
            target = turned_row(target, *turn)
        c_row, ahead, behind = c_ref[at], ahead_ref[at], behind_ref[at]
        for first, count, side in cell_tiles(cells[0], cells[1], block):
            c = c_row if side == 0 else c_row * masks[0 if side < 0 else 1]
            z = first - src_z
            row = low - src_t
            middle = src_ref[step + row, z - 1 : z + count + 1]
            gathered = (
                ahead * src_ref[step + (row + 1), z : z + count]
                + behind * src_ref[step + (row - 1), z : z + count]
                + (middle[:-2] + middle[2:])
            )
            if source:
                g_ref, g_t, g_z = source
                gathered += g_ref[step + (low - g_t), first - g_z : first - g_z + count]
            dst_ref[target, first - dst_z : first - dst_z + count] = (
                keep * middle[1:-1] + c * gathered
            )
        return carry

    lax.fori_loop(0, rows[1] - low, one, 0)


def first_sweep(rows, cells, block, source, dst, weights, masks):
    (g_ref, g_t, g_z), (dst_ref, dst_t, dst_z) = source, dst
    c_ref, w_t = weights[0], weights[3]
    low = rows[0]

    def one(step, carry):
        c_row = c_ref[step + (low - w_t)]
        for first, count, side in cell_tiles(cells[0], cells[1], block):
            c = c_row if side == 0 else c_row * masks[0 if side < 0 else 1]
            dst_ref[step + (low - dst_t), first - dst_z : first - dst_z + count] = (
                c * g_ref[step + (low - g_t), first - g_z : first - g_z + count]
            )
        return carry

    lax.fori_loop(0, rows[1] - low, one, 0)


def side_masks(position, shape):
    left = jnp.full(shape, position[1] > 0).astype(jnp.float32)
    right = jnp.full(shape, position[1] < position[2] - 1).astype(jnp.float32)
    return left, right


def smooth_columns(local_rows, block, cells, g, u1, u2, s, weights, masks):
    first = -DEEP
    low, high = cells
    c_ref, ahead_ref, behind_ref, _ = weights
    g_at, u1_at, u2_at = (g, first, low), (u1, first, low), (u2, first + 1, low + 1)
    total = g.shape[0]
    u1[total] = jnp.zeros(u1.shape[1:], jnp.float32)
    u2[total - 1] = jnp.zeros(u2.shape[1:], jnp.float32)
    first_sweep((first, local_rows), cells, block, g_at, u1_at, weights, masks)
    sweep(
        (first + 1, local_rows), (low + 1, high - 1), block, u1_at, None, u2_at, weights, masks
    )
    start = max(low + 2, 0)
    start += start % 2

    def paired(values):
        pairs = values.reshape(values.shape[0] // 2, 2, *values.shape[1:])
        return pairs[:, 0], pairs[:, 1]

    def pair_sums(values):
        even, odd = paired(values)
        return even + odd

    def restrict_row(index, carry):
        row = 2 * index + (DEEP - 2 * FAR)
        center = behind_ref[row + 1] - OMEGA / c_ref[row] + 1.0
        center_ahead = ahead_ref[row] - OMEGA / c_ref[row + 1] + 1.0
        behind, ahead = behind_ref[row], ahead_ref[row + 1]
        for at, count, _ in cell_tiles(start, start + 2 * s.shape[1], block):
            z = at - u2_at[2]
            here = u2[row - 1, z - 1 : z + count + 1]
            there = u2[row, z - 1 : z + count + 1]
            even, odd = paired(here + there)
            cells = slice(at - low, at - low + count)
            column = (at - start) // 2
            s[index, column : column + count // 2] = (
                pair_sums(g[row, cells] + g[row + 1, cells])
                + (even[:-1] + odd[1:])
                + behind * pair_sums(u2[row - 2, z : z + count])
                + center * pair_sums(here[1:-1])
                + center_ahead * pair_sums(there[1:-1])
                + ahead * pair_sums(u2[row + 1, z : z + count])
            )
        return carry

    lax.fori_loop(0, s.shape[0], restrict_row, 0)


def inner_kernel(
    local_rows, block, deep_ref, near_ref, far_ref, u_ref, s_ref,
    g, u1, u2, s, c_ref, ahead_ref, behind_ref, in_sems, out_sems,
):
    pairs, start = [], 0
    for ref in (deep_ref, near_ref, far_ref):
        pairs.append((ref, g.at[start : start + ref.shape[0]]))
        start += ref.shape[0]
    loads = started(pairs, in_sems)
    position, squares = place(), mode_squares(c_ref.shape[1:])
    upper = position[0] == 1
    row_weights(upper, local_rows, -DEEP, DEEP + local_rows, squares, c_ref, ahead_ref, behind_ref)
    weights = (c_ref, ahead_ref, behind_ref, -DEEP)
    finished(loads)
    smooth_columns(local_rows, block, (0, block), g, u1, u2, s, weights, None)
    pairs = [(u2.at[DEEP - 3 : DEEP - 1 + local_rows], u_ref), (s, s_ref)]
    finished(started(pairs, out_sems))


def outer_kernel(
    local_rows, block,
    deep_ref, near_ref, far_ref, left_ref, right_ref, inner_ref,
    u_left_ref, u_right_ref, head_ref, tail_ref,
    g_left, g_right, u1, u2_left, u2_right, s_left, s_right, head, tail,
    c_ref, ahead_ref, behind_ref, in_sems, out_sems,
):
    wide = g_left.shape[1]
    own = wide - NEAR
    pairs, start = [], 0
    for ref in (deep_ref, near_ref, far_ref):
        span = slice(start, start + ref.shape[0])
        pairs.append((ref.at[:, :own], g_left.at[span, NEAR:]))
        pairs.append((ref.at[:, block - own :], g_right.at[span, :own]))
        start = span.stop
    pairs += [(left_ref, g_left.at[:, :NEAR]), (right_ref, g_right.at[:, own:])]
    inner = inner_ref.shape[1]
    pairs += [(inner_ref.at[:, : FAR - 1], head.at[:, 1:])]
    pairs += [(inner_ref.at[:, inner - FAR + 1 :], tail.at[:, : FAR - 1])]
    loads = started(pairs, in_sems)
    position, squares = place(), mode_squares(c_ref.shape[1:])
    upper = position[0] == 1
    row_weights(upper, local_rows, -DEEP, DEEP + local_rows, squares, c_ref, ahead_ref, behind_ref)
    masks = side_masks(position, squares.shape)
    weights = (c_ref, ahead_ref, behind_ref, -DEEP)
    finished(loads)
    rows = slice(DEEP - 3, DEEP - 1 + local_rows)
    smooth_columns(local_rows, block, (-NEAR, own), g_left, u1, u2_left, s_left, weights, masks)
    head[:, 0] = s_left[:, 0]
    pairs = [(u2_left.at[rows, :NEAR], u_left_ref), (head, head_ref)]
    stores = started(pairs, out_sems)
    smooth_columns(
        local_rows, block, (block - own, block + NEAR), g_right, u1, u2_right, s_right, weights, masks
    )
    tail[:, FAR - 1] = s_right[:, 0]
    pairs = [(u2_right.at[rows, wide - 2 - NEAR :], u_right_ref), (tail, tail_ref)]
    finished(stores + started(pairs, out_sems, 2))


def finish_kernel(local_rows, block, tile_groups, *refs):
    (
        high_ref, low_ref, o_ref,
        s, e0, e1, u, v, g, w, o, t_high, t_low,
        c_ref, ahead_ref, behind_ref, cc_ref, cahead_ref, cbehind_ref, in_sems, out_sems,
    ) = refs[-21:]
    s_inner, s_head, s_tail, s_left, s_right, u_inner, u_left, u_right = refs[:8]
    g_refs = refs[8:13]
    position, squares = place(), mode_squares(c_ref.shape[1:])
    upper = position[0] == 1
    half_rows, half = local_rows // 2, block // 2
    pairs = [
        (s_inner, s.at[:, FAR + 1 : FAR + half - 1]),
        (s_head.at[:, 0:1], s.at[:, FAR : FAR + 1]),
        (s_tail.at[:, FAR - 1 : FAR], s.at[:, FAR + half - 1 : FAR + half]),
        (s_left, s.at[:, 0:FAR]),
        (s_right, s.at[:, FAR + half : FAR + half + FAR]),
    ]
    s_loads = started(pairs, in_sems)
    u_rows = slice(0, local_rows + 2)
    pairs, start = [
        (u_left, u.at[u_rows, :NEAR]),
        (u_inner, u.at[u_rows, NEAR : NEAR + block - 2]),
        (u_right, u.at[u_rows, NEAR + block - 2 :]),
    ], 0
    middle = slice(1, 1 + block)
    for ref in g_refs[:3]:
        rows = slice(DEEP - 1, DEEP) if start == 0 else slice(0, ref.shape[0])
        count = rows.stop - rows.start
        pairs.append((ref.at[rows], g.at[start : start + count, middle]))
        start += count
    rows = slice(DEEP - 1, DEEP + local_rows)
    pairs.append((g_refs[3].at[rows, NEAR - 1 : NEAR], g.at[:, 0:1]))
    pairs.append((g_refs[4].at[rows, 0:1], g.at[:, 1 + block : 2 + block]))
    pairs += [(high_ref, t_high), (low_ref, t_low)]
    loads = started(pairs, in_sems, len(s_loads))
    masks = side_masks(position, squares.shape)
    row_weights(upper, half_rows, -FAR, FAR + half_rows, squares, cc_ref, cahead_ref, cbehind_ref)
    row_weights(upper, local_rows, -1, 1 + local_rows, squares, c_ref, ahead_ref, behind_ref)
    coarse = (cc_ref, cahead_ref, cbehind_ref, -FAR)
    fine = (c_ref, ahead_ref, behind_ref, -1)
    for buffer in (e0, e1):
        buffer[FAR + half_rows] = jnp.zeros(buffer.shape[1:], jnp.float32)
    u[2 + local_rows] = jnp.zeros(u.shape[1:], jnp.float32)
    v[1 + local_rows] = jnp.zeros(v.shape[1:], jnp.float32)
    finished(s_loads)
    s_at = (s, -FAR, -FAR)
    here, there = (e0, -FAR, -FAR), (e1, -FAR, -FAR)
    first_sweep((-FAR, half_rows), (-FAR, half + FAR), half, s_at, here, coarse, masks)
    for step in range(1, COARSE):
        sweep(
            (step - FAR, half_rows), (step - FAR, half + FAR - step), half, here, s_at if step > 1 else None, there, coarse, masks
        )
        here, there = there, here
    e = here[0]
    finished(loads)

    def add_correction(index, carry):
        for first, count in ((-1, (half + 2) // 2), (-1 + (half + 2) // 2, half + 2 - (half + 2) // 2)):
            part = e[index + FAR - 1, first + FAR : first + FAR + count]
            twice = jnp.broadcast_to(part[:, None], (count, 2) + part.shape[1:])
            twice = twice.reshape(2 * count, *part.shape[1:])
            cells = slice(2 * first + 2, 2 * first + 2 + 2 * count)
            for offset in range(2):
                u[2 * index + offset, cells] = u[2 * index + offset, cells] + twice
        return carry

    lax.fori_loop(0, half_rows + 1, add_correction, 0)
    u_at, v_at, g_at = (u, -2, -2), (v, -1, -1), (g, -1, -1)
    sweep((-1, local_rows), (-1, block + 1), block, u_at, g_at, v_at, fine, masks)
    group_rows = TILE // tile_groups
    turn = (position[1] & (group_rows - 1), group_rows)
    sweep((0, local_rows), (0, block), block, v_at, g_at, (w, 0, 0), fine, masks, turn)
    stores = []
    for n in range(local_rows // TILE):
        span = slice(n * tile_groups, (n + 1) * tile_groups)
        synthesis_tile(w.at[n * TILE : (n + 1) * TILE], t_high, t_low, o.at[:, span])
        stores += started([(o.at[:, span], o_ref.at[:, span])], out_sems, n)
    finished(stores)


def params(mebibytes, *order):
    return pltpu.CompilerParams(
        dimension_semantics=order or None, vmem_limit_bytes=mebibytes * 1024 * 1024
    )


def cell_body(density):
    local_phi, local_rows, vertical_cells = density.shape
    az_count = lax.axis_size("az")
    azimuths = local_phi * az_count
    block = vertical_cells // az_count
    rows = LANES // block
    tiles = local_rows // TILE
    groups = TILE // rows
    chunks = 2
    chunk_tiles = tiles // chunks
    chunk_rows = local_rows // chunks
    analysis, synthesis = mode_tables(azimuths)
    point = (azimuths // LANES, LANES)
    f32 = jnp.float32
    a_high, a_low = high_low(analysis)
    s_high, s_low = high_low(synthesis)
    order = block_order(az_count)
    product = 2 * 3 * azimuths * azimuths // 2
    lane_tiles = vertical_cells // LANES
    anywhere = pl.BlockSpec(memory_space=pl.ANY)
    in_hbm = pl.BlockSpec(memory_space=pltpu.HBM)

    def field(row_count, cell_count):
        return jax.ShapeDtypeStruct((row_count, cell_count) + point, f32)

    def scratch(row_count, *cell_count):
        return pltpu.VMEM((row_count,) + cell_count + point, f32)

    def semaphores(count):
        return pltpu.SemaphoreType.DMA((count,))

    def cost(mebibytes):
        return pl.CostEstimate(flops=0, bytes_accessed=mebibytes * 1024 * 1024, transcendentals=0)

    def pack(first_tile):
        return pl.pallas_call(
            lambda *refs: pack_kernel(block, order, first_tile, *refs),
            in_specs=[in_hbm],
            out_specs=in_hbm,
            out_shape=jax.ShapeDtypeStruct(
                (az_count, chunk_tiles * groups, local_phi, LANES), f32
            ),
            scratch_shapes=[
                pltpu.VMEM((chunk_tiles, lane_tiles, local_phi, TILE, LANES), f32),
                pltpu.VMEM((az_count, chunk_tiles * groups, local_phi, LANES), f32),
                pltpu.SemaphoreType.DMA((chunk_tiles * lane_tiles,)),
                pltpu.SemaphoreType.DMA((chunk_tiles,)),
            ],
            compiler_params=params(56),
            name="pack",
        )(density)

    half_rows, half = local_rows // 2, block // 2
    all_rows, coarse_rows = DEEP + local_rows, FAR + half_rows
    tables = [pltpu.VMEM((azimuths // 2, azimuths), jnp.bfloat16)] * 2

    def analyse(received, held):
        out_shape = [field(chunk_rows, block)]
        out_shape += [field(all_rows, NEAR)] * 2 if held else [field(DEEP, block)]
        return pl.pallas_call(
            lambda *refs: analysis_kernel(groups, *refs),
            in_specs=[in_hbm] * 3 + [anywhere] * len(held),
            out_specs=[anywhere] * len(out_shape),
            out_shape=out_shape,
            scratch_shapes=[
                pltpu.VMEM((az_count, chunk_tiles * groups, local_phi, LANES), f32),
                *tables,
                scratch(chunk_rows, block),
                scratch(all_rows, 2 * NEAR) if held else scratch(DEEP, block),
                semaphores(chunk_tiles),
                semaphores(2),
                semaphores(chunk_rows + 6),
            ],
            compiler_params=params(56),
            cost_estimate=cost(12),
            name="analysis",
        )(received, a_high, a_low, *held)

    def exchange(value):
        return lax.all_to_all(value, "az", split_axis=0, concat_axis=0, tiled=True)

    to_right = [(order[i], order[i + 1]) for i in range(az_count - 1)]
    to_left = [(b, a) for a, b in to_right]

    def from_sides(head, tail):
        return lax.ppermute(tail, "az", to_right), lax.ppermute(head, "az", to_left)

    first_received = exchange(pack(0))
    second_received = exchange(pack(chunk_tiles))
    near, edge = analyse(first_received, ())
    deep = lax.ppermute(edge, "rad", [(0, 1), (1, 0)])
    far, head, tail = analyse(second_received, (deep, near))
    fields = (deep, near, far, *from_sides(head, tail))

    wide = 2 * NEAR + 1
    weight_scratch = [scratch(all_rows)] * 3
    u_inner, s_inner = pl.pallas_call(
        lambda *refs: inner_kernel(local_rows, block, *refs),
        in_specs=[anywhere] * 3,
        out_specs=[anywhere] * 2,
        out_shape=[field(local_rows + 2, block - 2), field(coarse_rows, half - 2)],
        scratch_shapes=[
            scratch(all_rows, block),
            scratch(all_rows + 1, block),
            scratch(all_rows, block - 2),
            scratch(coarse_rows, half - 2),
            *weight_scratch,
            semaphores(3),
            semaphores(2),
        ],
        compiler_params=params(28),
        cost_estimate=cost(32),
        name="inner",
    )(*fields[:3])
    u_left, u_right, s_head, s_tail = pl.pallas_call(
        lambda *refs: outer_kernel(local_rows, block, *refs),
        in_specs=[anywhere] * 6,
        out_specs=[anywhere] * 4,
        out_shape=[field(local_rows + 2, NEAR)] * 2 + [field(coarse_rows, FAR)] * 2,
        scratch_shapes=[
            scratch(all_rows, wide),
            scratch(all_rows, wide),
            scratch(all_rows + 1, wide),
            scratch(all_rows, wide - 2),
            scratch(all_rows, wide - 2),
            scratch(coarse_rows, 1),
            scratch(coarse_rows, 1),
            scratch(coarse_rows, FAR),
            scratch(coarse_rows, FAR),
            *weight_scratch,
            semaphores(10),
            semaphores(4),
        ],
        compiler_params=params(20),
        cost_estimate=cost(12),
        name="outer",
    )(*fields, s_inner)
    s_parts = (s_inner, s_head, s_tail, *from_sides(s_head, s_tail))

    received_shape = (az_count, tiles * groups, local_phi, LANES)
    physical = pl.pallas_call(
        lambda *refs: finish_kernel(local_rows, block, groups, *refs),
        in_specs=[anywhere] * 13 + [in_hbm] * 2,
        out_specs=in_hbm,
        out_shape=jax.ShapeDtypeStruct(received_shape, f32),
        scratch_shapes=[
            scratch(coarse_rows, half + 2 * FAR),
            scratch(coarse_rows + 1, half + 2 * FAR),
            scratch(coarse_rows + 1, half + 2 * FAR),
            scratch(local_rows + 3, block + 4),
            scratch(local_rows + 2, block + 2),
            scratch(local_rows + 1, block + 2),
            scratch(local_rows, block),
            pltpu.VMEM(received_shape, f32),
            *tables,
            scratch(local_rows + 1),
            scratch(local_rows + 1),
            scratch(local_rows + 1),
            scratch(coarse_rows),
            scratch(coarse_rows),
            scratch(coarse_rows),
            semaphores(15),
            semaphores(tiles),
        ],
        compiler_params=params(46),
        name="finish",
    )(*s_parts, u_inner, u_left, u_right, *fields, s_high, s_low)

    returned = exchange(physical)
    side = jnp.stack([lax.axis_index("rad"), lax.axis_index("az")]).astype(jnp.int32)
    return pl.pallas_call(
        lambda *refs: unpack_kernel(block, order, *refs),
        in_specs=[in_hbm, anywhere],
        out_specs=in_hbm,
        out_shape=jax.ShapeDtypeStruct(density.shape, f32),
        scratch_shapes=[
            pltpu.VMEM((az_count, tiles * groups, local_phi, LANES), f32),
            pltpu.VMEM((tiles, lane_tiles, local_phi, TILE, LANES), f32),
            pltpu.SemaphoreType.DMA((tiles,)),
            pltpu.SemaphoreType.DMA((tiles * lane_tiles,)),
        ],
        compiler_params=params(56),
        name="unpack",
    )(returned, side)


def block_order(az_count):
    return [i ^ 2 if (i // 4) % 2 else i for i in range(az_count)]


def fits_cells(density):
    local_phi, local_rows, vertical_cells = density.shape
    az_count, rad_count = lax.axis_size("az"), lax.axis_size("rad")
    block = vertical_cells // az_count
    return (
        rad_count == 2
        and vertical_cells % (az_count * 2) == 0
        and vertical_cells % LANES == 0
        and LANES // TILE <= block <= LANES
        and LANES % block == 0
        and block // 2 >= FAR
        and local_rows % (4 * TILE) == 0
        and local_rows // 2 >= DEEP
        and az_count % 4 == 0
        and local_phi % TILE == 0
        and (az_count * local_phi) % (2 * LANES) == 0
        and az_count * local_phi == TILE * LANES
    )


def body(density):
    return cell_body(density) if fits_cells(density) else general_body(density)


def solution(mesh):
    placed = (P("az", "rad", None),)
    return jax.shard_map(
        body, mesh=mesh, in_specs=placed, out_specs=P("az", "rad", None), check_vma=False
    )
```

```python
import math

import jax
import jax.numpy as jnp
import numpy as np
from jax import lax
from jax.experimental import pallas as pl
from jax.experimental.pallas import tpu as pltpu
from jax.sharding import PartitionSpec as P

PRE = 2
POST = 2
COARSE = 6


OMEGA = 0.8

LANES = 128
TILE = 8
DEEP = 2 * COARSE + 2
NEAR = 3
FAR = COARSE


def with_halo(cells, sides, width):
    for axis, dim in sides:
        count = lax.axis_size(axis)
        ends = count - 1
        head = lax.slice_in_dim(cells, 0, width, axis=dim)
        tail = lax.slice_in_dim(cells, cells.shape[dim] - width, cells.shape[dim], axis=dim)
        cells = jnp.concatenate(
            [
                lax.ppermute(tail, axis, [(i, (i + 1) % count) for i in range(ends)]),
                cells,
                lax.ppermute(head, axis, [((i + 1) % count, i) for i in range(ends)]),
            ],
            axis=dim,
        )
    return cells


def level_coefficients(first_row, row_count, spacing, mode_numbers):
    row_number = (jnp.arange(row_count, dtype=jnp.int32) + first_row).astype(jnp.float32)
    radius = spacing * (row_number + 0.5)
    outward = (row_number + 1.0) / (spacing * radius)
    inward = row_number / (spacing * radius)
    vertical = 1.0 / (spacing * spacing)
    diagonal = (outward + inward + 2.0 * vertical)[None, :] + (
        mode_numbers[:, None] / radius[None, :]
    ) ** 2
    return (diagonal[:, :, None], outward[None, :, None], inward[None, :, None], vertical)


def apply_op(iterate, padded, coefficients):
    diagonal, outward, inward, vertical = coefficients
    return (
        diagonal * iterate
        - outward * padded[:, 2:, 1:-1]
        - inward * padded[:, :-2, 1:-1]
        - vertical * (padded[:, 1:-1, 2:] + padded[:, 1:-1, :-2])
    )


def relax(iterate, source, coefficients, pad_both):
    return (
        iterate
        + OMEGA * (source - apply_op(iterate, pad_both(iterate), coefficients)) / coefficients[0]
    )


def restrict(residual):
    k_count, r_count, z_count = residual.shape
    parts = residual.reshape(k_count, r_count // 2, 2, z_count // 2, 2)
    return 0.25 * (
        parts[:, :, 0, :, 0] + parts[:, :, 1, :, 0] + parts[:, :, 0, :, 1] + parts[:, :, 1, :, 1]
    )


def prolong(correction):
    return jnp.repeat(jnp.repeat(correction, 2, axis=1), 2, axis=2)


def pad_level(field):
    rows = with_halo(field, (("rad", 1),), 1)
    return jnp.pad(rows, ((0, 0), (0, 0), (1, 1)))


def mode_values(mode_index, azimuths):
    return jnp.where(mode_index <= azimuths // 2, mode_index, mode_index - azimuths // 2).astype(
        jnp.float32
    )


def fine_cycle(source, fine_coef, pad_sweep, coarse_solve):
    iterate = OMEGA * source / fine_coef[0]
    for sweep_index in range(PRE - 1):
        iterate = relax(iterate, source, fine_coef, pad_sweep)
    residual = source - apply_op(iterate, pad_sweep(iterate), fine_coef)
    iterate = iterate + prolong(coarse_solve(restrict(residual)))
    for sweep_index in range(POST):
        iterate = relax(iterate, source, fine_coef, pad_sweep)
    return iterate


def general_body(density):
    local_phi, local_rows, vertical_cells = density.shape
    az_count = lax.axis_size("az")
    azimuths = local_phi * az_count
    cell_count = local_rows * vertical_cells // az_count
    numbers = jnp.arange(azimuths, dtype=jnp.int32)
    all_modes = jnp.where(numbers <= azimuths // 2, numbers, numbers - azimuths // 2)
    phase = all_modes[:, None] * numbers[None, :] % azimuths
    phase_angle = phase.astype(jnp.float32) * (2.0 * math.pi / azimuths)
    analysis_table = jnp.where(
        (numbers <= azimuths // 2)[:, None], jnp.cos(phase_angle), jnp.sin(phase_angle)
    )
    synth_weight = jnp.where(
        (numbers == 0) | (numbers == azimuths // 2), 1.0 / azimuths, 2.0 / azimuths
    )
    synthesis_table = analysis_table.T * synth_weight[None, :]

    def transform_with(table, columns):
        width = columns.shape[2]
        matrix = columns.reshape(azimuths, width)
        result = jnp.dot(
            table, matrix, precision=lax.Precision.HIGHEST, preferred_element_type=jnp.float32
        )
        return result.reshape(azimuths, 1, width)

    lines = density.reshape(local_phi, az_count, cell_count)
    spectral = transform_with(
        analysis_table, lax.all_to_all(lines, "az", split_axis=1, concat_axis=0, tiled=True)
    )
    coefficients = lax.all_to_all(spectral, "az", split_axis=0, concat_axis=1, tiled=True)
    source = -coefficients.reshape(local_phi, local_rows, vertical_cells)
    rad_index = lax.axis_index("rad")
    half_rows = local_rows // 2
    mode_index = lax.axis_index("az") * local_phi + jnp.arange(local_phi, dtype=jnp.int32)
    mode_numbers = mode_values(mode_index, azimuths)
    fine_coef = level_coefficients(rad_index * local_rows, local_rows, 1.0, mode_numbers)
    coarse_coef = level_coefficients(rad_index * half_rows, half_rows, 2.0, mode_numbers)

    def coarse_halo(coarse_source):
        correction = OMEGA * coarse_source / coarse_coef[0]
        for sweep_index in range(COARSE - 1):
            correction = relax(correction, coarse_source, coarse_coef, pad_level)
        return correction

    iterate = fine_cycle(source, fine_coef, pad_level, coarse_halo)
    mode_lines = iterate.reshape(local_phi, az_count, cell_count)
    physical = transform_with(
        synthesis_table, lax.all_to_all(mode_lines, "az", split_axis=1, concat_axis=0, tiled=True)
    )
    field = lax.all_to_all(physical, "az", split_axis=0, concat_axis=1, tiled=True)
    return field.reshape(local_phi, local_rows, vertical_cells)


def mode_tables(azimuths):
    half = azimuths // 2
    even = np.concatenate([np.arange(0, half + 1, 2), np.arange(2, half, 2)])
    odd = np.concatenate([np.arange(1, half, 2), np.arange(1, half, 2)])
    even_cos = np.arange(half) <= half // 2
    odd_cos = np.arange(half) < half // 2
    modes = np.concatenate([even, odd])
    is_cos = np.concatenate([even_cos, odd_cos])
    angle = 2.0 * np.pi / azimuths * (np.arange(half)[:, None] * modes[None, :] % azimuths)
    values = np.where(is_cos[None, :], np.cos(angle), np.sin(angle))
    weight = np.where((modes == 0) | (modes == half), 1.0, 2.0) / azimuths
    return -values, values * weight[None, :]


def high_low(values):
    values = values.astype(np.float32)
    high = values.astype(jnp.bfloat16)
    low = (values - high.astype(np.float32)).astype(jnp.bfloat16)
    return jnp.asarray(high), jnp.asarray(low)


def split_value(value):
    high = value.astype(jnp.bfloat16)
    return high, (value - high.astype(jnp.float32)).astype(jnp.bfloat16)


def place():
    az = lax.axis_index("az")
    return lax.axis_index("rad"), az ^ (((az >> 2) & 1) << 1), lax.axis_size("az")


def mode_squares(shape):
    half = shape[0] * shape[1] // 2
    index = lax.broadcasted_iota(jnp.int32, shape, 0) * shape[1] + lax.broadcasted_iota(jnp.int32, shape, 1)
    even = 2 * jnp.where(index <= half // 2, index, index - half // 2)
    odd = 2 * (index & (half // 2 - 1)) + 1
    modes = jnp.where(index < half, even, odd)
    return (modes * modes).astype(jnp.float32)


def row_tile(position, local_rows, tile):
    return jnp.where(position[0] == 0, local_rows // TILE - 1 - tile, tile)


def chunk_masks(count, shape):
    lane = lax.broadcasted_iota(jnp.int32, shape, len(shape) - 1) // (LANES // count)
    return [lane == p for p in range(1, count)]


def pick_chunks(parts, masks):
    result = parts[0]
    for part, mask in zip(parts[1:], masks):
        result = jnp.where(mask, part, result)
    return result


def gather_rows(parts, masks):
    count = len(parts)
    chunk = LANES // count
    turned = [pltpu.roll(part, i * chunk, 1) if i else part for i, part in enumerate(parts)]
    return [pick_chunks([turned[(p - q) % count] for p in range(count)], masks) for q in range(count)]


def scatter_rows(parts, masks):
    count = len(parts)
    chunk = LANES // count
    rows = [pick_chunks([parts[(p - i) % count] for p in range(count)], masks) for i in range(count)]
    return [pltpu.roll(row, LANES - i * chunk, 1) if i else row for i, row in enumerate(rows)]


def turned_row(row, turn, rows):
    low = row & (rows - 1)
    return row - low + ((low + turn) & (rows - 1))


def tile_row(position, row):
    return jnp.where(position[0] == 0, TILE - 1 - row, row)


def pack_kernel(block, order, first_tile, x_ref, o_ref, x, o, in_sems, out_sems):
    position = place()
    rows = LANES // block
    local_phi, local_rows, cells = x_ref.shape
    tiles, lane_tiles, groups = x.shape[0], x.shape[1], TILE // rows
    pieces = [(j, k) for j in range(tiles) for k in range(lane_tiles)]
    masks = chunk_masks(rows, (local_phi, LANES))
    loads, stores = [], []
    for n, (j, k) in enumerate(pieces):
        start = pl.multiple_of(row_tile(position, local_rows, first_tile + j) * TILE, TILE)
        source = x_ref.at[:, pl.ds(start, TILE), k * LANES : (k + 1) * LANES]
        loads.append(pltpu.make_async_copy(source, x.at[j, k], in_sems.at[n]))
        loads[-1].start()
    for n, (j, k) in enumerate(pieces):
        loads[n].wait()
        flat = x.at[j, k].reshape(local_phi * TILE, LANES)
        for group in range(groups):
            parts = [
                flat[pl.ds(tile_row(position, group * rows + i), local_phi, stride=TILE), :]
                for i in range(rows)
            ]
            for q, part in enumerate(gather_rows(parts, masks)):
                o[order[k * rows + q], j * groups + group] = part
        if k == lane_tiles - 1:
            span = slice(j * groups, (j + 1) * groups)
            stores.append(pltpu.make_async_copy(o.at[:, span], o_ref.at[:, span], out_sems.at[j]))
            stores[-1].start()
    for store in stores:
        store.wait()


def unpack_kernel(block, order, x_ref, _, o_ref, x, o, in_sems, out_sems):
    position = place()
    rows = LANES // block
    local_phi, local_rows, cells = o_ref.shape
    tiles, lane_tiles, groups = o.shape[0], o.shape[1], TILE // rows
    masks = chunk_masks(rows, (local_phi, LANES))
    loads, stores = [], []
    for j in range(tiles):
        span = slice(j * groups, (j + 1) * groups)
        loads.append(pltpu.make_async_copy(x_ref.at[:, span], x.at[:, span], in_sems.at[j]))
        loads[-1].start()
    for j in range(tiles):
        loads[j].wait()
        start = pl.multiple_of(row_tile(position, local_rows, j) * TILE, TILE)
        for k in range(lane_tiles):
            flat = o.at[j, k].reshape(local_phi * TILE, LANES)
            for group in range(groups):
                parts = [x[order[k * rows + q], j * groups + group] for q in range(rows)]
                for i, part in enumerate(scatter_rows(parts, masks)):
                    at = tile_row(position, group * rows + i)
                    flat[pl.ds(at, local_phi, stride=TILE), :] = part
            target = o_ref.at[:, pl.ds(start, TILE), k * LANES : (k + 1) * LANES]
            stores.append(
                pltpu.make_async_copy(o.at[j, k], target, out_sems.at[j * lane_tiles + k])
            )
            stores[-1].start()
    for store in stores:
        store.wait()


def started(pairs, sems, first=0):
    copies = []
    for n, (src, dst) in enumerate(pairs):
        copies.append(pltpu.make_async_copy(src, dst, sems.at[first + n]))
        copies[-1].start()
    return copies


def finished(copies):
    for copy in copies:
        copy.wait()


def sides_of(field, depth):
    cells = field.shape[1]
    return field, field.at[:, :depth], field.at[:, cells - depth : cells]


def analysis_kernel(tile_groups, held_count, *refs):
    position = place()
    x_ref, high_ref, low_ref = refs[:3]
    outs = refs[3:-8]
    x, t_high, t_low, o, edge, in_sems, t_sems, out_sems = refs[-8:]
    held_refs, outs = outs[:held_count], outs[held_count:]
    sources, width, lanes = x.shape[0], x.shape[2], x.shape[3]
    cells = o.shape[1]
    half = sources // 2 * width
    tiles = x.shape[1] // tile_groups
    spans = [slice(n * tile_groups, (n + 1) * tile_groups) for n in range(tiles)]
    pairs = [(x_ref.at[:, span], x.at[:, span]) for span in spans]
    tables = started([(high_ref, t_high), (low_ref, t_low)], t_sems)
    loads = started(pairs, in_sems)
    group_rows = TILE // tile_groups
    turn = position[1] & (group_rows - 1)
    gathers, start = [], 0
    for held in held_refs:
        span = slice(start, start + held.shape[0])
        if held.shape[1] == 2 * NEAR:
            pairs = [(held, edge.at[span])]
        else:
            sides = zip(sides_of(held, NEAR)[1:], (slice(0, NEAR), slice(NEAR, 2 * NEAR)))
            pairs = [(side, edge.at[span, columns]) for side, columns in sides]
        gathers += started(pairs, out_sems, out_sems.shape[0] - 4 + len(gathers))
        start += held.shape[0]
    stores = []
    for n in range(tiles):
        loads[n].wait()
        parts = []
        for parity in range(2):
            turned = []
            for group in range(n * tile_groups, (n + 1) * tile_groups):
                near, far = x[: sources // 2, group], x[sources // 2 :, group]
                folded = near + far if parity == 0 else near - far
                turned.append(folded.reshape(half, lanes).T)
            parts.append(split_value(jnp.concatenate(turned, axis=0)))
        if n == 0:
            finished(tables)
        rows = slice(n * TILE, (n + 1) * TILE)
        for parity, (high, low) in enumerate(parts):
            columns = slice(parity * half, (parity + 1) * half)
            result = (
                jnp.dot(high, t_high[:, columns], preferred_element_type=jnp.float32)
                + jnp.dot(high, t_low[:, columns], preferred_element_type=jnp.float32)
                + jnp.dot(low, t_high[:, columns], preferred_element_type=jnp.float32)
            )
            for part in range(half // LANES):
                piece = result[:, part * LANES : (part + 1) * LANES]
                o[rows, :, parity * (half // LANES) + part, :] = piece.reshape(TILE, cells, LANES)
        pairs = [
            (o.at[turned_row(row, turn, group_rows)], outs[0].at[row])
            for row in range(n * TILE, (n + 1) * TILE)
        ]
        stores += started(pairs, out_sems, len(stores))
    if held_refs:
        finished(gathers)
        for row in range(o.shape[0]):
            at = turned_row(row, turn, group_rows)
            edge[start + row, :NEAR] = o[at, :NEAR]
            edge[start + row, NEAR:] = o[at, cells - NEAR :]
        pairs = [(edge.at[:, :NEAR], outs[1]), (edge.at[:, NEAR:], outs[2])]
        stores += started(pairs, out_sems, len(stores))
    else:
        for row in range(DEEP):
            edge[DEEP - 1 - row] = o[turned_row(row, turn, group_rows)]
        _, head, tail = sides_of(edge, NEAR)
        pairs = [(head, outs[1].at[:, :NEAR]), (tail, outs[1].at[:, NEAR:]), (edge, outs[2])]
        stores += started(pairs, out_sems, len(stores))
    finished(stores)


def synthesis_tile(u, t_high, t_low, o):
    rows, cells = u.shape[0], u.shape[1]
    half = t_high.shape[0]
    parts = half // LANES
    sums = []
    for parity in range(2):
        field = jnp.concatenate(
            [u[:, :, parity * parts + i, :].reshape(rows * cells, LANES) for i in range(parts)],
            axis=1,
        )
        high, low = split_value(field)
        columns = slice(parity * half, (parity + 1) * half)
        contract = (((1,), (1,)), ((), ()))
        sums.append(
            lax.dot_general(t_high[:, columns], high, contract, preferred_element_type=jnp.float32)
            + lax.dot_general(t_high[:, columns], low, contract, preferred_element_type=jnp.float32)
            + lax.dot_general(t_low[:, columns], high, contract, preferred_element_type=jnp.float32)
        )
    near, far = sums[0] + sums[1], sums[0] - sums[1]
    targets, groups, width, lanes = o.shape
    for group in range(groups):
        columns = slice(group * lanes, (group + 1) * lanes)
        o[: targets // 2, group] = near[:, columns].reshape(targets // 2, width, lanes)
        o[targets // 2 :, group] = far[:, columns].reshape(targets // 2, width, lanes)


def row_weights(upper, boundary, first, count, squares, c_ref, ahead_ref, behind_ref):
    def one(index, carry):
        row = jnp.where(upper, index + (boundary + first), (boundary - 1 - first) - index)
        number = jnp.full(squares.shape, row, jnp.int32).astype(jnp.float32)
        radius = number + 0.5
        outward = (number + 1.0) / radius
        inward = number / radius
        diagonal = outward + inward + 2.0 + squares / (radius * radius)
        c_ref[index] = OMEGA / diagonal
        ahead_ref[index] = jnp.where(upper, outward, inward)
        behind_ref[index] = jnp.where(upper, inward, outward)
        return carry

    lax.fori_loop(0, count, one, 0)


def cell_tiles(first, last, cells, size=16):
    tiles = []
    if first < 0:
        tiles.append((first, -first, -1))
    for start in range(max(first, 0), min(last, cells), size):
        tiles.append((start, min(size, min(last, cells) - start), 0))
    if last > cells:
        tiles.append((cells, last - cells, 1))
    return tiles


def sweep(rows, cells, block, src, source, dst, weights, masks, turn=None):
    (src_ref, src_t, src_z), (dst_ref, dst_t, dst_z) = src, dst
    keep = 1.0 - OMEGA if source else 2.0 - OMEGA
    c_ref, ahead_ref, behind_ref, w_t = weights
    low = rows[0]

    def one(step, carry):
        at = step + (low - w_t)
        target = step + (low - dst_t)
        if turn:
            target = turned_row(target, *turn)
        c_row, ahead, behind = c_ref[at], ahead_ref[at], behind_ref[at]
        for first, count, side in cell_tiles(cells[0], cells[1], block):
            c = c_row if side == 0 else c_row * masks[0 if side < 0 else 1]
            z = first - src_z
            row = low - src_t
            middle = src_ref[step + row, z - 1 : z + count + 1]
            gathered = (
                ahead * src_ref[step + (row + 1), z : z + count]
                + behind * src_ref[step + (row - 1), z : z + count]
                + (middle[:-2] + middle[2:])
            )
            if source:
                g_ref, g_t, g_z = source
                gathered += g_ref[step + (low - g_t), first - g_z : first - g_z + count]
            dst_ref[target, first - dst_z : first - dst_z + count] = (
                keep * middle[1:-1] + c * gathered
            )
        return carry

    lax.fori_loop(0, rows[1] - low, one, 0)


def first_sweep(rows, cells, block, source, dst, weights, masks):
    (g_ref, g_t, g_z), (dst_ref, dst_t, dst_z) = source, dst
    c_ref, w_t = weights[0], weights[3]
    low = rows[0]

    def one(step, carry):
        c_row = c_ref[step + (low - w_t)]
        for first, count, side in cell_tiles(cells[0], cells[1], block):
            c = c_row if side == 0 else c_row * masks[0 if side < 0 else 1]
            dst_ref[step + (low - dst_t), first - dst_z : first - dst_z + count] = (
                c * g_ref[step + (low - g_t), first - g_z : first - g_z + count]
            )
        return carry

    lax.fori_loop(0, rows[1] - low, one, 0)


def side_masks(position, shape):
    left = jnp.full(shape, position[1] > 0).astype(jnp.float32)
    right = jnp.full(shape, position[1] < position[2] - 1).astype(jnp.float32)
    return left, right


def smooth_columns(local_rows, block, cells, g, u1, u2, s, weights, masks):
    first = -DEEP
    low, high = cells
    c_ref, ahead_ref, behind_ref, _ = weights
    g_at, u1_at, u2_at = (g, first, low), (u1, first, low), (u2, first + 1, low + 1)
    total = g.shape[0]
    u1[total] = jnp.zeros(u1.shape[1:], jnp.float32)
    u2[total - 1] = jnp.zeros(u2.shape[1:], jnp.float32)
    first_sweep((first, local_rows), cells, block, g_at, u1_at, weights, masks)
    sweep(
        (first + 1, local_rows), (low + 1, high - 1), block, u1_at, None, u2_at, weights, masks
    )
    start = max(low + 2, 0)
    start += start % 2

    def paired(values):
        pairs = values.reshape(values.shape[0] // 2, 2, *values.shape[1:])
        return pairs[:, 0], pairs[:, 1]

    def pair_sums(values):
        even, odd = paired(values)
        return even + odd

    def restrict_row(index, carry):
        row = 2 * index + (DEEP - 2 * FAR)
        center = behind_ref[row + 1] - OMEGA / c_ref[row] + 1.0
        center_ahead = ahead_ref[row] - OMEGA / c_ref[row + 1] + 1.0
        behind, ahead = behind_ref[row], ahead_ref[row + 1]
        for at, count, _ in cell_tiles(start, start + 2 * s.shape[1], block):
            z = at - u2_at[2]
            here = u2[row - 1, z - 1 : z + count + 1]
            there = u2[row, z - 1 : z + count + 1]
            even, odd = paired(here + there)
            cells = slice(at - low, at - low + count)
            column = (at - start) // 2
            s[index, column : column + count // 2] = (
                pair_sums(g[row, cells] + g[row + 1, cells])
                + (even[:-1] + odd[1:])
                + behind * pair_sums(u2[row - 2, z : z + count])
                + center * pair_sums(here[1:-1])
                + center_ahead * pair_sums(there[1:-1])
                + ahead * pair_sums(u2[row + 1, z : z + count])
            )
        return carry

    lax.fori_loop(0, s.shape[0], restrict_row, 0)


def inner_kernel(
    local_rows, block, deep_ref, near_ref, far_ref, u_ref, s_ref,
    g, u1, u2, s, c_ref, ahead_ref, behind_ref, in_sems, out_sems,
):
    pairs, start = [], 0
    for ref in (deep_ref, near_ref, far_ref):
        pairs.append((ref, g.at[start : start + ref.shape[0]]))
        start += ref.shape[0]
    loads = started(pairs, in_sems)
    position, squares = place(), mode_squares(c_ref.shape[1:])
    upper = position[0] == 1
    row_weights(upper, local_rows, -DEEP, DEEP + local_rows, squares, c_ref, ahead_ref, behind_ref)
    weights = (c_ref, ahead_ref, behind_ref, -DEEP)
    finished(loads)
    smooth_columns(local_rows, block, (0, block), g, u1, u2, s, weights, None)
    pairs = [(u2.at[DEEP - 3 : DEEP - 1 + local_rows], u_ref), (s, s_ref)]
    finished(started(pairs, out_sems))


def outer_kernel(
    local_rows, block,
    deep_ref, near_ref, far_ref, left_ref, right_ref, inner_ref,
    u_left_ref, u_right_ref, head_ref, tail_ref,
    g_left, g_right, u1, u2_left, u2_right, s_left, s_right, head, tail,
    c_ref, ahead_ref, behind_ref, in_sems, out_sems,
):
    wide = g_left.shape[1]
    own = wide - NEAR
    pairs, start = [], 0
    for ref in (deep_ref, near_ref, far_ref):
        span = slice(start, start + ref.shape[0])
        pairs.append((ref.at[:, :own], g_left.at[span, NEAR:]))
        pairs.append((ref.at[:, block - own :], g_right.at[span, :own]))
        start = span.stop
    pairs += [(left_ref, g_left.at[:, :NEAR]), (right_ref, g_right.at[:, own:])]
    inner = inner_ref.shape[1]
    pairs += [(inner_ref.at[:, : FAR - 1], head.at[:, 1:])]
    pairs += [(inner_ref.at[:, inner - FAR + 1 :], tail.at[:, : FAR - 1])]
    loads = started(pairs, in_sems)
    position, squares = place(), mode_squares(c_ref.shape[1:])
    upper = position[0] == 1
    row_weights(upper, local_rows, -DEEP, DEEP + local_rows, squares, c_ref, ahead_ref, behind_ref)
    masks = side_masks(position, squares.shape)
    weights = (c_ref, ahead_ref, behind_ref, -DEEP)
    finished(loads)
    rows = slice(DEEP - 3, DEEP - 1 + local_rows)
    smooth_columns(local_rows, block, (-NEAR, own), g_left, u1, u2_left, s_left, weights, masks)
    head[:, 0] = s_left[:, 0]
    pairs = [(u2_left.at[rows, :NEAR], u_left_ref), (head, head_ref)]
    stores = started(pairs, out_sems)
    smooth_columns(
        local_rows, block, (block - own, block + NEAR), g_right, u1, u2_right, s_right, weights, masks
    )
    tail[:, FAR - 1] = s_right[:, 0]
    pairs = [(u2_right.at[rows, wide - 2 - NEAR :], u_right_ref), (tail, tail_ref)]
    finished(stores + started(pairs, out_sems, 2))


def finish_kernel(local_rows, block, tile_groups, *refs):
    (
        high_ref, low_ref, o_ref,
        s, e0, e1, u, v, g, w, o, t_high, t_low,
        c_ref, ahead_ref, behind_ref, cc_ref, cahead_ref, cbehind_ref, in_sems, out_sems,
    ) = refs[-21:]
    s_inner, s_head, s_tail, s_left, s_right, u_inner, u_left, u_right = refs[:8]
    g_refs = refs[8:13]
    position, squares = place(), mode_squares(c_ref.shape[1:])
    upper = position[0] == 1
    half_rows, half = local_rows // 2, block // 2
    pairs = [
        (s_inner, s.at[:, FAR + 1 : FAR + half - 1]),
        (s_head.at[:, 0:1], s.at[:, FAR : FAR + 1]),
        (s_tail.at[:, FAR - 1 : FAR], s.at[:, FAR + half - 1 : FAR + half]),
        (s_left, s.at[:, 0:FAR]),
        (s_right, s.at[:, FAR + half : FAR + half + FAR]),
    ]
    s_loads = started(pairs, in_sems)
    u_rows = slice(0, local_rows + 2)
    pairs, start = [
        (u_left, u.at[u_rows, :NEAR]),
        (u_inner, u.at[u_rows, NEAR : NEAR + block - 2]),
        (u_right, u.at[u_rows, NEAR + block - 2 :]),
    ], 0
    middle = slice(1, 1 + block)
    for ref in g_refs[:3]:
        rows = slice(DEEP - 1, DEEP) if start == 0 else slice(0, ref.shape[0])
        count = rows.stop - rows.start
        pairs.append((ref.at[rows], g.at[start : start + count, middle]))
        start += count
    rows = slice(DEEP - 1, DEEP + local_rows)
    pairs.append((g_refs[3].at[rows, NEAR - 1 : NEAR], g.at[:, 0:1]))
    pairs.append((g_refs[4].at[rows, 0:1], g.at[:, 1 + block : 2 + block]))
    pairs += [(high_ref, t_high), (low_ref, t_low)]
    loads = started(pairs, in_sems, len(s_loads))
    masks = side_masks(position, squares.shape)
    row_weights(upper, half_rows, -FAR, FAR + half_rows, squares, cc_ref, cahead_ref, cbehind_ref)
    row_weights(upper, local_rows, -1, 1 + local_rows, squares, c_ref, ahead_ref, behind_ref)
    coarse = (cc_ref, cahead_ref, cbehind_ref, -FAR)
    fine = (c_ref, ahead_ref, behind_ref, -1)
    for buffer in (e0, e1):
        buffer[FAR + half_rows] = jnp.zeros(buffer.shape[1:], jnp.float32)
    u[2 + local_rows] = jnp.zeros(u.shape[1:], jnp.float32)
    v[1 + local_rows] = jnp.zeros(v.shape[1:], jnp.float32)
    finished(s_loads)
    s_at = (s, -FAR, -FAR)
    here, there = (e0, -FAR, -FAR), (e1, -FAR, -FAR)
    first_sweep((-FAR, half_rows), (-FAR, half + FAR), half, s_at, here, coarse, masks)
    for step in range(1, COARSE):
        sweep(
            (step - FAR, half_rows), (step - FAR, half + FAR - step), half, here, s_at if step > 1 else None, there, coarse, masks
        )
        here, there = there, here
    e = here[0]
    finished(loads)

    def add_correction(index, carry):
        for first, count in ((-1, (half + 2) // 2), (-1 + (half + 2) // 2, half + 2 - (half + 2) // 2)):
            part = e[index + FAR - 1, first + FAR : first + FAR + count]
            twice = jnp.broadcast_to(part[:, None], (count, 2) + part.shape[1:])
            twice = twice.reshape(2 * count, *part.shape[1:])
            cells = slice(2 * first + 2, 2 * first + 2 + 2 * count)
            for offset in range(2):
                u[2 * index + offset, cells] = u[2 * index + offset, cells] + twice
        return carry

    lax.fori_loop(0, half_rows + 1, add_correction, 0)
    u_at, v_at, g_at = (u, -2, -2), (v, -1, -1), (g, -1, -1)
    sweep((-1, local_rows), (-1, block + 1), block, u_at, g_at, v_at, fine, masks)
    group_rows = TILE // tile_groups
    turn = (position[1] & (group_rows - 1), group_rows)
    sweep((0, local_rows), (0, block), block, v_at, g_at, (w, 0, 0), fine, masks, turn)
    stores = []
    for n in range(local_rows // TILE):
        span = slice(n * tile_groups, (n + 1) * tile_groups)
        synthesis_tile(w.at[n * TILE : (n + 1) * TILE], t_high, t_low, o.at[:, span])
        stores += started([(o.at[:, span], o_ref.at[:, span])], out_sems, n)
    finished(stores)


def params(mebibytes, *order):
    return pltpu.CompilerParams(
        dimension_semantics=order or None, vmem_limit_bytes=mebibytes * 1024 * 1024
    )


def cell_body(density):
    local_phi, local_rows, vertical_cells = density.shape
    az_count = lax.axis_size("az")
    azimuths = local_phi * az_count
    block = vertical_cells // az_count
    rows = LANES // block
    tiles = local_rows // TILE
    groups = TILE // rows
    chunks = 2
    chunk_tiles = tiles // chunks
    chunk_rows = local_rows // chunks
    analysis, synthesis = mode_tables(azimuths)
    point = (azimuths // LANES, LANES)
    f32 = jnp.float32
    a_high, a_low = high_low(analysis)
    s_high, s_low = high_low(synthesis)
    order = block_order(az_count)
    product = 2 * 3 * azimuths * azimuths // 2
    lane_tiles = vertical_cells // LANES
    anywhere = pl.BlockSpec(memory_space=pl.ANY)
    in_hbm = pl.BlockSpec(memory_space=pltpu.HBM)

    def field(row_count, cell_count):
        return jax.ShapeDtypeStruct((row_count, cell_count) + point, f32)

    def scratch(row_count, *cell_count):
        return pltpu.VMEM((row_count,) + cell_count + point, f32)

    def semaphores(count):
        return pltpu.SemaphoreType.DMA((count,))

    def cost(mebibytes):
        return pl.CostEstimate(flops=0, bytes_accessed=mebibytes * 1024 * 1024, transcendentals=0)

    def pack(first_tile):
        return pl.pallas_call(
            lambda *refs: pack_kernel(block, order, first_tile, *refs),
            in_specs=[in_hbm],
            out_specs=in_hbm,
            out_shape=jax.ShapeDtypeStruct(
                (az_count, chunk_tiles * groups, local_phi, LANES), f32
            ),
            scratch_shapes=[
                pltpu.VMEM((chunk_tiles, lane_tiles, local_phi, TILE, LANES), f32),
                pltpu.VMEM((az_count, chunk_tiles * groups, local_phi, LANES), f32),
                pltpu.SemaphoreType.DMA((chunk_tiles * lane_tiles,)),
                pltpu.SemaphoreType.DMA((chunk_tiles,)),
            ],
            compiler_params=params(56),
            name="pack",
        )(density)

    half_rows, half = local_rows // 2, block // 2
    all_rows, coarse_rows = DEEP + local_rows, FAR + half_rows
    tables = [pltpu.VMEM((azimuths // 2, azimuths), jnp.bfloat16)] * 2

    def analyse(received, held):
        out_shape = [field(chunk_rows, block)]
        out_shape += [field(all_rows, NEAR)] * 2 if held else [field(DEEP, 2 * NEAR), field(DEEP, block)]
        return pl.pallas_call(
            lambda *refs: analysis_kernel(groups, len(held), *refs),
            in_specs=[in_hbm] * 3 + [anywhere] * len(held),
            out_specs=[anywhere] * len(out_shape),
            out_shape=out_shape,
            scratch_shapes=[
                pltpu.VMEM((az_count, chunk_tiles * groups, local_phi, LANES), f32),
                *tables,
                scratch(chunk_rows, block),
                scratch(all_rows, 2 * NEAR) if held else scratch(DEEP, block),
                semaphores(chunk_tiles),
                semaphores(2),
                semaphores(chunk_rows + 6),
            ],
            compiler_params=params(56),
            cost_estimate=cost(12),
            name="analysis",
        )(received, a_high, a_low, *held)

    def exchange(value):
        return lax.all_to_all(value, "az", split_axis=0, concat_axis=0, tiled=True)

    to_right = [(order[i], order[i + 1]) for i in range(az_count - 1)]
    to_left = [(b, a) for a, b in to_right]

    def from_sides(head, tail):
        return lax.ppermute(tail, "az", to_right), lax.ppermute(head, "az", to_left)

    first_received = exchange(pack(0))
    second_received = exchange(pack(chunk_tiles))
    near, edge_sides, edge = analyse(first_received, ())
    deep_sides = lax.ppermute(edge_sides, "rad", [(0, 1), (1, 0)])
    deep_sides, edge = lax.optimization_barrier((deep_sides, edge))
    deep = lax.ppermute(edge, "rad", [(0, 1), (1, 0)])
    far, head, tail = analyse(second_received, (deep_sides, near))
    fields = (deep, near, far, *from_sides(head, tail))

    wide = 2 * NEAR + 1
    weight_scratch = [scratch(all_rows)] * 3
    u_inner, s_inner = pl.pallas_call(
        lambda *refs: inner_kernel(local_rows, block, *refs),
        in_specs=[anywhere] * 3,
        out_specs=[anywhere] * 2,
        out_shape=[field(local_rows + 2, block - 2), field(coarse_rows, half - 2)],
        scratch_shapes=[
            scratch(all_rows, block),
            scratch(all_rows + 1, block),
            scratch(all_rows, block - 2),
            scratch(coarse_rows, half - 2),
            *weight_scratch,
            semaphores(3),
            semaphores(2),
        ],
        compiler_params=params(28),
        cost_estimate=cost(32),
        name="inner",
    )(*fields[:3])
    u_left, u_right, s_head, s_tail = pl.pallas_call(
        lambda *refs: outer_kernel(local_rows, block, *refs),
        in_specs=[anywhere] * 6,
        out_specs=[anywhere] * 4,
        out_shape=[field(local_rows + 2, NEAR)] * 2 + [field(coarse_rows, FAR)] * 2,
        scratch_shapes=[
            scratch(all_rows, wide),
            scratch(all_rows, wide),
            scratch(all_rows + 1, wide),
            scratch(all_rows, wide - 2),
            scratch(all_rows, wide - 2),
            scratch(coarse_rows, 1),
            scratch(coarse_rows, 1),
            scratch(coarse_rows, FAR),
            scratch(coarse_rows, FAR),
            *weight_scratch,
            semaphores(10),
            semaphores(4),
        ],
        compiler_params=params(20),
        cost_estimate=cost(12),
        name="outer",
    )(*fields, s_inner)
    s_parts = (s_inner, s_head, s_tail, *from_sides(s_head, s_tail))

    received_shape = (az_count, tiles * groups, local_phi, LANES)
    physical = pl.pallas_call(
        lambda *refs: finish_kernel(local_rows, block, groups, *refs),
        in_specs=[anywhere] * 13 + [in_hbm] * 2,
        out_specs=in_hbm,
        out_shape=jax.ShapeDtypeStruct(received_shape, f32),
        scratch_shapes=[
            scratch(coarse_rows, half + 2 * FAR),
            scratch(coarse_rows + 1, half + 2 * FAR),
            scratch(coarse_rows + 1, half + 2 * FAR),
            scratch(local_rows + 3, block + 4),
            scratch(local_rows + 2, block + 2),
            scratch(local_rows + 1, block + 2),
            scratch(local_rows, block),
            pltpu.VMEM(received_shape, f32),
            *tables,
            scratch(local_rows + 1),
            scratch(local_rows + 1),
            scratch(local_rows + 1),
            scratch(coarse_rows),
            scratch(coarse_rows),
            scratch(coarse_rows),
            semaphores(15),
            semaphores(tiles),
        ],
        compiler_params=params(46),
        name="finish",
    )(*s_parts, u_inner, u_left, u_right, *fields, s_high, s_low)

    returned = exchange(physical)
    side = jnp.stack([lax.axis_index("rad"), lax.axis_index("az")]).astype(jnp.int32)
    return pl.pallas_call(
        lambda *refs: unpack_kernel(block, order, *refs),
        in_specs=[in_hbm, anywhere],
        out_specs=in_hbm,
        out_shape=jax.ShapeDtypeStruct(density.shape, f32),
        scratch_shapes=[
            pltpu.VMEM((az_count, tiles * groups, local_phi, LANES), f32),
            pltpu.VMEM((tiles, lane_tiles, local_phi, TILE, LANES), f32),
            pltpu.SemaphoreType.DMA((tiles,)),
            pltpu.SemaphoreType.DMA((tiles * lane_tiles,)),
        ],
        compiler_params=params(56),
        name="unpack",
    )(returned, side)


def block_order(az_count):
    return [i ^ 2 if (i // 4) % 2 else i for i in range(az_count)]


def fits_cells(density):
    local_phi, local_rows, vertical_cells = density.shape
    az_count, rad_count = lax.axis_size("az"), lax.axis_size("rad")
    block = vertical_cells // az_count
    return (
        rad_count == 2
        and vertical_cells % (az_count * 2) == 0
        and vertical_cells % LANES == 0
        and LANES // TILE <= block <= LANES
        and LANES % block == 0
        and block // 2 >= FAR
        and local_rows % (4 * TILE) == 0
        and local_rows // 2 >= DEEP
        and az_count % 4 == 0
        and local_phi % TILE == 0
        and (az_count * local_phi) % (2 * LANES) == 0
        and az_count * local_phi == TILE * LANES
    )


def body(density):
    return cell_body(density) if fits_cells(density) else general_body(density)


def solution(mesh):
    placed = (P("az", "rad", None),)
    return jax.shard_map(
        body, mesh=mesh, in_specs=placed, out_specs=P("az", "rad", None), check_vma=False
    )
```

```python
import math

import jax
import jax.numpy as jnp
import numpy as np
from jax import lax
from jax.experimental import pallas as pl
from jax.experimental.pallas import tpu as pltpu
from jax.sharding import PartitionSpec as P

PRE = 2
POST = 2
COARSE = 6


OMEGA = 0.8

LANES = 128
TILE = 8
DEEP = 2 * COARSE + 2
NEAR = 3
FAR = COARSE


def with_halo(cells, sides, width):
    for axis, dim in sides:
        count = lax.axis_size(axis)
        ends = count - 1
        head = lax.slice_in_dim(cells, 0, width, axis=dim)
        tail = lax.slice_in_dim(cells, cells.shape[dim] - width, cells.shape[dim], axis=dim)
        cells = jnp.concatenate(
            [
                lax.ppermute(tail, axis, [(i, (i + 1) % count) for i in range(ends)]),
                cells,
                lax.ppermute(head, axis, [((i + 1) % count, i) for i in range(ends)]),
            ],
            axis=dim,
        )
    return cells


def level_coefficients(first_row, row_count, spacing, mode_numbers):
    row_number = (jnp.arange(row_count, dtype=jnp.int32) + first_row).astype(jnp.float32)
    radius = spacing * (row_number + 0.5)
    outward = (row_number + 1.0) / (spacing * radius)
    inward = row_number / (spacing * radius)
    vertical = 1.0 / (spacing * spacing)
    diagonal = (outward + inward + 2.0 * vertical)[None, :] + (
        mode_numbers[:, None] / radius[None, :]
    ) ** 2
    return (diagonal[:, :, None], outward[None, :, None], inward[None, :, None], vertical)


def apply_op(iterate, padded, coefficients):
    diagonal, outward, inward, vertical = coefficients
    return (
        diagonal * iterate
        - outward * padded[:, 2:, 1:-1]
        - inward * padded[:, :-2, 1:-1]
        - vertical * (padded[:, 1:-1, 2:] + padded[:, 1:-1, :-2])
    )


def relax(iterate, source, coefficients, pad_both):
    return (
        iterate
        + OMEGA * (source - apply_op(iterate, pad_both(iterate), coefficients)) / coefficients[0]
    )


def restrict(residual):
    k_count, r_count, z_count = residual.shape
    parts = residual.reshape(k_count, r_count // 2, 2, z_count // 2, 2)
    return 0.25 * (
        parts[:, :, 0, :, 0] + parts[:, :, 1, :, 0] + parts[:, :, 0, :, 1] + parts[:, :, 1, :, 1]
    )


def prolong(correction):
    return jnp.repeat(jnp.repeat(correction, 2, axis=1), 2, axis=2)


def pad_level(field):
    rows = with_halo(field, (("rad", 1),), 1)
    return jnp.pad(rows, ((0, 0), (0, 0), (1, 1)))


def mode_values(mode_index, azimuths):
    return jnp.where(mode_index <= azimuths // 2, mode_index, mode_index - azimuths // 2).astype(
        jnp.float32
    )


def fine_cycle(source, fine_coef, pad_sweep, coarse_solve):
    iterate = OMEGA * source / fine_coef[0]
    for sweep_index in range(PRE - 1):
        iterate = relax(iterate, source, fine_coef, pad_sweep)
    residual = source - apply_op(iterate, pad_sweep(iterate), fine_coef)
    iterate = iterate + prolong(coarse_solve(restrict(residual)))
    for sweep_index in range(POST):
        iterate = relax(iterate, source, fine_coef, pad_sweep)
    return iterate


def general_body(density):
    local_phi, local_rows, vertical_cells = density.shape
    az_count = lax.axis_size("az")
    azimuths = local_phi * az_count
    cell_count = local_rows * vertical_cells // az_count
    numbers = jnp.arange(azimuths, dtype=jnp.int32)
    all_modes = jnp.where(numbers <= azimuths // 2, numbers, numbers - azimuths // 2)
    phase = all_modes[:, None] * numbers[None, :] % azimuths
    phase_angle = phase.astype(jnp.float32) * (2.0 * math.pi / azimuths)
    analysis_table = jnp.where(
        (numbers <= azimuths // 2)[:, None], jnp.cos(phase_angle), jnp.sin(phase_angle)
    )
    synth_weight = jnp.where(
        (numbers == 0) | (numbers == azimuths // 2), 1.0 / azimuths, 2.0 / azimuths
    )
    synthesis_table = analysis_table.T * synth_weight[None, :]

    def transform_with(table, columns):
        width = columns.shape[2]
        matrix = columns.reshape(azimuths, width)
        result = jnp.dot(
            table, matrix, precision=lax.Precision.HIGHEST, preferred_element_type=jnp.float32
        )
        return result.reshape(azimuths, 1, width)

    lines = density.reshape(local_phi, az_count, cell_count)
    spectral = transform_with(
        analysis_table, lax.all_to_all(lines, "az", split_axis=1, concat_axis=0, tiled=True)
    )
    coefficients = lax.all_to_all(spectral, "az", split_axis=0, concat_axis=1, tiled=True)
    source = -coefficients.reshape(local_phi, local_rows, vertical_cells)
    rad_index = lax.axis_index("rad")
    half_rows = local_rows // 2
    mode_index = lax.axis_index("az") * local_phi + jnp.arange(local_phi, dtype=jnp.int32)
    mode_numbers = mode_values(mode_index, azimuths)
    fine_coef = level_coefficients(rad_index * local_rows, local_rows, 1.0, mode_numbers)
    coarse_coef = level_coefficients(rad_index * half_rows, half_rows, 2.0, mode_numbers)

    def coarse_halo(coarse_source):
        correction = OMEGA * coarse_source / coarse_coef[0]
        for sweep_index in range(COARSE - 1):
            correction = relax(correction, coarse_source, coarse_coef, pad_level)
        return correction

    iterate = fine_cycle(source, fine_coef, pad_level, coarse_halo)
    mode_lines = iterate.reshape(local_phi, az_count, cell_count)
    physical = transform_with(
        synthesis_table, lax.all_to_all(mode_lines, "az", split_axis=1, concat_axis=0, tiled=True)
    )
    field = lax.all_to_all(physical, "az", split_axis=0, concat_axis=1, tiled=True)
    return field.reshape(local_phi, local_rows, vertical_cells)


def mode_tables(azimuths):
    half, quarter = azimuths // 2, azimuths // 4
    fours = np.concatenate([np.arange(0, half + 1, 4), np.arange(4, half, 4)])
    twos = np.concatenate([np.arange(2, half, 4)] * 2)
    odd = np.concatenate([np.arange(1, half, 2)] * 2)
    modes = np.concatenate([fours, twos, odd])
    index = np.arange(quarter)
    is_cos = np.concatenate(
        [index <= quarter // 2, index < quarter // 2, np.arange(half) < quarter]
    )
    angle = 2.0 * np.pi / azimuths * (np.arange(half)[:, None] * modes[None, :] % azimuths)
    values = np.where(is_cos[None, :], np.cos(angle), np.sin(angle))
    weighted = values * (np.where((modes == 0) | (modes == half), 1.0, 2.0) / azimuths)[None, :]
    return -values, weighted


def table_parts(table, azimuths):
    quarter = azimuths // 4
    return [
        (table.at[0:quarter, 0:quarter], 0),
        (table.at[0:quarter, quarter : 2 * quarter], quarter),
        (table.at[:, 2 * quarter :], 2 * quarter),
    ]


def high_low(values):
    values = values.astype(np.float32)
    high = values.astype(jnp.bfloat16)
    low = (values - high.astype(np.float32)).astype(jnp.bfloat16)
    return jnp.asarray(high), jnp.asarray(low)


def split_value(value):
    high = value.astype(jnp.bfloat16)
    return high, (value - high.astype(jnp.float32)).astype(jnp.bfloat16)


def place():
    az = lax.axis_index("az")
    return lax.axis_index("rad"), az ^ (((az >> 2) & 1) << 1), lax.axis_size("az")


def mode_squares(shape):
    half = shape[0] * shape[1] // 2
    quarter, eighth = half // 2, half // 4
    index = lax.broadcasted_iota(jnp.int32, shape, 0) * shape[1] + lax.broadcasted_iota(jnp.int32, shape, 1)
    fours = 4 * jnp.where(index <= eighth, index, index - eighth)
    twos = 4 * (index & (eighth - 1)) + 2
    odd = 2 * (index & (quarter - 1)) + 1
    modes = jnp.where(index < quarter, fours, jnp.where(index < half, twos, odd))
    return (modes * modes).astype(jnp.float32)


def row_tile(position, local_rows, tile):
    return jnp.where(position[0] == 0, local_rows // TILE - 1 - tile, tile)


def chunk_masks(count, shape):
    lane = lax.broadcasted_iota(jnp.int32, shape, len(shape) - 1) // (LANES // count)
    return [lane == p for p in range(1, count)]


def pick_chunks(parts, masks):
    result = parts[0]
    for part, mask in zip(parts[1:], masks):
        result = jnp.where(mask, part, result)
    return result


def gather_rows(parts, masks):
    count = len(parts)
    chunk = LANES // count
    turned = [pltpu.roll(part, i * chunk, 1) if i else part for i, part in enumerate(parts)]
    return [pick_chunks([turned[(p - q) % count] for p in range(count)], masks) for q in range(count)]


def scatter_rows(parts, masks):
    count = len(parts)
    chunk = LANES // count
    rows = [pick_chunks([parts[(p - i) % count] for p in range(count)], masks) for i in range(count)]
    return [pltpu.roll(row, LANES - i * chunk, 1) if i else row for i, row in enumerate(rows)]


def turned_row(row, turn, rows):
    low = row & (rows - 1)
    return row - low + ((low + turn) & (rows - 1))


def tile_row(position, row):
    return jnp.where(position[0] == 0, TILE - 1 - row, row)


def pack_kernel(block, order, first_tile, x_ref, o_ref, x, o, in_sems, out_sems):
    position = place()
    rows = LANES // block
    local_phi, local_rows, cells = x_ref.shape
    tiles, lane_tiles, groups = x.shape[0], x.shape[1], TILE // rows
    pieces = [(j, k) for j in range(tiles) for k in range(lane_tiles)]
    masks = chunk_masks(rows, (local_phi, LANES))
    loads, stores = [], []
    for n, (j, k) in enumerate(pieces):
        start = pl.multiple_of(row_tile(position, local_rows, first_tile + j) * TILE, TILE)
        source = x_ref.at[:, pl.ds(start, TILE), k * LANES : (k + 1) * LANES]
        loads.append(pltpu.make_async_copy(source, x.at[j, k], in_sems.at[n]))
        loads[-1].start()
    for n, (j, k) in enumerate(pieces):
        loads[n].wait()
        flat = x.at[j, k].reshape(local_phi * TILE, LANES)
        for group in range(groups):
            parts = [
                flat[pl.ds(tile_row(position, group * rows + i), local_phi, stride=TILE), :]
                for i in range(rows)
            ]
            for q, part in enumerate(gather_rows(parts, masks)):
                o[order[k * rows + q], j * groups + group] = part
        if k == lane_tiles - 1:
            span = slice(j * groups, (j + 1) * groups)
            stores.append(pltpu.make_async_copy(o.at[:, span], o_ref.at[:, span], out_sems.at[j]))
            stores[-1].start()
    for store in stores:
        store.wait()


def unpack_kernel(block, order, x_ref, _, o_ref, x, o, in_sems, out_sems):
    position = place()
    rows = LANES // block
    local_phi, local_rows, cells = o_ref.shape
    tiles, lane_tiles, groups = o.shape[0], o.shape[1], TILE // rows
    masks = chunk_masks(rows, (local_phi, LANES))
    loads, stores = [], []
    for j in range(tiles):
        span = slice(j * groups, (j + 1) * groups)
        loads.append(pltpu.make_async_copy(x_ref.at[:, span], x.at[:, span], in_sems.at[j]))
        loads[-1].start()
    for j in range(tiles):
        loads[j].wait()
        start = pl.multiple_of(row_tile(position, local_rows, j) * TILE, TILE)
        for k in range(lane_tiles):
            flat = o.at[j, k].reshape(local_phi * TILE, LANES)
            for group in range(groups):
                parts = [x[order[k * rows + q], j * groups + group] for q in range(rows)]
                for i, part in enumerate(scatter_rows(parts, masks)):
                    at = tile_row(position, group * rows + i)
                    flat[pl.ds(at, local_phi, stride=TILE), :] = part
            target = o_ref.at[:, pl.ds(start, TILE), k * LANES : (k + 1) * LANES]
            stores.append(
                pltpu.make_async_copy(o.at[j, k], target, out_sems.at[j * lane_tiles + k])
            )
            stores[-1].start()
    for store in stores:
        store.wait()


def started(pairs, sems, first=0):
    copies = []
    for n, (src, dst) in enumerate(pairs):
        copies.append(pltpu.make_async_copy(src, dst, sems.at[first + n]))
        copies[-1].start()
    return copies


def finished(copies):
    for copy in copies:
        copy.wait()


def sides_of(field, depth):
    cells = field.shape[1]
    return field, field.at[:, :depth], field.at[:, cells - depth : cells]


def analysis_kernel(tile_groups, held_count, *refs):
    position = place()
    x_ref, high_ref, low_ref = refs[:3]
    outs = refs[3:-8]
    x, t_high, t_low, o, edge, in_sems, t_sems, out_sems = refs[-8:]
    held_refs, outs = outs[:held_count], outs[held_count:]
    sources, width, lanes = x.shape[0], x.shape[2], x.shape[3]
    cells = o.shape[1]
    half = sources // 2 * width
    tiles = x.shape[1] // tile_groups
    spans = [slice(n * tile_groups, (n + 1) * tile_groups) for n in range(tiles)]
    pairs = [(x_ref.at[:, span], x.at[:, span]) for span in spans]
    tables = started([(high_ref, t_high), (low_ref, t_low)], t_sems)
    loads = started(pairs, in_sems)
    group_rows = TILE // tile_groups
    turn = position[1] & (group_rows - 1)
    gathers, start = [], 0
    for held in held_refs:
        span = slice(start, start + held.shape[0])
        if held.shape[1] == 2 * NEAR:
            pairs = [(held, edge.at[span])]
        else:
            sides = zip(sides_of(held, NEAR)[1:], (slice(0, NEAR), slice(NEAR, 2 * NEAR)))
            pairs = [(side, edge.at[span, columns]) for side, columns in sides]
        gathers += started(pairs, out_sems, out_sems.shape[0] - 4 + len(gathers))
        start += held.shape[0]
    stores = []
    for n in range(tiles):
        loads[n].wait()
        turned = [[], [], []]
        for group in range(n * tile_groups, (n + 1) * tile_groups):
            near = x[: sources // 2, group].reshape(half, lanes)
            far = x[sources // 2 :, group].reshape(half, lanes)
            even = near + far
            low_half, high_half = even[: half // 2], even[half // 2 :]
            for part, folded in zip(turned, (low_half + high_half, low_half - high_half, near - far)):
                part.append(folded.T)
        parts = [split_value(jnp.concatenate(part, axis=0)) for part in turned]
        if n == 0:
            finished(tables)
        rows = slice(n * TILE, (n + 1) * TILE)
        columns = zip(parts, table_parts(t_high, 2 * half), table_parts(t_low, 2 * half))
        for (high, low), (part_high, first), (part_low, _) in columns:
            result = (
                jnp.dot(high, part_high[...], preferred_element_type=jnp.float32)
                + jnp.dot(high, part_low[...], preferred_element_type=jnp.float32)
                + jnp.dot(low, part_high[...], preferred_element_type=jnp.float32)
            )
            for part in range(result.shape[1] // LANES):
                piece = result[:, part * LANES : (part + 1) * LANES]
                o[rows, :, first // LANES + part, :] = piece.reshape(TILE, cells, LANES)
        pairs = [
            (o.at[turned_row(row, turn, group_rows)], outs[0].at[row])
            for row in range(n * TILE, (n + 1) * TILE)
        ]
        stores += started(pairs, out_sems, len(stores))
    if held_refs:
        finished(gathers)
        for row in range(o.shape[0]):
            at = turned_row(row, turn, group_rows)
            edge[start + row, :NEAR] = o[at, :NEAR]
            edge[start + row, NEAR:] = o[at, cells - NEAR :]
        pairs = [(edge.at[:, :NEAR], outs[1]), (edge.at[:, NEAR:], outs[2])]
        stores += started(pairs, out_sems, len(stores))
    else:
        for row in range(DEEP):
            edge[DEEP - 1 - row] = o[turned_row(row, turn, group_rows)]
        _, head, tail = sides_of(edge, NEAR)
        pairs = [(head, outs[1].at[:, :NEAR]), (tail, outs[1].at[:, NEAR:]), (edge, outs[2])]
        stores += started(pairs, out_sems, len(stores))
    finished(stores)


def synthesis_tile(u, t_high, t_low, o):
    rows, cells = u.shape[0], u.shape[1]
    half = t_high.shape[0]
    contract = (((1,), (1,)), ((), ()))
    sums = []
    for (part_high, first), (part_low, _) in zip(table_parts(t_high, 2 * half), table_parts(t_low, 2 * half)):
        parts = range(first // LANES, (first + part_high.shape[1]) // LANES)
        field = jnp.concatenate([u[:, :, i, :].reshape(rows * cells, LANES) for i in parts], axis=1)
        high, low = split_value(field)
        sums.append(
            lax.dot_general(part_high[...], high, contract, preferred_element_type=jnp.float32)
            + lax.dot_general(part_high[...], low, contract, preferred_element_type=jnp.float32)
            + lax.dot_general(part_low[...], high, contract, preferred_element_type=jnp.float32)
        )
    fours, twos, odd = sums
    even = jnp.concatenate([fours + twos, fours - twos], axis=0)
    near, far = even + odd, even - odd
    targets, groups, width, lanes = o.shape
    for group in range(groups):
        columns = slice(group * lanes, (group + 1) * lanes)
        o[: targets // 2, group] = near[:, columns].reshape(targets // 2, width, lanes)
        o[targets // 2 :, group] = far[:, columns].reshape(targets // 2, width, lanes)


def row_weights(upper, boundary, first, count, squares, c_ref, ahead_ref, behind_ref):
    def one(index, carry):
        row = jnp.where(upper, index + (boundary + first), (boundary - 1 - first) - index)
        number = jnp.full(squares.shape, row, jnp.int32).astype(jnp.float32)
        radius = number + 0.5
        outward = (number + 1.0) / radius
        inward = number / radius
        diagonal = outward + inward + 2.0 + squares / (radius * radius)
        c_ref[index] = OMEGA / diagonal
        ahead_ref[index] = jnp.where(upper, outward, inward)
        behind_ref[index] = jnp.where(upper, inward, outward)
        return carry

    lax.fori_loop(0, count, one, 0)


def cell_tiles(first, last, cells, size=16):
    tiles = []
    if first < 0:
        tiles.append((first, -first, -1))
    for start in range(max(first, 0), min(last, cells), size):
        tiles.append((start, min(size, min(last, cells) - start), 0))
    if last > cells:
        tiles.append((cells, last - cells, 1))
    return tiles


def sweep(rows, cells, block, src, source, dst, weights, masks, turn=None):
    (src_ref, src_t, src_z), (dst_ref, dst_t, dst_z) = src, dst
    keep = 1.0 - OMEGA if source else 2.0 - OMEGA
    c_ref, ahead_ref, behind_ref, w_t = weights
    low = rows[0]

    def one(step, carry):
        at = step + (low - w_t)
        target = step + (low - dst_t)
        if turn:
            target = turned_row(target, *turn)
        c_row, ahead, behind = c_ref[at], ahead_ref[at], behind_ref[at]
        for first, count, side in cell_tiles(cells[0], cells[1], block):
            c = c_row if side == 0 else c_row * masks[0 if side < 0 else 1]
            z = first - src_z
            row = low - src_t
            middle = src_ref[step + row, z - 1 : z + count + 1]
            gathered = (
                ahead * src_ref[step + (row + 1), z : z + count]
                + behind * src_ref[step + (row - 1), z : z + count]
                + (middle[:-2] + middle[2:])
            )
            if source:
                g_ref, g_t, g_z = source
                gathered += g_ref[step + (low - g_t), first - g_z : first - g_z + count]
            dst_ref[target, first - dst_z : first - dst_z + count] = (
                keep * middle[1:-1] + c * gathered
            )
        return carry

    lax.fori_loop(0, rows[1] - low, one, 0)


def first_sweep(rows, cells, block, source, dst, weights, masks):
    (g_ref, g_t, g_z), (dst_ref, dst_t, dst_z) = source, dst
    c_ref, w_t = weights[0], weights[3]
    low = rows[0]

    def one(step, carry):
        c_row = c_ref[step + (low - w_t)]
        for first, count, side in cell_tiles(cells[0], cells[1], block):
            c = c_row if side == 0 else c_row * masks[0 if side < 0 else 1]
            dst_ref[step + (low - dst_t), first - dst_z : first - dst_z + count] = (
                c * g_ref[step + (low - g_t), first - g_z : first - g_z + count]
            )
        return carry

    lax.fori_loop(0, rows[1] - low, one, 0)


def side_masks(position, shape):
    left = jnp.full(shape, position[1] > 0).astype(jnp.float32)
    right = jnp.full(shape, position[1] < position[2] - 1).astype(jnp.float32)
    return left, right


def smooth_columns(local_rows, block, cells, g, u1, u2, s, weights, masks):
    first = -DEEP
    low, high = cells
    c_ref, ahead_ref, behind_ref, _ = weights
    g_at, u1_at, u2_at = (g, first, low), (u1, first, low), (u2, first + 1, low + 1)
    total = g.shape[0]
    u1[total] = jnp.zeros(u1.shape[1:], jnp.float32)
    u2[total - 1] = jnp.zeros(u2.shape[1:], jnp.float32)
    first_sweep((first, local_rows), cells, block, g_at, u1_at, weights, masks)
    sweep(
        (first + 1, local_rows), (low + 1, high - 1), block, u1_at, None, u2_at, weights, masks
    )
    start = max(low + 2, 0)
    start += start % 2

    def paired(values):
        pairs = values.reshape(values.shape[0] // 2, 2, *values.shape[1:])
        return pairs[:, 0], pairs[:, 1]

    def pair_sums(values):
        even, odd = paired(values)
        return even + odd

    def restrict_row(index, carry):
        row = 2 * index + (DEEP - 2 * FAR)
        center = behind_ref[row + 1] - OMEGA / c_ref[row] + 1.0
        center_ahead = ahead_ref[row] - OMEGA / c_ref[row + 1] + 1.0
        behind, ahead = behind_ref[row], ahead_ref[row + 1]
        for at, count, _ in cell_tiles(start, start + 2 * s.shape[1], block):
            z = at - u2_at[2]
            here = u2[row - 1, z - 1 : z + count + 1]
            there = u2[row, z - 1 : z + count + 1]
            even, odd = paired(here + there)
            cells = slice(at - low, at - low + count)
            column = (at - start) // 2
            s[index, column : column + count // 2] = (
                pair_sums(g[row, cells] + g[row + 1, cells])
                + (even[:-1] + odd[1:])
                + behind * pair_sums(u2[row - 2, z : z + count])
                + center * pair_sums(here[1:-1])
                + center_ahead * pair_sums(there[1:-1])
                + ahead * pair_sums(u2[row + 1, z : z + count])
            )
        return carry

    lax.fori_loop(0, s.shape[0], restrict_row, 0)


def inner_kernel(
    local_rows, block, deep_ref, near_ref, far_ref, u_ref, s_ref,
    g, u1, u2, s, c_ref, ahead_ref, behind_ref, in_sems, out_sems,
):
    pairs, start = [], 0
    for ref in (deep_ref, near_ref, far_ref):
        pairs.append((ref, g.at[start : start + ref.shape[0]]))
        start += ref.shape[0]
    loads = started(pairs, in_sems)
    position, squares = place(), mode_squares(c_ref.shape[1:])
    upper = position[0] == 1
    row_weights(upper, local_rows, -DEEP, DEEP + local_rows, squares, c_ref, ahead_ref, behind_ref)
    weights = (c_ref, ahead_ref, behind_ref, -DEEP)
    finished(loads)
    smooth_columns(local_rows, block, (0, block), g, u1, u2, s, weights, None)
    pairs = [(u2.at[DEEP - 3 : DEEP - 1 + local_rows], u_ref), (s, s_ref)]
    finished(started(pairs, out_sems))


def outer_kernel(
    local_rows, block,
    deep_ref, near_ref, far_ref, left_ref, right_ref, inner_ref,
    u_left_ref, u_right_ref, head_ref, tail_ref,
    g_left, g_right, u1, u2_left, u2_right, s_left, s_right, head, tail,
    c_ref, ahead_ref, behind_ref, in_sems, out_sems,
):
    wide = g_left.shape[1]
    own = wide - NEAR
    pairs, start = [], 0
    for ref in (deep_ref, near_ref, far_ref):
        span = slice(start, start + ref.shape[0])
        pairs.append((ref.at[:, :own], g_left.at[span, NEAR:]))
        pairs.append((ref.at[:, block - own :], g_right.at[span, :own]))
        start = span.stop
    pairs += [(left_ref, g_left.at[:, :NEAR]), (right_ref, g_right.at[:, own:])]
    inner = inner_ref.shape[1]
    pairs += [(inner_ref.at[:, : FAR - 1], head.at[:, 1:])]
    pairs += [(inner_ref.at[:, inner - FAR + 1 :], tail.at[:, : FAR - 1])]
    loads = started(pairs, in_sems)
    position, squares = place(), mode_squares(c_ref.shape[1:])
    upper = position[0] == 1
    row_weights(upper, local_rows, -DEEP, DEEP + local_rows, squares, c_ref, ahead_ref, behind_ref)
    masks = side_masks(position, squares.shape)
    weights = (c_ref, ahead_ref, behind_ref, -DEEP)
    finished(loads)
    rows = slice(DEEP - 3, DEEP - 1 + local_rows)
    smooth_columns(local_rows, block, (-NEAR, own), g_left, u1, u2_left, s_left, weights, masks)
    head[:, 0] = s_left[:, 0]
    pairs = [(u2_left.at[rows, :NEAR], u_left_ref), (head, head_ref)]
    stores = started(pairs, out_sems)
    smooth_columns(
        local_rows, block, (block - own, block + NEAR), g_right, u1, u2_right, s_right, weights, masks
    )
    tail[:, FAR - 1] = s_right[:, 0]
    pairs = [(u2_right.at[rows, wide - 2 - NEAR :], u_right_ref), (tail, tail_ref)]
    finished(stores + started(pairs, out_sems, 2))


def field_pairs(g_refs, g):
    pairs, start = [], 0
    local_rows, middle = g.shape[0] - 1, slice(1, g.shape[1] - 1)
    for ref in g_refs[:3]:
        rows = slice(DEEP - 1, DEEP) if start == 0 else slice(0, ref.shape[0])
        count = rows.stop - rows.start
        pairs.append((ref.at[rows], g.at[start : start + count, middle]))
        start += count
    rows = slice(DEEP - 1, DEEP + local_rows)
    pairs.append((g_refs[3].at[rows, NEAR - 1 : NEAR], g.at[:, 0:1]))
    pairs.append((g_refs[4].at[rows, 0:1], g.at[:, middle.stop : middle.stop + 1]))
    return pairs


def settle_kernel(
    local_rows, block, inner_ref, left_ref, right_ref, *refs
):
    g_refs = refs[:5]
    v_ref, u, g, v, c_ref, ahead_ref, behind_ref, in_sems, out_sems = refs[5:]
    rows = slice(0, local_rows + 2)
    pairs = [
        (left_ref, u.at[rows, :NEAR]),
        (inner_ref, u.at[rows, NEAR : NEAR + block - 2]),
        (right_ref, u.at[rows, NEAR + block - 2 :]),
    ]
    loads = started(pairs + field_pairs(g_refs, g), in_sems)
    position, squares = place(), mode_squares(c_ref.shape[1:])
    masks = side_masks(position, squares.shape)
    upper = position[0] == 1
    row_weights(upper, local_rows, -1, 1 + local_rows, squares, c_ref, ahead_ref, behind_ref)
    u[2 + local_rows] = jnp.zeros(u.shape[1:], jnp.float32)
    finished(loads)
    u_at, v_at, g_at = (u, -2, -2), (v, -1, -1), (g, -1, -1)
    weights = (c_ref, ahead_ref, behind_ref, -1)
    sweep((-1, local_rows), (-1, block + 1), block, u_at, g_at, v_at, weights, masks)
    finished(started([(v, v_ref)], out_sems))


def add_share(v, row, e, here, other, weights, masks, half):
    c, stay, cross = weights
    keep = 1.0 - OMEGA
    count = half // 2
    for first in (0, count):
        line = e[here, FAR + first - 1 : FAR + first + count + 1]
        common = (keep + c * stay + c) * line[1:-1] + (c * cross) * e[other, FAR + first : FAR + first + count]
        beside = c * line
        pairs = jnp.stack([common + beside[:-2], common + beside[2:]], axis=1)
        cells = slice(1 + 2 * first, 1 + 2 * (first + count))
        v[row, cells] = v[row, cells] + pairs.reshape(2 * count, *pairs.shape[2:])
    for near, beside, cell, mask in (
        (FAR - 1, FAR, 0, masks[0]), (FAR + half, FAR + half - 1, 2 * half + 1, masks[1]),
    ):
        c_side = c * mask
        v[row, cell] = v[row, cell] + (
            (keep + c_side * stay + c_side) * e[here, near]
            + (c_side * cross) * e[other, near]
            + c_side * e[here, beside]
        )


def finish_kernel(local_rows, block, tile_groups, *refs):
    (
        high_ref, low_ref, o_ref,
        s, e0, e1, v, g, w, o, t_high, t_low,
        c_ref, ahead_ref, behind_ref, cc_ref, cahead_ref, cbehind_ref, in_sems, out_sems,
    ) = refs[-20:]
    s_inner, s_head, s_tail, s_left, s_right, v_ref = refs[:6]
    position, squares = place(), mode_squares(c_ref.shape[1:])
    upper = position[0] == 1
    half_rows, half = local_rows // 2, block // 2
    pairs = [
        (s_inner, s.at[:, FAR + 1 : FAR + half - 1]),
        (s_head.at[:, 0:1], s.at[:, FAR : FAR + 1]),
        (s_tail.at[:, FAR - 1 : FAR], s.at[:, FAR + half - 1 : FAR + half]),
        (s_left, s.at[:, 0:FAR]),
        (s_right, s.at[:, FAR + half : FAR + half + FAR]),
    ]
    s_loads = started(pairs, in_sems)
    pairs = [(v_ref, v.at[: local_rows + 1])] + field_pairs(refs[6:11], g)
    pairs += [(high_ref, t_high), (low_ref, t_low)]
    loads = started(pairs, in_sems, len(s_loads))
    masks = side_masks(position, squares.shape)
    row_weights(upper, half_rows, -FAR, FAR + half_rows, squares, cc_ref, cahead_ref, cbehind_ref)
    row_weights(upper, local_rows, -1, 1 + local_rows, squares, c_ref, ahead_ref, behind_ref)
    coarse = (cc_ref, cahead_ref, cbehind_ref, -FAR)
    fine = (c_ref, ahead_ref, behind_ref, -1)
    for buffer in (e0, e1):
        buffer[FAR + half_rows] = jnp.zeros(buffer.shape[1:], jnp.float32)
    v[1 + local_rows] = jnp.zeros(v.shape[1:], jnp.float32)
    finished(s_loads)
    s_at = (s, -FAR, -FAR)
    here, there = (e0, -FAR, -FAR), (e1, -FAR, -FAR)
    first_sweep((-FAR, half_rows), (-FAR, half + FAR), half, s_at, here, coarse, masks)
    for step in range(1, COARSE):
        sweep(
            (step - FAR, half_rows), (step - FAR, half + FAR - step), half,
            here, s_at if step > 1 else None, there, coarse, masks,
        )
        here, there = there, here
    e = here[0]
    finished(loads)

    def add_rows(index, carry):
        row, at = 2 * index + 1, index + FAR
        even = (c_ref[row], ahead_ref[row], behind_ref[row])
        add_share(v, row, e, at, at - 1, even, masks, half)
        odd = (c_ref[row + 1], behind_ref[row + 1], ahead_ref[row + 1])
        add_share(v, row + 1, e, at, at + 1, odd, masks, half)
        return carry

    add_share(v, 0, e, FAR - 1, FAR, (c_ref[0], behind_ref[0], ahead_ref[0]), masks, half)
    lax.fori_loop(0, half_rows, add_rows, 0)
    v_at, g_at = (v, -1, -1), (g, -1, -1)
    group_rows = TILE // tile_groups
    turn = (position[1] & (group_rows - 1), group_rows)
    sweep((0, local_rows), (0, block), block, v_at, g_at, (w, 0, 0), fine, masks, turn)
    stores = []
    for n in range(local_rows // TILE):
        span = slice(n * tile_groups, (n + 1) * tile_groups)
        synthesis_tile(w.at[n * TILE : (n + 1) * TILE], t_high, t_low, o.at[:, span])
        stores += started([(o.at[:, span], o_ref.at[:, span])], out_sems, n)
    finished(stores)


def params(mebibytes, *order):
    return pltpu.CompilerParams(
        dimension_semantics=order or None, vmem_limit_bytes=mebibytes * 1024 * 1024
    )


def cell_body(density):
    local_phi, local_rows, vertical_cells = density.shape
    az_count = lax.axis_size("az")
    azimuths = local_phi * az_count
    block = vertical_cells // az_count
    rows = LANES // block
    tiles = local_rows // TILE
    groups = TILE // rows
    chunks = 2
    chunk_tiles = tiles // chunks
    chunk_rows = local_rows // chunks
    analysis, synthesis = mode_tables(azimuths)
    point = (azimuths // LANES, LANES)
    f32 = jnp.float32
    a_high, a_low = high_low(analysis)
    s_high, s_low = high_low(synthesis)
    order = block_order(az_count)
    product = 2 * 3 * azimuths * azimuths // 2
    lane_tiles = vertical_cells // LANES
    anywhere = pl.BlockSpec(memory_space=pl.ANY)
    in_hbm = pl.BlockSpec(memory_space=pltpu.HBM)

    def field(row_count, cell_count):
        return jax.ShapeDtypeStruct((row_count, cell_count) + point, f32)

    def scratch(row_count, *cell_count):
        return pltpu.VMEM((row_count,) + cell_count + point, f32)

    def semaphores(count):
        return pltpu.SemaphoreType.DMA((count,))

    def cost(mebibytes):
        return pl.CostEstimate(flops=0, bytes_accessed=mebibytes * 1024 * 1024, transcendentals=0)

    def pack(first_tile):
        return pl.pallas_call(
            lambda *refs: pack_kernel(block, order, first_tile, *refs),
            in_specs=[in_hbm],
            out_specs=in_hbm,
            out_shape=jax.ShapeDtypeStruct(
                (az_count, chunk_tiles * groups, local_phi, LANES), f32
            ),
            scratch_shapes=[
                pltpu.VMEM((chunk_tiles, lane_tiles, local_phi, TILE, LANES), f32),
                pltpu.VMEM((az_count, chunk_tiles * groups, local_phi, LANES), f32),
                pltpu.SemaphoreType.DMA((chunk_tiles * lane_tiles,)),
                pltpu.SemaphoreType.DMA((chunk_tiles,)),
            ],
            compiler_params=params(56),
            name="pack",
        )(density)

    half_rows, half = local_rows // 2, block // 2
    all_rows, coarse_rows = DEEP + local_rows, FAR + half_rows
    tables = [pltpu.VMEM((azimuths // 2, azimuths), jnp.bfloat16)] * 2

    def analyse(received, held):
        out_shape = [field(chunk_rows, block)]
        out_shape += [field(all_rows, NEAR)] * 2 if held else [field(DEEP, 2 * NEAR), field(DEEP, block)]
        return pl.pallas_call(
            lambda *refs: analysis_kernel(groups, len(held), *refs),
            in_specs=[in_hbm] * 3 + [anywhere] * len(held),
            out_specs=[anywhere] * len(out_shape),
            out_shape=out_shape,
            scratch_shapes=[
                pltpu.VMEM((az_count, chunk_tiles * groups, local_phi, LANES), f32),
                *tables,
                scratch(chunk_rows, block),
                scratch(all_rows, 2 * NEAR) if held else scratch(DEEP, block),
                semaphores(chunk_tiles),
                semaphores(2),
                semaphores(chunk_rows + 6),
            ],
            compiler_params=params(56),
            cost_estimate=cost(12),
            name="analysis",
        )(received, a_high, a_low, *held)

    def exchange(value):
        return lax.all_to_all(value, "az", split_axis=0, concat_axis=0, tiled=True)

    to_right = [(order[i], order[i + 1]) for i in range(az_count - 1)]
    to_left = [(b, a) for a, b in to_right]

    def from_sides(head, tail):
        return lax.ppermute(tail, "az", to_right), lax.ppermute(head, "az", to_left)

    first_received = exchange(pack(0))
    second_received = exchange(pack(chunk_tiles))
    near, edge_sides, edge = analyse(first_received, ())
    deep_sides = lax.ppermute(edge_sides, "rad", [(0, 1), (1, 0)])
    deep_sides, edge = lax.optimization_barrier((deep_sides, edge))
    deep = lax.ppermute(edge, "rad", [(0, 1), (1, 0)])
    far, head, tail = analyse(second_received, (deep_sides, near))
    fields = (deep, near, far, *from_sides(head, tail))

    wide = 2 * NEAR + 1
    weight_scratch = [scratch(all_rows)] * 3
    u_inner, s_inner = pl.pallas_call(
        lambda *refs: inner_kernel(local_rows, block, *refs),
        in_specs=[anywhere] * 3,
        out_specs=[anywhere] * 2,
        out_shape=[field(local_rows + 2, block - 2), field(coarse_rows, half - 2)],
        scratch_shapes=[
            scratch(all_rows, block),
            scratch(all_rows + 1, block),
            scratch(all_rows, block - 2),
            scratch(coarse_rows, half - 2),
            *weight_scratch,
            semaphores(3),
            semaphores(2),
        ],
        compiler_params=params(28),
        cost_estimate=cost(32),
        name="inner",
    )(*fields[:3])
    u_left, u_right, s_head, s_tail = pl.pallas_call(
        lambda *refs: outer_kernel(local_rows, block, *refs),
        in_specs=[anywhere] * 6,
        out_specs=[anywhere] * 4,
        out_shape=[field(local_rows + 2, NEAR)] * 2 + [field(coarse_rows, FAR)] * 2,
        scratch_shapes=[
            scratch(all_rows, wide),
            scratch(all_rows, wide),
            scratch(all_rows + 1, wide),
            scratch(all_rows, wide - 2),
            scratch(all_rows, wide - 2),
            scratch(coarse_rows, 1),
            scratch(coarse_rows, 1),
            scratch(coarse_rows, FAR),
            scratch(coarse_rows, FAR),
            *weight_scratch,
            semaphores(10),
            semaphores(4),
        ],
        compiler_params=params(20),
        cost_estimate=cost(12),
        name="outer",
    )(*fields, s_inner)
    s_parts = (s_inner, s_head, s_tail, *from_sides(s_head, s_tail))

    settled = pl.pallas_call(
        lambda *refs: settle_kernel(local_rows, block, *refs),
        in_specs=[anywhere] * 8,
        out_specs=anywhere,
        out_shape=field(local_rows + 1, block + 2),
        scratch_shapes=[
            scratch(local_rows + 3, block + 4),
            scratch(local_rows + 1, block + 2),
            scratch(local_rows + 1, block + 2),
            *[scratch(local_rows + 1)] * 3,
            semaphores(8),
            semaphores(1),
        ],
        compiler_params=params(24),
        cost_estimate=cost(16),
        name="settle",
    )(u_inner, u_left, u_right, *fields)

    received_shape = (az_count, tiles * groups, local_phi, LANES)
    physical = pl.pallas_call(
        lambda *refs: finish_kernel(local_rows, block, groups, *refs),
        in_specs=[anywhere] * 11 + [in_hbm] * 2,
        out_specs=in_hbm,
        out_shape=jax.ShapeDtypeStruct(received_shape, f32),
        scratch_shapes=[
            scratch(coarse_rows, half + 2 * FAR),
            scratch(coarse_rows + 1, half + 2 * FAR),
            scratch(coarse_rows + 1, half + 2 * FAR),
            scratch(local_rows + 2, block + 2),
            scratch(local_rows + 1, block + 2),
            scratch(local_rows, block),
            pltpu.VMEM(received_shape, f32),
            *tables,
            scratch(local_rows + 1),
            scratch(local_rows + 1),
            scratch(local_rows + 1),
            scratch(coarse_rows),
            scratch(coarse_rows),
            scratch(coarse_rows),
            semaphores(13),
            semaphores(tiles),
        ],
        compiler_params=params(46),
        name="finish",
    )(*s_parts, settled, *fields, s_high, s_low)

    returned = exchange(physical)
    side = jnp.stack([lax.axis_index("rad"), lax.axis_index("az")]).astype(jnp.int32)
    return pl.pallas_call(
        lambda *refs: unpack_kernel(block, order, *refs),
        in_specs=[in_hbm, anywhere],
        out_specs=in_hbm,
        out_shape=jax.ShapeDtypeStruct(density.shape, f32),
        scratch_shapes=[
            pltpu.VMEM((az_count, tiles * groups, local_phi, LANES), f32),
            pltpu.VMEM((tiles, lane_tiles, local_phi, TILE, LANES), f32),
            pltpu.SemaphoreType.DMA((tiles,)),
            pltpu.SemaphoreType.DMA((tiles * lane_tiles,)),
        ],
        compiler_params=params(56),
        name="unpack",
    )(returned, side)


def block_order(az_count):
    return [i ^ 2 if (i // 4) % 2 else i for i in range(az_count)]


def fits_cells(density):
    local_phi, local_rows, vertical_cells = density.shape
    az_count, rad_count = lax.axis_size("az"), lax.axis_size("rad")
    block = vertical_cells // az_count
    return (
        rad_count == 2
        and vertical_cells % (az_count * 2) == 0
        and vertical_cells % LANES == 0
        and LANES // TILE <= block <= LANES
        and LANES % block == 0
        and block // 2 >= FAR
        and local_rows % (4 * TILE) == 0
        and local_rows // 2 >= DEEP
        and az_count % 4 == 0
        and local_phi % TILE == 0
        and (az_count * local_phi) % (2 * LANES) == 0
        and az_count * local_phi == TILE * LANES
    )


def body(density):
    return cell_body(density) if fits_cells(density) else general_body(density)


def solution(mesh):
    placed = (P("az", "rad", None),)
    return jax.shard_map(
        body, mesh=mesh, in_specs=placed, out_specs=P("az", "rad", None), check_vma=False
    )
```

```python
import math

import jax
import jax.numpy as jnp
import numpy as np
from jax import lax
from jax.experimental import pallas as pl
from jax.experimental.pallas import tpu as pltpu
from jax.sharding import PartitionSpec as P

PRE = 2
POST = 2
COARSE = 6


OMEGA = 0.8

LANES = 128
TILE = 8
DEEP = 2 * COARSE + 2
NEAR = 3
FAR = COARSE


def with_halo(cells, sides, width):
    for axis, dim in sides:
        count = lax.axis_size(axis)
        ends = count - 1
        head = lax.slice_in_dim(cells, 0, width, axis=dim)
        tail = lax.slice_in_dim(cells, cells.shape[dim] - width, cells.shape[dim], axis=dim)
        cells = jnp.concatenate(
            [
                lax.ppermute(tail, axis, [(i, (i + 1) % count) for i in range(ends)]),
                cells,
                lax.ppermute(head, axis, [((i + 1) % count, i) for i in range(ends)]),
            ],
            axis=dim,
        )
    return cells


def level_coefficients(first_row, row_count, spacing, mode_numbers):
    row_number = (jnp.arange(row_count, dtype=jnp.int32) + first_row).astype(jnp.float32)
    radius = spacing * (row_number + 0.5)
    outward = (row_number + 1.0) / (spacing * radius)
    inward = row_number / (spacing * radius)
    vertical = 1.0 / (spacing * spacing)
    diagonal = (outward + inward + 2.0 * vertical)[None, :] + (
        mode_numbers[:, None] / radius[None, :]
    ) ** 2
    return (diagonal[:, :, None], outward[None, :, None], inward[None, :, None], vertical)


def apply_op(iterate, padded, coefficients):
    diagonal, outward, inward, vertical = coefficients
    return (
        diagonal * iterate
        - outward * padded[:, 2:, 1:-1]
        - inward * padded[:, :-2, 1:-1]
        - vertical * (padded[:, 1:-1, 2:] + padded[:, 1:-1, :-2])
    )


def relax(iterate, source, coefficients, pad_both):
    return (
        iterate
        + OMEGA * (source - apply_op(iterate, pad_both(iterate), coefficients)) / coefficients[0]
    )


def restrict(residual):
    k_count, r_count, z_count = residual.shape
    parts = residual.reshape(k_count, r_count // 2, 2, z_count // 2, 2)
    return 0.25 * (
        parts[:, :, 0, :, 0] + parts[:, :, 1, :, 0] + parts[:, :, 0, :, 1] + parts[:, :, 1, :, 1]
    )


def prolong(correction):
    return jnp.repeat(jnp.repeat(correction, 2, axis=1), 2, axis=2)


def pad_level(field):
    rows = with_halo(field, (("rad", 1),), 1)
    return jnp.pad(rows, ((0, 0), (0, 0), (1, 1)))


def mode_values(mode_index, azimuths):
    return jnp.where(mode_index <= azimuths // 2, mode_index, mode_index - azimuths // 2).astype(
        jnp.float32
    )


def fine_cycle(source, fine_coef, pad_sweep, coarse_solve):
    iterate = OMEGA * source / fine_coef[0]
    for sweep_index in range(PRE - 1):
        iterate = relax(iterate, source, fine_coef, pad_sweep)
    residual = source - apply_op(iterate, pad_sweep(iterate), fine_coef)
    iterate = iterate + prolong(coarse_solve(restrict(residual)))
    for sweep_index in range(POST):
        iterate = relax(iterate, source, fine_coef, pad_sweep)
    return iterate


def general_body(density):
    local_phi, local_rows, vertical_cells = density.shape
    az_count = lax.axis_size("az")
    azimuths = local_phi * az_count
    cell_count = local_rows * vertical_cells // az_count
    numbers = jnp.arange(azimuths, dtype=jnp.int32)
    all_modes = jnp.where(numbers <= azimuths // 2, numbers, numbers - azimuths // 2)
    phase = all_modes[:, None] * numbers[None, :] % azimuths
    phase_angle = phase.astype(jnp.float32) * (2.0 * math.pi / azimuths)
    analysis_table = jnp.where(
        (numbers <= azimuths // 2)[:, None], jnp.cos(phase_angle), jnp.sin(phase_angle)
    )
    synth_weight = jnp.where(
        (numbers == 0) | (numbers == azimuths // 2), 1.0 / azimuths, 2.0 / azimuths
    )
    synthesis_table = analysis_table.T * synth_weight[None, :]

    def transform_with(table, columns):
        width = columns.shape[2]
        matrix = columns.reshape(azimuths, width)
        result = jnp.dot(
            table, matrix, precision=lax.Precision.HIGHEST, preferred_element_type=jnp.float32
        )
        return result.reshape(azimuths, 1, width)

    lines = density.reshape(local_phi, az_count, cell_count)
    spectral = transform_with(
        analysis_table, lax.all_to_all(lines, "az", split_axis=1, concat_axis=0, tiled=True)
    )
    coefficients = lax.all_to_all(spectral, "az", split_axis=0, concat_axis=1, tiled=True)
    source = -coefficients.reshape(local_phi, local_rows, vertical_cells)
    rad_index = lax.axis_index("rad")
    half_rows = local_rows // 2
    mode_index = lax.axis_index("az") * local_phi + jnp.arange(local_phi, dtype=jnp.int32)
    mode_numbers = mode_values(mode_index, azimuths)
    fine_coef = level_coefficients(rad_index * local_rows, local_rows, 1.0, mode_numbers)
    coarse_coef = level_coefficients(rad_index * half_rows, half_rows, 2.0, mode_numbers)

    def coarse_halo(coarse_source):
        correction = OMEGA * coarse_source / coarse_coef[0]
        for sweep_index in range(COARSE - 1):
            correction = relax(correction, coarse_source, coarse_coef, pad_level)
        return correction

    iterate = fine_cycle(source, fine_coef, pad_level, coarse_halo)
    mode_lines = iterate.reshape(local_phi, az_count, cell_count)
    physical = transform_with(
        synthesis_table, lax.all_to_all(mode_lines, "az", split_axis=1, concat_axis=0, tiled=True)
    )
    field = lax.all_to_all(physical, "az", split_axis=0, concat_axis=1, tiled=True)
    return field.reshape(local_phi, local_rows, vertical_cells)


def mode_tables(azimuths):
    half, quarter = azimuths // 2, azimuths // 4
    fours = np.concatenate([np.arange(0, half + 1, 4), np.arange(4, half, 4)])
    twos = np.concatenate([np.arange(2, half, 4)] * 2)
    odd = np.concatenate([np.arange(1, half, 2)] * 2)
    modes = np.concatenate([fours, twos, odd])
    index = np.arange(quarter)
    is_cos = np.concatenate(
        [index <= quarter // 2, index < quarter // 2, np.arange(half) < quarter]
    )
    angle = 2.0 * np.pi / azimuths * (np.arange(half)[:, None] * modes[None, :] % azimuths)
    values = np.where(is_cos[None, :], np.cos(angle), np.sin(angle))
    weighted = values * (np.where((modes == 0) | (modes == half), 1.0, 2.0) / azimuths)[None, :]
    return -values, weighted


def table_parts(table, azimuths):
    quarter = azimuths // 4
    return [
        (table.at[0:quarter, 0:quarter], 0),
        (table.at[0:quarter, quarter : 2 * quarter], quarter),
        (table.at[:, 2 * quarter :], 2 * quarter),
    ]


def high_low(values):
    values = values.astype(np.float32)
    high = values.astype(jnp.bfloat16)
    low = (values - high.astype(np.float32)).astype(jnp.bfloat16)
    return jnp.asarray(high), jnp.asarray(low)


def split_value(value):
    high = value.astype(jnp.bfloat16)
    return high, (value - high.astype(jnp.float32)).astype(jnp.bfloat16)


def place():
    az = lax.axis_index("az")
    return lax.axis_index("rad"), az ^ (((az >> 2) & 1) << 1), lax.axis_size("az")


def mode_squares(shape):
    half = shape[0] * shape[1] // 2
    quarter, eighth = half // 2, half // 4
    index = lax.broadcasted_iota(jnp.int32, shape, 0) * shape[1] + lax.broadcasted_iota(jnp.int32, shape, 1)
    fours = 4 * jnp.where(index <= eighth, index, index - eighth)
    twos = 4 * (index & (eighth - 1)) + 2
    odd = 2 * (index & (quarter - 1)) + 1
    modes = jnp.where(index < quarter, fours, jnp.where(index < half, twos, odd))
    return (modes * modes).astype(jnp.float32)


def row_tile(position, local_rows, tile):
    return jnp.where(position[0] == 0, local_rows // TILE - 1 - tile, tile)


def chunk_masks(count, shape):
    lane = lax.broadcasted_iota(jnp.int32, shape, len(shape) - 1) // (LANES // count)
    return [lane == p for p in range(1, count)]


def pick_chunks(parts, masks):
    result = parts[0]
    for part, mask in zip(parts[1:], masks):
        result = jnp.where(mask, part, result)
    return result


def gather_rows(parts, masks):
    count = len(parts)
    chunk = LANES // count
    turned = [pltpu.roll(part, i * chunk, 1) if i else part for i, part in enumerate(parts)]
    return [pick_chunks([turned[(p - q) % count] for p in range(count)], masks) for q in range(count)]


def scatter_rows(parts, masks):
    count = len(parts)
    chunk = LANES // count
    rows = [pick_chunks([parts[(p - i) % count] for p in range(count)], masks) for i in range(count)]
    return [pltpu.roll(row, LANES - i * chunk, 1) if i else row for i, row in enumerate(rows)]


def turned_row(row, turn, rows):
    low = row & (rows - 1)
    return row - low + ((low + turn) & (rows - 1))


def tile_row(position, row):
    return jnp.where(position[0] == 0, TILE - 1 - row, row)


def pack_kernel(block, order, first_tile, x_ref, o_ref, x, o, in_sems, out_sems):
    position = place()
    rows = LANES // block
    local_phi, local_rows, cells = x_ref.shape
    tiles, lane_tiles, groups = x.shape[0], x.shape[1], TILE // rows
    pieces = [(j, k) for j in range(tiles) for k in range(lane_tiles)]
    masks = chunk_masks(rows, (local_phi, LANES))
    loads, stores = [], []
    for n, (j, k) in enumerate(pieces):
        start = pl.multiple_of(row_tile(position, local_rows, first_tile + j) * TILE, TILE)
        source = x_ref.at[:, pl.ds(start, TILE), k * LANES : (k + 1) * LANES]
        loads.append(pltpu.make_async_copy(source, x.at[j, k], in_sems.at[n]))
        loads[-1].start()
    for n, (j, k) in enumerate(pieces):
        loads[n].wait()
        flat = x.at[j, k].reshape(local_phi * TILE, LANES)
        for group in range(groups):
            parts = [
                flat[pl.ds(tile_row(position, group * rows + i), local_phi, stride=TILE), :]
                for i in range(rows)
            ]
            for q, part in enumerate(gather_rows(parts, masks)):
                o[order[k * rows + q], j * groups + group] = part
        if k == lane_tiles - 1:
            span = slice(j * groups, (j + 1) * groups)
            stores.append(pltpu.make_async_copy(o.at[:, span], o_ref.at[:, span], out_sems.at[j]))
            stores[-1].start()
    for store in stores:
        store.wait()


def unpack_kernel(block, order, x_ref, _, o_ref, x, o, in_sems, out_sems):
    position = place()
    rows = LANES // block
    local_phi, local_rows, cells = o_ref.shape
    tiles, lane_tiles, groups = o.shape[0], o.shape[1], TILE // rows
    masks = chunk_masks(rows, (local_phi, LANES))
    loads, stores = [], []
    for j in range(tiles):
        span = slice(j * groups, (j + 1) * groups)
        loads.append(pltpu.make_async_copy(x_ref.at[:, span], x.at[:, span], in_sems.at[j]))
        loads[-1].start()
    for j in range(tiles):
        loads[j].wait()
        start = pl.multiple_of(row_tile(position, local_rows, j) * TILE, TILE)
        for k in range(lane_tiles):
            flat = o.at[j, k].reshape(local_phi * TILE, LANES)
            for group in range(groups):
                parts = [x[order[k * rows + q], j * groups + group] for q in range(rows)]
                for i, part in enumerate(scatter_rows(parts, masks)):
                    at = tile_row(position, group * rows + i)
                    flat[pl.ds(at, local_phi, stride=TILE), :] = part
            target = o_ref.at[:, pl.ds(start, TILE), k * LANES : (k + 1) * LANES]
            stores.append(
                pltpu.make_async_copy(o.at[j, k], target, out_sems.at[j * lane_tiles + k])
            )
            stores[-1].start()
    for store in stores:
        store.wait()


def started(pairs, sems, first=0):
    copies = []
    for n, (src, dst) in enumerate(pairs):
        copies.append(pltpu.make_async_copy(src, dst, sems.at[first + n]))
        copies[-1].start()
    return copies


def finished(copies):
    for copy in copies:
        copy.wait()


def sides_of(field, depth):
    cells = field.shape[1]
    return field, field.at[:, :depth], field.at[:, cells - depth : cells]


def analysis_kernel(tile_groups, held_count, *refs):
    position = place()
    x_ref, high_ref, low_ref = refs[:3]
    outs = refs[3:-8]
    x, t_high, t_low, o, edge, in_sems, t_sems, out_sems = refs[-8:]
    held_refs, outs = outs[:held_count], outs[held_count:]
    sources, width, lanes = x.shape[0], x.shape[2], x.shape[3]
    cells = o.shape[1]
    half = sources // 2 * width
    tiles = x.shape[1] // tile_groups
    spans = [slice(n * tile_groups, (n + 1) * tile_groups) for n in range(tiles)]
    pairs = [(x_ref.at[:, span], x.at[:, span]) for span in spans]
    tables = started([(high_ref, t_high), (low_ref, t_low)], t_sems)
    loads = started(pairs, in_sems)
    group_rows = TILE // tile_groups
    turn = position[1] & (group_rows - 1)
    gathers, start = [], 0
    for held in held_refs:
        span = slice(start, start + held.shape[0])
        if held.shape[1] == 2 * NEAR:
            pairs = [(held, edge.at[span])]
        else:
            sides = zip(sides_of(held, NEAR)[1:], (slice(0, NEAR), slice(NEAR, 2 * NEAR)))
            pairs = [(side, edge.at[span, columns]) for side, columns in sides]
        gathers += started(pairs, out_sems, out_sems.shape[0] - 4 + len(gathers))
        start += held.shape[0]
    stores = []
    for n in range(tiles):
        loads[n].wait()
        turned = [[], [], []]
        for group in range(n * tile_groups, (n + 1) * tile_groups):
            near = x[: sources // 2, group].reshape(half, lanes)
            far = x[sources // 2 :, group].reshape(half, lanes)
            even = near + far
            low_half, high_half = even[: half // 2], even[half // 2 :]
            for part, folded in zip(turned, (low_half + high_half, low_half - high_half, near - far)):
                part.append(folded.T)
        parts = [split_value(jnp.concatenate(part, axis=0)) for part in turned]
        if n == 0:
            finished(tables)
        rows = slice(n * TILE, (n + 1) * TILE)
        columns = zip(parts, table_parts(t_high, 2 * half), table_parts(t_low, 2 * half))
        for (high, low), (part_high, first), (part_low, _) in columns:
            result = (
                jnp.dot(high, part_high[...], preferred_element_type=jnp.float32)
                + jnp.dot(high, part_low[...], preferred_element_type=jnp.float32)
                + jnp.dot(low, part_high[...], preferred_element_type=jnp.float32)
            )
            for part in range(result.shape[1] // LANES):
                piece = result[:, part * LANES : (part + 1) * LANES]
                o[rows, :, first // LANES + part, :] = piece.reshape(TILE, cells, LANES)
        pairs = [
            (o.at[turned_row(row, turn, group_rows)], outs[0].at[row])
            for row in range(n * TILE, (n + 1) * TILE)
        ]
        stores += started(pairs, out_sems, len(stores))
    if held_refs:
        finished(gathers)
        for row in range(o.shape[0]):
            at = turned_row(row, turn, group_rows)
            edge[start + row, :NEAR] = o[at, :NEAR]
            edge[start + row, NEAR:] = o[at, cells - NEAR :]
        pairs = [(edge.at[:, :NEAR], outs[1]), (edge.at[:, NEAR:], outs[2])]
        stores += started(pairs, out_sems, len(stores))
    else:
        for row in range(DEEP):
            edge[DEEP - 1 - row] = o[turned_row(row, turn, group_rows)]
        _, head, tail = sides_of(edge, NEAR)
        pairs = [(head, outs[1].at[:, :NEAR]), (tail, outs[1].at[:, NEAR:]), (edge, outs[2])]
        stores += started(pairs, out_sems, len(stores))
    finished(stores)


def synthesis_tile(u, t_high, t_low, o):
    rows, cells = u.shape[0], u.shape[1]
    half = t_high.shape[0]
    contract = (((1,), (1,)), ((), ()))
    sums = []
    for (part_high, first), (part_low, _) in zip(table_parts(t_high, 2 * half), table_parts(t_low, 2 * half)):
        parts = range(first // LANES, (first + part_high.shape[1]) // LANES)
        field = jnp.concatenate([u[:, :, i, :].reshape(rows * cells, LANES) for i in parts], axis=1)
        high, low = split_value(field)
        sums.append(
            lax.dot_general(part_high[...], high, contract, preferred_element_type=jnp.float32)
            + lax.dot_general(part_high[...], low, contract, preferred_element_type=jnp.float32)
            + lax.dot_general(part_low[...], high, contract, preferred_element_type=jnp.float32)
        )
    fours, twos, odd = sums
    even = jnp.concatenate([fours + twos, fours - twos], axis=0)
    near, far = even + odd, even - odd
    targets, groups, width, lanes = o.shape
    for group in range(groups):
        columns = slice(group * lanes, (group + 1) * lanes)
        o[: targets // 2, group] = near[:, columns].reshape(targets // 2, width, lanes)
        o[targets // 2 :, group] = far[:, columns].reshape(targets // 2, width, lanes)


def row_weights(upper, boundary, first, count, squares, c_ref, ahead_ref, behind_ref):
    def one(index, carry):
        row = jnp.where(upper, index + (boundary + first), (boundary - 1 - first) - index)
        number = jnp.full(squares.shape, row, jnp.int32).astype(jnp.float32)
        radius = number + 0.5
        outward = (number + 1.0) / radius
        inward = number / radius
        diagonal = outward + inward + 2.0 + squares / (radius * radius)
        c_ref[index] = OMEGA / diagonal
        ahead_ref[index] = jnp.where(upper, outward, inward)
        behind_ref[index] = jnp.where(upper, inward, outward)
        return carry

    lax.fori_loop(0, count, one, 0)


def cell_tiles(first, last, cells, size=16):
    tiles = []
    if first < 0:
        tiles.append((first, -first, -1))
    for start in range(max(first, 0), min(last, cells), size):
        tiles.append((start, min(size, min(last, cells) - start), 0))
    if last > cells:
        tiles.append((cells, last - cells, 1))
    return tiles


def run_rows(count, *bodies):
    def both(pair, carry):
        for body in bodies:
            body(2 * pair + count % 2, None)
        for body in bodies:
            body(2 * pair + (1 + count % 2), None)
        return carry

    if count % 2:
        for body in bodies:
            body(0, None)
    lax.fori_loop(0, count // 2, both, 0)


def sweep(*args):
    run_rows(*sweep_rows(*args))


def first_sweep(*args):
    run_rows(*first_sweep_rows(*args))


def sweep_rows(rows, cells, block, src, source, dst, weights, masks, turn=None):
    (src_ref, src_t, src_z), (dst_ref, dst_t, dst_z) = src, dst
    keep = 1.0 - OMEGA if source else 2.0 - OMEGA
    c_ref, ahead_ref, behind_ref, w_t = weights
    low = rows[0]

    def one(step, carry):
        at = step + (low - w_t)
        target = step + (low - dst_t)
        if turn:
            target = turned_row(target, *turn)
        c_row, ahead, behind = c_ref[at], ahead_ref[at], behind_ref[at]
        for first, count, side in cell_tiles(cells[0], cells[1], block):
            c = c_row if side == 0 else c_row * masks[0 if side < 0 else 1]
            z = first - src_z
            row = low - src_t
            middle = src_ref[step + row, z - 1 : z + count + 1]
            gathered = (
                ahead * src_ref[step + (row + 1), z : z + count]
                + behind * src_ref[step + (row - 1), z : z + count]
                + (middle[:-2] + middle[2:])
            )
            if source:
                g_ref, g_t, g_z = source
                gathered += g_ref[step + (low - g_t), first - g_z : first - g_z + count]
            dst_ref[target, first - dst_z : first - dst_z + count] = (
                keep * middle[1:-1] + c * gathered
            )
        return carry

    return rows[1] - low, one


def first_sweep_rows(rows, cells, block, source, dst, weights, masks):
    (g_ref, g_t, g_z), (dst_ref, dst_t, dst_z) = source, dst
    c_ref, w_t = weights[0], weights[3]
    low = rows[0]

    def one(step, carry):
        c_row = c_ref[step + (low - w_t)]
        for first, count, side in cell_tiles(cells[0], cells[1], block):
            c = c_row if side == 0 else c_row * masks[0 if side < 0 else 1]
            dst_ref[step + (low - dst_t), first - dst_z : first - dst_z + count] = (
                c * g_ref[step + (low - g_t), first - g_z : first - g_z + count]
            )
        return carry

    return rows[1] - low, one


def side_masks(position, shape):
    left = jnp.full(shape, position[1] > 0).astype(jnp.float32)
    right = jnp.full(shape, position[1] < position[2] - 1).astype(jnp.float32)
    return left, right


def smooth_columns(local_rows, block, strips, weights, masks):
    first = -DEEP
    firsts, seconds, restricts = [], [], []
    for cells, g, u1, u2, s in strips:
        low, high = cells
        g_at, u1_at, u2_at = (g, first, low), (u1, first, low), (u2, first + 1, low + 1)
        total = g.shape[0]
        u1[total] = jnp.zeros(u1.shape[1:], jnp.float32)
        u2[total - 1] = jnp.zeros(u2.shape[1:], jnp.float32)
        firsts.append(first_sweep_rows((first, local_rows), cells, block, g_at, u1_at, weights, masks))
        rows, inside = (first + 1, local_rows), (low + 1, high - 1)
        seconds.append(sweep_rows(rows, inside, block, u1_at, None, u2_at, weights, masks))
        restricts.append(restrict_rows(cells, block, g, u2, s, weights))
    for stage in (firsts, seconds, restricts):
        run_rows(stage[0][0], *[body for _, body in stage])


def restrict_rows(cells, block, g, u2, s, weights):
    low = cells[0]
    c_ref, ahead_ref, behind_ref, _ = weights
    start = max(low + 2, 0)
    start += start % 2

    def paired(values):
        pairs = values.reshape(values.shape[0] // 2, 2, *values.shape[1:])
        return pairs[:, 0], pairs[:, 1]

    def pair_sums(values):
        even, odd = paired(values)
        return even + odd

    def restrict_row(index, carry):
        row = 2 * index + (DEEP - 2 * FAR)
        center = behind_ref[row + 1] - OMEGA / c_ref[row] + 1.0
        center_ahead = ahead_ref[row] - OMEGA / c_ref[row + 1] + 1.0
        behind, ahead = behind_ref[row], ahead_ref[row + 1]
        for at, count, _ in cell_tiles(start, start + 2 * s.shape[1], block):
            z = at - (low + 1)
            here = u2[row - 1, z - 1 : z + count + 1]
            there = u2[row, z - 1 : z + count + 1]
            even, odd = paired(here + there)
            cells = slice(at - low, at - low + count)
            column = (at - start) // 2
            s[index, column : column + count // 2] = (
                pair_sums(g[row, cells] + g[row + 1, cells])
                + (even[:-1] + odd[1:])
                + behind * pair_sums(u2[row - 2, z : z + count])
                + center * pair_sums(here[1:-1])
                + center_ahead * pair_sums(there[1:-1])
                + ahead * pair_sums(u2[row + 1, z : z + count])
            )
        return carry

    return s.shape[0], restrict_row


def inner_kernel(
    local_rows, block, deep_ref, near_ref, far_ref, u_ref, s_ref,
    g, u1, u2, s, c_ref, ahead_ref, behind_ref, in_sems, out_sems,
):
    pairs, start = [], 0
    for ref in (deep_ref, near_ref, far_ref):
        pairs.append((ref, g.at[start : start + ref.shape[0]]))
        start += ref.shape[0]
    loads = started(pairs, in_sems)
    position, squares = place(), mode_squares(c_ref.shape[1:])
    upper = position[0] == 1
    row_weights(upper, local_rows, -DEEP, DEEP + local_rows, squares, c_ref, ahead_ref, behind_ref)
    weights = (c_ref, ahead_ref, behind_ref, -DEEP)
    finished(loads)
    smooth_columns(local_rows, block, [((0, block), g, u1, u2, s)], weights, None)
    pairs = [(u2.at[DEEP - 3 : DEEP - 1 + local_rows], u_ref), (s, s_ref)]
    finished(started(pairs, out_sems))


def outer_kernel(
    local_rows, block,
    deep_ref, near_ref, far_ref, left_ref, right_ref, inner_ref,
    u_left_ref, u_right_ref, head_ref, tail_ref,
    g_left, g_right, u1_left, u1_right, u2_left, u2_right, s_left, s_right, head, tail,
    c_ref, ahead_ref, behind_ref, in_sems, out_sems,
):
    wide = g_left.shape[1]
    own = wide - NEAR
    pairs, start = [], 0
    for ref in (deep_ref, near_ref, far_ref):
        span = slice(start, start + ref.shape[0])
        pairs.append((ref.at[:, :own], g_left.at[span, NEAR:]))
        pairs.append((ref.at[:, block - own :], g_right.at[span, :own]))
        start = span.stop
    pairs += [(left_ref, g_left.at[:, :NEAR]), (right_ref, g_right.at[:, own:])]
    inner = inner_ref.shape[1]
    pairs += [(inner_ref.at[:, : FAR - 1], head.at[:, 1:])]
    pairs += [(inner_ref.at[:, inner - FAR + 1 :], tail.at[:, : FAR - 1])]
    loads = started(pairs, in_sems)
    position, squares = place(), mode_squares(c_ref.shape[1:])
    upper = position[0] == 1
    row_weights(upper, local_rows, -DEEP, DEEP + local_rows, squares, c_ref, ahead_ref, behind_ref)
    masks = side_masks(position, squares.shape)
    weights = (c_ref, ahead_ref, behind_ref, -DEEP)
    finished(loads)
    rows = slice(DEEP - 3, DEEP - 1 + local_rows)
    strips = [
        ((-NEAR, own), g_left, u1_left, u2_left, s_left),
        ((block - own, block + NEAR), g_right, u1_right, u2_right, s_right),
    ]
    smooth_columns(local_rows, block, strips, weights, masks)
    head[:, 0] = s_left[:, 0]
    tail[:, FAR - 1] = s_right[:, 0]
    pairs = [(head, head_ref), (tail, tail_ref), (u2_left.at[rows, :NEAR], u_left_ref)]
    pairs.append((u2_right.at[rows, wide - 2 - NEAR :], u_right_ref))
    finished(started(pairs, out_sems))


def field_pairs(g_refs, g):
    pairs, start = [], 0
    local_rows, middle = g.shape[0] - 1, slice(1, g.shape[1] - 1)
    for ref in g_refs[:3]:
        rows = slice(DEEP - 1, DEEP) if start == 0 else slice(0, ref.shape[0])
        count = rows.stop - rows.start
        pairs.append((ref.at[rows], g.at[start : start + count, middle]))
        start += count
    rows = slice(DEEP - 1, DEEP + local_rows)
    pairs.append((g_refs[3].at[rows, NEAR - 1 : NEAR], g.at[:, 0:1]))
    pairs.append((g_refs[4].at[rows, 0:1], g.at[:, middle.stop : middle.stop + 1]))
    return pairs


def settle_kernel(
    local_rows, block, inner_ref, left_ref, right_ref, *refs
):
    g_refs = refs[:5]
    v_ref, u, g, v, c_ref, ahead_ref, behind_ref, in_sems, out_sems = refs[5:]
    rows = slice(0, local_rows + 2)
    pairs = [
        (left_ref, u.at[rows, :NEAR]),
        (inner_ref, u.at[rows, NEAR : NEAR + block - 2]),
        (right_ref, u.at[rows, NEAR + block - 2 :]),
    ]
    loads = started(pairs + field_pairs(g_refs, g), in_sems)
    position, squares = place(), mode_squares(c_ref.shape[1:])
    masks = side_masks(position, squares.shape)
    upper = position[0] == 1
    row_weights(upper, local_rows, -1, 1 + local_rows, squares, c_ref, ahead_ref, behind_ref)
    u[2 + local_rows] = jnp.zeros(u.shape[1:], jnp.float32)
    finished(loads)
    u_at, v_at, g_at = (u, -2, -2), (v, -1, -1), (g, -1, -1)
    weights = (c_ref, ahead_ref, behind_ref, -1)
    sweep((-1, local_rows), (-1, block + 1), block, u_at, g_at, v_at, weights, masks)
    finished(started([(v, v_ref)], out_sems))


def add_share(v, row, e, here, other, weights, masks, half):
    c, stay, cross = weights
    keep = 1.0 - OMEGA
    count = half // 2
    for first in (0, count):
        line = e[here, FAR + first - 1 : FAR + first + count + 1]
        common = (keep + c * stay + c) * line[1:-1] + (c * cross) * e[other, FAR + first : FAR + first + count]
        beside = c * line
        pairs = jnp.stack([common + beside[:-2], common + beside[2:]], axis=1)
        cells = slice(1 + 2 * first, 1 + 2 * (first + count))
        v[row, cells] = v[row, cells] + pairs.reshape(2 * count, *pairs.shape[2:])
    for near, beside, cell, mask in (
        (FAR - 1, FAR, 0, masks[0]), (FAR + half, FAR + half - 1, 2 * half + 1, masks[1]),
    ):
        c_side = c * mask
        v[row, cell] = v[row, cell] + (
            (keep + c_side * stay + c_side) * e[here, near]
            + (c_side * cross) * e[other, near]
            + c_side * e[here, beside]
        )


def finish_kernel(local_rows, block, tile_groups, *refs):
    (
        high_ref, low_ref, o_ref,
        s, e0, e1, v, g, w, o, t_high, t_low,
        c_ref, ahead_ref, behind_ref, cc_ref, cahead_ref, cbehind_ref, in_sems, out_sems,
    ) = refs[-20:]
    s_inner, s_head, s_tail, s_left, s_right, v_ref = refs[:6]
    position, squares = place(), mode_squares(c_ref.shape[1:])
    upper = position[0] == 1
    half_rows, half = local_rows // 2, block // 2
    pairs = [
        (s_inner, s.at[:, FAR + 1 : FAR + half - 1]),
        (s_head.at[:, 0:1], s.at[:, FAR : FAR + 1]),
        (s_tail.at[:, FAR - 1 : FAR], s.at[:, FAR + half - 1 : FAR + half]),
        (s_left, s.at[:, 0:FAR]),
        (s_right, s.at[:, FAR + half : FAR + half + FAR]),
    ]
    s_loads = started(pairs, in_sems)
    pairs = [(v_ref, v.at[: local_rows + 1])] + field_pairs(refs[6:11], g)
    pairs += [(high_ref, t_high), (low_ref, t_low)]
    loads = started(pairs, in_sems, len(s_loads))
    masks = side_masks(position, squares.shape)
    row_weights(upper, half_rows, -FAR, FAR + half_rows, squares, cc_ref, cahead_ref, cbehind_ref)
    row_weights(upper, local_rows, -1, 1 + local_rows, squares, c_ref, ahead_ref, behind_ref)
    coarse = (cc_ref, cahead_ref, cbehind_ref, -FAR)
    fine = (c_ref, ahead_ref, behind_ref, -1)
    for buffer in (e0, e1):
        buffer[FAR + half_rows] = jnp.zeros(buffer.shape[1:], jnp.float32)
    v[1 + local_rows] = jnp.zeros(v.shape[1:], jnp.float32)
    finished(s_loads)
    s_at = (s, -FAR, -FAR)
    here, there = (e0, -FAR, -FAR), (e1, -FAR, -FAR)
    first_sweep((-FAR, half_rows), (-FAR, half + FAR), half, s_at, here, coarse, masks)
    for step in range(1, COARSE):
        sweep(
            (step - FAR, half_rows), (step - FAR, half + FAR - step), half,
            here, s_at if step > 1 else None, there, coarse, masks,
        )
        here, there = there, here
    e = here[0]
    finished(loads)

    def add_rows(index, carry):
        row, at = 2 * index + 1, index + FAR
        even = (c_ref[row], ahead_ref[row], behind_ref[row])
        add_share(v, row, e, at, at - 1, even, masks, half)
        odd = (c_ref[row + 1], behind_ref[row + 1], ahead_ref[row + 1])
        add_share(v, row + 1, e, at, at + 1, odd, masks, half)
        return carry

    add_share(v, 0, e, FAR - 1, FAR, (c_ref[0], behind_ref[0], ahead_ref[0]), masks, half)
    lax.fori_loop(0, half_rows, add_rows, 0)
    v_at, g_at = (v, -1, -1), (g, -1, -1)
    group_rows = TILE // tile_groups
    turn = (position[1] & (group_rows - 1), group_rows)
    sweep((0, local_rows), (0, block), block, v_at, g_at, (w, 0, 0), fine, masks, turn)
    stores = []
    for n in range(local_rows // TILE):
        span = slice(n * tile_groups, (n + 1) * tile_groups)
        synthesis_tile(w.at[n * TILE : (n + 1) * TILE], t_high, t_low, o.at[:, span])
        stores += started([(o.at[:, span], o_ref.at[:, span])], out_sems, n)
    finished(stores)


def params(mebibytes, *order):
    return pltpu.CompilerParams(
        dimension_semantics=order or None, vmem_limit_bytes=mebibytes * 1024 * 1024
    )


def cell_body(density):
    local_phi, local_rows, vertical_cells = density.shape
    az_count = lax.axis_size("az")
    azimuths = local_phi * az_count
    block = vertical_cells // az_count
    rows = LANES // block
    tiles = local_rows // TILE
    groups = TILE // rows
    chunks = 2
    chunk_tiles = tiles // chunks
    chunk_rows = local_rows // chunks
    analysis, synthesis = mode_tables(azimuths)
    point = (azimuths // LANES, LANES)
    f32 = jnp.float32
    a_high, a_low = high_low(analysis)
    s_high, s_low = high_low(synthesis)
    order = block_order(az_count)
    product = 2 * 3 * azimuths * azimuths // 2
    lane_tiles = vertical_cells // LANES
    anywhere = pl.BlockSpec(memory_space=pl.ANY)
    in_hbm = pl.BlockSpec(memory_space=pltpu.HBM)

    def field(row_count, cell_count):
        return jax.ShapeDtypeStruct((row_count, cell_count) + point, f32)

    def scratch(row_count, *cell_count):
        return pltpu.VMEM((row_count,) + cell_count + point, f32)

    def semaphores(count):
        return pltpu.SemaphoreType.DMA((count,))

    def cost(mebibytes):
        return pl.CostEstimate(flops=0, bytes_accessed=mebibytes * 1024 * 1024, transcendentals=0)

    def pack(first_tile):
        return pl.pallas_call(
            lambda *refs: pack_kernel(block, order, first_tile, *refs),
            in_specs=[in_hbm],
            out_specs=in_hbm,
            out_shape=jax.ShapeDtypeStruct(
                (az_count, chunk_tiles * groups, local_phi, LANES), f32
            ),
            scratch_shapes=[
                pltpu.VMEM((chunk_tiles, lane_tiles, local_phi, TILE, LANES), f32),
                pltpu.VMEM((az_count, chunk_tiles * groups, local_phi, LANES), f32),
                pltpu.SemaphoreType.DMA((chunk_tiles * lane_tiles,)),
                pltpu.SemaphoreType.DMA((chunk_tiles,)),
            ],
            compiler_params=params(56),
            name="pack",
        )(density)

    half_rows, half = local_rows // 2, block // 2
    all_rows, coarse_rows = DEEP + local_rows, FAR + half_rows
    tables = [pltpu.VMEM((azimuths // 2, azimuths), jnp.bfloat16)] * 2

    def analyse(received, held):
        out_shape = [field(chunk_rows, block)]
        out_shape += [field(all_rows, NEAR)] * 2 if held else [field(DEEP, 2 * NEAR), field(DEEP, block)]
        return pl.pallas_call(
            lambda *refs: analysis_kernel(groups, len(held), *refs),
            in_specs=[in_hbm] * 3 + [anywhere] * len(held),
            out_specs=[anywhere] * len(out_shape),
            out_shape=out_shape,
            scratch_shapes=[
                pltpu.VMEM((az_count, chunk_tiles * groups, local_phi, LANES), f32),
                *tables,
                scratch(chunk_rows, block),
                scratch(all_rows, 2 * NEAR) if held else scratch(DEEP, block),
                semaphores(chunk_tiles),
                semaphores(2),
                semaphores(chunk_rows + 6),
            ],
            compiler_params=params(56),
            cost_estimate=cost(12),
            name="analysis",
        )(received, a_high, a_low, *held)

    def exchange(value):
        return lax.all_to_all(value, "az", split_axis=0, concat_axis=0, tiled=True)

    to_right = [(order[i], order[i + 1]) for i in range(az_count - 1)]
    to_left = [(b, a) for a, b in to_right]

    def from_sides(head, tail):
        return lax.ppermute(tail, "az", to_right), lax.ppermute(head, "az", to_left)

    first_received = exchange(pack(0))
    second_received = exchange(pack(chunk_tiles))
    near, edge_sides, edge = analyse(first_received, ())
    deep_sides = lax.ppermute(edge_sides, "rad", [(0, 1), (1, 0)])
    deep_sides, edge = lax.optimization_barrier((deep_sides, edge))
    deep = lax.ppermute(edge, "rad", [(0, 1), (1, 0)])
    far, head, tail = analyse(second_received, (deep_sides, near))
    fields = (deep, near, far, *from_sides(head, tail))

    wide = 2 * NEAR + 1
    weight_scratch = [scratch(all_rows)] * 3
    u_inner, s_inner = pl.pallas_call(
        lambda *refs: inner_kernel(local_rows, block, *refs),
        in_specs=[anywhere] * 3,
        out_specs=[anywhere] * 2,
        out_shape=[field(local_rows + 2, block - 2), field(coarse_rows, half - 2)],
        scratch_shapes=[
            scratch(all_rows, block),
            scratch(all_rows + 1, block),
            scratch(all_rows, block - 2),
            scratch(coarse_rows, half - 2),
            *weight_scratch,
            semaphores(3),
            semaphores(2),
        ],
        compiler_params=params(28),
        cost_estimate=cost(32),
        name="inner",
    )(*fields[:3])
    u_left, u_right, s_head, s_tail = pl.pallas_call(
        lambda *refs: outer_kernel(local_rows, block, *refs),
        in_specs=[anywhere] * 6,
        out_specs=[anywhere] * 4,
        out_shape=[field(local_rows + 2, NEAR)] * 2 + [field(coarse_rows, FAR)] * 2,
        scratch_shapes=[
            scratch(all_rows, wide),
            scratch(all_rows, wide),
            scratch(all_rows + 1, wide),
            scratch(all_rows + 1, wide),
            scratch(all_rows, wide - 2),
            scratch(all_rows, wide - 2),
            scratch(coarse_rows, 1),
            scratch(coarse_rows, 1),
            scratch(coarse_rows, FAR),
            scratch(coarse_rows, FAR),
            *weight_scratch,
            semaphores(10),
            semaphores(4),
        ],
        compiler_params=params(20),
        cost_estimate=cost(12),
        name="outer",
    )(*fields, s_inner)
    s_parts = (s_inner, s_head, s_tail, *from_sides(s_head, s_tail))

    settled = pl.pallas_call(
        lambda *refs: settle_kernel(local_rows, block, *refs),
        in_specs=[anywhere] * 8,
        out_specs=anywhere,
        out_shape=field(local_rows + 1, block + 2),
        scratch_shapes=[
            scratch(local_rows + 3, block + 4),
            scratch(local_rows + 1, block + 2),
            scratch(local_rows + 1, block + 2),
            *[scratch(local_rows + 1)] * 3,
            semaphores(8),
            semaphores(1),
        ],
        compiler_params=params(24),
        cost_estimate=cost(16),
        name="settle",
    )(u_inner, u_left, u_right, *fields)

    received_shape = (az_count, tiles * groups, local_phi, LANES)
    physical = pl.pallas_call(
        lambda *refs: finish_kernel(local_rows, block, groups, *refs),
        in_specs=[anywhere] * 11 + [in_hbm] * 2,
        out_specs=in_hbm,
        out_shape=jax.ShapeDtypeStruct(received_shape, f32),
        scratch_shapes=[
            scratch(coarse_rows, half + 2 * FAR),
            scratch(coarse_rows + 1, half + 2 * FAR),
            scratch(coarse_rows + 1, half + 2 * FAR),
            scratch(local_rows + 2, block + 2),
            scratch(local_rows + 1, block + 2),
            scratch(local_rows, block),
            pltpu.VMEM(received_shape, f32),
            *tables,
            scratch(local_rows + 1),
            scratch(local_rows + 1),
            scratch(local_rows + 1),
            scratch(coarse_rows),
            scratch(coarse_rows),
            scratch(coarse_rows),
            semaphores(13),
            semaphores(tiles),
        ],
        compiler_params=params(46),
        name="finish",
    )(*s_parts, settled, *fields, s_high, s_low)

    returned = exchange(physical)
    side = jnp.stack([lax.axis_index("rad"), lax.axis_index("az")]).astype(jnp.int32)
    return pl.pallas_call(
        lambda *refs: unpack_kernel(block, order, *refs),
        in_specs=[in_hbm, anywhere],
        out_specs=in_hbm,
        out_shape=jax.ShapeDtypeStruct(density.shape, f32),
        scratch_shapes=[
            pltpu.VMEM((az_count, tiles * groups, local_phi, LANES), f32),
            pltpu.VMEM((tiles, lane_tiles, local_phi, TILE, LANES), f32),
            pltpu.SemaphoreType.DMA((tiles,)),
            pltpu.SemaphoreType.DMA((tiles * lane_tiles,)),
        ],
        compiler_params=params(56),
        name="unpack",
    )(returned, side)


def block_order(az_count):
    return [i ^ 2 if (i // 4) % 2 else i for i in range(az_count)]


def fits_cells(density):
    local_phi, local_rows, vertical_cells = density.shape
    az_count, rad_count = lax.axis_size("az"), lax.axis_size("rad")
    block = vertical_cells // az_count
    return (
        rad_count == 2
        and vertical_cells % (az_count * 2) == 0
        and vertical_cells % LANES == 0
        and LANES // TILE <= block <= LANES
        and LANES % block == 0
        and block // 2 >= FAR
        and local_rows % (4 * TILE) == 0
        and local_rows // 2 >= DEEP
        and az_count % 4 == 0
        and local_phi % TILE == 0
        and (az_count * local_phi) % (2 * LANES) == 0
        and az_count * local_phi == TILE * LANES
    )


def body(density):
    return cell_body(density) if fits_cells(density) else general_body(density)


def solution(mesh):
    placed = (P("az", "rad", None),)
    return jax.shard_map(
        body, mesh=mesh, in_specs=placed, out_specs=P("az", "rad", None), check_vma=False
    )
```

```python
import math

import jax
import jax.numpy as jnp
import numpy as np
from jax import lax
from jax.experimental import pallas as pl
from jax.experimental.pallas import tpu as pltpu
from jax.sharding import PartitionSpec as P

PRE = 2
POST = 2
COARSE = 6


OMEGA = 0.8

LANES = 128
TILE = 8
DEEP = 2 * COARSE + 2
NEAR = 3
FAR = COARSE


def with_halo(cells, sides, width):
    for axis, dim in sides:
        count = lax.axis_size(axis)
        ends = count - 1
        head = lax.slice_in_dim(cells, 0, width, axis=dim)
        tail = lax.slice_in_dim(cells, cells.shape[dim] - width, cells.shape[dim], axis=dim)
        cells = jnp.concatenate(
            [
                lax.ppermute(tail, axis, [(i, (i + 1) % count) for i in range(ends)]),
                cells,
                lax.ppermute(head, axis, [((i + 1) % count, i) for i in range(ends)]),
            ],
            axis=dim,
        )
    return cells


def level_coefficients(first_row, row_count, spacing, mode_numbers):
    row_number = (jnp.arange(row_count, dtype=jnp.int32) + first_row).astype(jnp.float32)
    radius = spacing * (row_number + 0.5)
    outward = (row_number + 1.0) / (spacing * radius)
    inward = row_number / (spacing * radius)
    vertical = 1.0 / (spacing * spacing)
    diagonal = (outward + inward + 2.0 * vertical)[None, :] + (
        mode_numbers[:, None] / radius[None, :]
    ) ** 2
    return (diagonal[:, :, None], outward[None, :, None], inward[None, :, None], vertical)


def apply_op(iterate, padded, coefficients):
    diagonal, outward, inward, vertical = coefficients
    return (
        diagonal * iterate
        - outward * padded[:, 2:, 1:-1]
        - inward * padded[:, :-2, 1:-1]
        - vertical * (padded[:, 1:-1, 2:] + padded[:, 1:-1, :-2])
    )


def relax(iterate, source, coefficients, pad_both):
    return (
        iterate
        + OMEGA * (source - apply_op(iterate, pad_both(iterate), coefficients)) / coefficients[0]
    )


def restrict(residual):
    k_count, r_count, z_count = residual.shape
    parts = residual.reshape(k_count, r_count // 2, 2, z_count // 2, 2)
    return 0.25 * (
        parts[:, :, 0, :, 0] + parts[:, :, 1, :, 0] + parts[:, :, 0, :, 1] + parts[:, :, 1, :, 1]
    )


def prolong(correction):
    return jnp.repeat(jnp.repeat(correction, 2, axis=1), 2, axis=2)


def pad_level(field):
    rows = with_halo(field, (("rad", 1),), 1)
    return jnp.pad(rows, ((0, 0), (0, 0), (1, 1)))


def mode_values(mode_index, azimuths):
    return jnp.where(mode_index <= azimuths // 2, mode_index, mode_index - azimuths // 2).astype(
        jnp.float32
    )


def fine_cycle(source, fine_coef, pad_sweep, coarse_solve):
    iterate = OMEGA * source / fine_coef[0]
    for sweep_index in range(PRE - 1):
        iterate = relax(iterate, source, fine_coef, pad_sweep)
    residual = source - apply_op(iterate, pad_sweep(iterate), fine_coef)
    iterate = iterate + prolong(coarse_solve(restrict(residual)))
    for sweep_index in range(POST):
        iterate = relax(iterate, source, fine_coef, pad_sweep)
    return iterate


def general_body(density):
    local_phi, local_rows, vertical_cells = density.shape
    az_count = lax.axis_size("az")
    azimuths = local_phi * az_count
    cell_count = local_rows * vertical_cells // az_count
    numbers = jnp.arange(azimuths, dtype=jnp.int32)
    all_modes = jnp.where(numbers <= azimuths // 2, numbers, numbers - azimuths // 2)
    phase = all_modes[:, None] * numbers[None, :] % azimuths
    phase_angle = phase.astype(jnp.float32) * (2.0 * math.pi / azimuths)
    analysis_table = jnp.where(
        (numbers <= azimuths // 2)[:, None], jnp.cos(phase_angle), jnp.sin(phase_angle)
    )
    synth_weight = jnp.where(
        (numbers == 0) | (numbers == azimuths // 2), 1.0 / azimuths, 2.0 / azimuths
    )
    synthesis_table = analysis_table.T * synth_weight[None, :]

    def transform_with(table, columns):
        width = columns.shape[2]
        matrix = columns.reshape(azimuths, width)
        result = jnp.dot(
            table, matrix, precision=lax.Precision.HIGHEST, preferred_element_type=jnp.float32
        )
        return result.reshape(azimuths, 1, width)

    lines = density.reshape(local_phi, az_count, cell_count)
    spectral = transform_with(
        analysis_table, lax.all_to_all(lines, "az", split_axis=1, concat_axis=0, tiled=True)
    )
    coefficients = lax.all_to_all(spectral, "az", split_axis=0, concat_axis=1, tiled=True)
    source = -coefficients.reshape(local_phi, local_rows, vertical_cells)
    rad_index = lax.axis_index("rad")
    half_rows = local_rows // 2
    mode_index = lax.axis_index("az") * local_phi + jnp.arange(local_phi, dtype=jnp.int32)
    mode_numbers = mode_values(mode_index, azimuths)
    fine_coef = level_coefficients(rad_index * local_rows, local_rows, 1.0, mode_numbers)
    coarse_coef = level_coefficients(rad_index * half_rows, half_rows, 2.0, mode_numbers)

    def coarse_halo(coarse_source):
        correction = OMEGA * coarse_source / coarse_coef[0]
        for sweep_index in range(COARSE - 1):
            correction = relax(correction, coarse_source, coarse_coef, pad_level)
        return correction

    iterate = fine_cycle(source, fine_coef, pad_level, coarse_halo)
    mode_lines = iterate.reshape(local_phi, az_count, cell_count)
    physical = transform_with(
        synthesis_table, lax.all_to_all(mode_lines, "az", split_axis=1, concat_axis=0, tiled=True)
    )
    field = lax.all_to_all(physical, "az", split_axis=0, concat_axis=1, tiled=True)
    return field.reshape(local_phi, local_rows, vertical_cells)


def mode_tables(azimuths):
    half, quarter = azimuths // 2, azimuths // 4
    fours = np.concatenate([np.arange(0, half + 1, 4), np.arange(4, half, 4)])
    twos = np.concatenate([np.arange(2, half, 4)] * 2)
    odd = np.concatenate([np.arange(1, half, 2)] * 2)
    modes = np.concatenate([fours, twos, odd])
    index = np.arange(quarter)
    is_cos = np.concatenate(
        [index <= quarter // 2, index < quarter // 2, np.arange(half) < quarter]
    )
    angle = 2.0 * np.pi / azimuths * (np.arange(half)[:, None] * modes[None, :] % azimuths)
    values = np.where(is_cos[None, :], np.cos(angle), np.sin(angle))
    weighted = values * (np.where((modes == 0) | (modes == half), 1.0, 2.0) / azimuths)[None, :]
    return -values, weighted


def table_parts(table, azimuths):
    quarter = azimuths // 4
    return [
        (table.at[0:quarter, 0:quarter], 0),
        (table.at[0:quarter, quarter : 2 * quarter], quarter),
        (table.at[:, 2 * quarter :], 2 * quarter),
    ]


def high_low(values):
    values = values.astype(np.float32)
    high = values.astype(jnp.bfloat16)
    low = (values - high.astype(np.float32)).astype(jnp.bfloat16)
    return jnp.asarray(high), jnp.asarray(low)


def split_value(value):
    high = value.astype(jnp.bfloat16)
    return high, (value - high.astype(jnp.float32)).astype(jnp.bfloat16)


def place():
    az = lax.axis_index("az")
    return lax.axis_index("rad"), az ^ (((az >> 2) & 1) << 1), lax.axis_size("az")


def mode_squares(shape):
    half = shape[0] * shape[1] // 2
    quarter, eighth = half // 2, half // 4
    index = lax.broadcasted_iota(jnp.int32, shape, 0) * shape[1] + lax.broadcasted_iota(jnp.int32, shape, 1)
    fours = 4 * jnp.where(index <= eighth, index, index - eighth)
    twos = 4 * (index & (eighth - 1)) + 2
    odd = 2 * (index & (quarter - 1)) + 1
    modes = jnp.where(index < quarter, fours, jnp.where(index < half, twos, odd))
    return (modes * modes).astype(jnp.float32)


def row_tile(position, local_rows, tile):
    return jnp.where(position[0] == 0, local_rows // TILE - 1 - tile, tile)


def chunk_masks(count, shape):
    lane = lax.broadcasted_iota(jnp.int32, shape, len(shape) - 1) // (LANES // count)
    return [lane == p for p in range(1, count)]


def pick_chunks(parts, masks):
    result = parts[0]
    for part, mask in zip(parts[1:], masks):
        result = jnp.where(mask, part, result)
    return result


def gather_rows(parts, masks):
    count = len(parts)
    chunk = LANES // count
    turned = [pltpu.roll(part, i * chunk, 1) if i else part for i, part in enumerate(parts)]
    return [pick_chunks([turned[(p - q) % count] for p in range(count)], masks) for q in range(count)]


def scatter_rows(parts, masks):
    count = len(parts)
    chunk = LANES // count
    rows = [pick_chunks([parts[(p - i) % count] for p in range(count)], masks) for i in range(count)]
    return [pltpu.roll(row, LANES - i * chunk, 1) if i else row for i, row in enumerate(rows)]


def turned_row(row, turn, rows):
    low = row & (rows - 1)
    return row - low + ((low + turn) & (rows - 1))


def tile_row(position, row):
    return jnp.where(position[0] == 0, TILE - 1 - row, row)


def pack_kernel(block, order, first_tile, x_ref, o_ref, x, o, in_sems, out_sems):
    position = place()
    rows = LANES // block
    local_phi, local_rows, cells = x_ref.shape
    tiles, lane_tiles, groups = x.shape[0], x.shape[1], TILE // rows
    pieces = [(j, k) for j in range(tiles) for k in range(lane_tiles)]
    masks = chunk_masks(rows, (local_phi, LANES))
    loads, stores = [], []
    for n, (j, k) in enumerate(pieces):
        start = pl.multiple_of(row_tile(position, local_rows, first_tile + j) * TILE, TILE)
        source = x_ref.at[:, pl.ds(start, TILE), k * LANES : (k + 1) * LANES]
        loads.append(pltpu.make_async_copy(source, x.at[j, k], in_sems.at[n]))
        loads[-1].start()
    for n, (j, k) in enumerate(pieces):
        loads[n].wait()
        flat = x.at[j, k].reshape(local_phi * TILE, LANES)
        for group in range(groups):
            parts = [
                flat[pl.ds(tile_row(position, group * rows + i), local_phi, stride=TILE), :]
                for i in range(rows)
            ]
            for q, part in enumerate(gather_rows(parts, masks)):
                o[order[k * rows + q], j * groups + group] = part
        if k == lane_tiles - 1:
            span = slice(j * groups, (j + 1) * groups)
            stores.append(pltpu.make_async_copy(o.at[:, span], o_ref.at[:, span], out_sems.at[j]))
            stores[-1].start()
    for store in stores:
        store.wait()


def unpack_kernel(block, order, x_ref, _, o_ref, x, o, in_sems, out_sems):
    position = place()
    rows = LANES // block
    local_phi, local_rows, cells = o_ref.shape
    tiles, lane_tiles, groups = o.shape[0], o.shape[1], TILE // rows
    masks = chunk_masks(rows, (local_phi, LANES))
    loads, stores = [], []
    for j in range(tiles):
        span = slice(j * groups, (j + 1) * groups)
        loads.append(pltpu.make_async_copy(x_ref.at[:, span], x.at[:, span], in_sems.at[j]))
        loads[-1].start()
    for j in range(tiles):
        loads[j].wait()
        start = pl.multiple_of(row_tile(position, local_rows, j) * TILE, TILE)
        for k in range(lane_tiles):
            flat = o.at[j, k].reshape(local_phi * TILE, LANES)
            for group in range(groups):
                parts = [x[order[k * rows + q], j * groups + group] for q in range(rows)]
                for i, part in enumerate(scatter_rows(parts, masks)):
                    at = tile_row(position, group * rows + i)
                    flat[pl.ds(at, local_phi, stride=TILE), :] = part
            target = o_ref.at[:, pl.ds(start, TILE), k * LANES : (k + 1) * LANES]
            stores.append(
                pltpu.make_async_copy(o.at[j, k], target, out_sems.at[j * lane_tiles + k])
            )
            stores[-1].start()
    for store in stores:
        store.wait()


def started(pairs, sems, first=0):
    copies = []
    for n, (src, dst) in enumerate(pairs):
        copies.append(pltpu.make_async_copy(src, dst, sems.at[first + n]))
        copies[-1].start()
    return copies


def finished(copies):
    for copy in copies:
        copy.wait()


def sides_of(field, depth):
    cells = field.shape[1]
    return field, field.at[:, :depth], field.at[:, cells - depth : cells]


def analysis_kernel(tile_groups, held_count, *refs):
    position = place()
    x_ref, high_ref, low_ref = refs[:3]
    outs = refs[3:-8]
    x, t_high, t_low, o, edge, in_sems, t_sems, out_sems = refs[-8:]
    held_refs, outs = outs[:held_count], outs[held_count:]
    sources, width, lanes = x.shape[0], x.shape[2], x.shape[3]
    cells = o.shape[1]
    half = sources // 2 * width
    tiles = x.shape[1] // tile_groups
    spans = [slice(n * tile_groups, (n + 1) * tile_groups) for n in range(tiles)]
    pairs = [(x_ref.at[:, span], x.at[:, span]) for span in spans]
    tables = started([(high_ref, t_high), (low_ref, t_low)], t_sems)
    loads = started(pairs, in_sems)
    group_rows = TILE // tile_groups
    turn = position[1] & (group_rows - 1)
    gathers, start = [], 0
    for held in held_refs:
        span = slice(start, start + held.shape[0])
        if held.shape[1] == 2 * NEAR:
            pairs = [(held, edge.at[span])]
        else:
            sides = zip(sides_of(held, NEAR)[1:], (slice(0, NEAR), slice(NEAR, 2 * NEAR)))
            pairs = [(side, edge.at[span, columns]) for side, columns in sides]
        gathers += started(pairs, out_sems, out_sems.shape[0] - 4 + len(gathers))
        start += held.shape[0]
    stores = []
    for n in range(tiles):
        loads[n].wait()
        turned = [[], [], []]
        for group in range(n * tile_groups, (n + 1) * tile_groups):
            near = x[: sources // 2, group].reshape(half, lanes)
            far = x[sources // 2 :, group].reshape(half, lanes)
            even = near + far
            low_half, high_half = even[: half // 2], even[half // 2 :]
            for part, folded in zip(turned, (low_half + high_half, low_half - high_half, near - far)):
                part.append(folded.T)
        parts = [split_value(jnp.concatenate(part, axis=0)) for part in turned]
        if n == 0:
            finished(tables)
        rows = slice(n * TILE, (n + 1) * TILE)
        columns = zip(parts, table_parts(t_high, 2 * half), table_parts(t_low, 2 * half))
        for (high, low), (part_high, first), (part_low, _) in columns:
            result = (
                jnp.dot(high, part_high[...], preferred_element_type=jnp.float32)
                + jnp.dot(high, part_low[...], preferred_element_type=jnp.float32)
                + jnp.dot(low, part_high[...], preferred_element_type=jnp.float32)
            )
            for part in range(result.shape[1] // LANES):
                piece = result[:, part * LANES : (part + 1) * LANES]
                o[rows, :, first // LANES + part, :] = piece.reshape(TILE, cells, LANES)
        pairs = [
            (o.at[turned_row(row, turn, group_rows)], outs[0].at[row])
            for row in range(n * TILE, (n + 1) * TILE)
        ]
        stores += started(pairs, out_sems, len(stores))
    if held_refs:
        finished(gathers)
        for row in range(o.shape[0]):
            at = turned_row(row, turn, group_rows)
            edge[start + row, :NEAR] = o[at, :NEAR]
            edge[start + row, NEAR:] = o[at, cells - NEAR :]
        pairs = [(edge.at[:, :NEAR], outs[1]), (edge.at[:, NEAR:], outs[2])]
        stores += started(pairs, out_sems, len(stores))
    else:
        for row in range(DEEP):
            edge[DEEP - 1 - row] = o[turned_row(row, turn, group_rows)]
        _, head, tail = sides_of(edge, NEAR)
        pairs = [(head, outs[1].at[:, :NEAR]), (tail, outs[1].at[:, NEAR:]), (edge, outs[2])]
        stores += started(pairs, out_sems, len(stores))
    finished(stores)


def synthesis_tile(u, t_high, t_low, o):
    rows, cells = u.shape[0], u.shape[1]
    half = t_high.shape[0]
    contract = (((1,), (1,)), ((), ()))
    sums = []
    for (part_high, first), (part_low, _) in zip(table_parts(t_high, 2 * half), table_parts(t_low, 2 * half)):
        parts = range(first // LANES, (first + part_high.shape[1]) // LANES)
        field = jnp.concatenate([u[:, :, i, :].reshape(rows * cells, LANES) for i in parts], axis=1)
        high, low = split_value(field)
        sums.append(
            lax.dot_general(part_high[...], high, contract, preferred_element_type=jnp.float32)
            + lax.dot_general(part_high[...], low, contract, preferred_element_type=jnp.float32)
            + lax.dot_general(part_low[...], high, contract, preferred_element_type=jnp.float32)
        )
    fours, twos, odd = sums
    even = jnp.concatenate([fours + twos, fours - twos], axis=0)
    near, far = even + odd, even - odd
    targets, groups, width, lanes = o.shape
    for group in range(groups):
        columns = slice(group * lanes, (group + 1) * lanes)
        o[: targets // 2, group] = near[:, columns].reshape(targets // 2, width, lanes)
        o[targets // 2 :, group] = far[:, columns].reshape(targets // 2, width, lanes)


def row_weights(upper, boundary, first, count, squares, c_ref, ahead_ref, behind_ref):
    def one(index, carry):
        row = jnp.where(upper, index + (boundary + first), (boundary - 1 - first) - index)
        number = jnp.full(squares.shape, row, jnp.int32).astype(jnp.float32)
        radius = number + 0.5
        outward = (number + 1.0) / radius
        inward = number / radius
        diagonal = outward + inward + 2.0 + squares / (radius * radius)
        c_ref[index] = OMEGA / diagonal
        ahead_ref[index] = jnp.where(upper, outward, inward)
        behind_ref[index] = jnp.where(upper, inward, outward)
        return carry

    lax.fori_loop(0, count, one, 0)


def cell_tiles(first, last, cells, size=16):
    tiles = []
    if first < 0:
        tiles.append((first, -first, -1))
    for start in range(max(first, 0), min(last, cells), size):
        tiles.append((start, min(size, min(last, cells) - start), 0))
    if last > cells:
        tiles.append((cells, last - cells, 1))
    return tiles


def run_rows(count, *bodies, together=4):
    rest = count % together

    def several(index, carry):
        for row in range(together):
            for body in bodies:
                body(together * index + (rest + row), None)
        return carry

    for row in range(rest):
        for body in bodies:
            body(row, None)
    lax.fori_loop(0, count // together, several, 0)


def sweep(*args):
    run_rows(*sweep_rows(*args))


def first_sweep(*args):
    run_rows(*first_sweep_rows(*args))


def sweep_rows(rows, cells, block, src, source, dst, weights, masks, turn=None):
    (src_ref, src_t, src_z), (dst_ref, dst_t, dst_z) = src, dst
    keep = 1.0 - OMEGA if source else 2.0 - OMEGA
    c_ref, ahead_ref, behind_ref, w_t = weights
    low = rows[0]

    def one(step, carry):
        at = step + (low - w_t)
        target = step + (low - dst_t)
        if turn:
            target = turned_row(target, *turn)
        c_row, ahead, behind = c_ref[at], ahead_ref[at], behind_ref[at]
        for first, count, side in cell_tiles(cells[0], cells[1], block):
            c = c_row if side == 0 else c_row * masks[0 if side < 0 else 1]
            z = first - src_z
            row = low - src_t
            middle = src_ref[step + row, z - 1 : z + count + 1]
            gathered = (
                ahead * src_ref[step + (row + 1), z : z + count]
                + behind * src_ref[step + (row - 1), z : z + count]
                + (middle[:-2] + middle[2:])
            )
            if source:
                g_ref, g_t, g_z = source
                gathered += g_ref[step + (low - g_t), first - g_z : first - g_z + count]
            dst_ref[target, first - dst_z : first - dst_z + count] = (
                keep * middle[1:-1] + c * gathered
            )
        return carry

    return rows[1] - low, one


def first_sweep_rows(rows, cells, block, source, dst, weights, masks):
    (g_ref, g_t, g_z), (dst_ref, dst_t, dst_z) = source, dst
    c_ref, w_t = weights[0], weights[3]
    low = rows[0]

    def one(step, carry):
        c_row = c_ref[step + (low - w_t)]
        for first, count, side in cell_tiles(cells[0], cells[1], block):
            c = c_row if side == 0 else c_row * masks[0 if side < 0 else 1]
            dst_ref[step + (low - dst_t), first - dst_z : first - dst_z + count] = (
                c * g_ref[step + (low - g_t), first - g_z : first - g_z + count]
            )
        return carry

    return rows[1] - low, one


def side_masks(position, shape):
    left = jnp.full(shape, position[1] > 0).astype(jnp.float32)
    right = jnp.full(shape, position[1] < position[2] - 1).astype(jnp.float32)
    return left, right


def smooth_columns(local_rows, block, strips, weights, masks):
    first = -DEEP
    firsts, seconds, restricts = [], [], []
    for cells, g, u1, u2, s in strips:
        low, high = cells
        g_at, u1_at, u2_at = (g, first, low), (u1, first, low), (u2, first + 1, low + 1)
        total = g.shape[0]
        u1[total] = jnp.zeros(u1.shape[1:], jnp.float32)
        u2[total - 1] = jnp.zeros(u2.shape[1:], jnp.float32)
        firsts.append(first_sweep_rows((first, local_rows), cells, block, g_at, u1_at, weights, masks))
        rows, inside = (first + 1, local_rows), (low + 1, high - 1)
        seconds.append(sweep_rows(rows, inside, block, u1_at, None, u2_at, weights, masks))
        restricts.append(restrict_rows(cells, block, g, u2, s, weights))
    for stage in (firsts, seconds, restricts):
        run_rows(stage[0][0], *[body for _, body in stage])


def restrict_rows(cells, block, g, u2, s, weights):
    low = cells[0]
    c_ref, ahead_ref, behind_ref, _ = weights
    start = max(low + 2, 0)
    start += start % 2

    def paired(values):
        pairs = values.reshape(values.shape[0] // 2, 2, *values.shape[1:])
        return pairs[:, 0], pairs[:, 1]

    def pair_sums(values):
        even, odd = paired(values)
        return even + odd

    def restrict_row(index, carry):
        row = 2 * index + (DEEP - 2 * FAR)
        center = behind_ref[row + 1] - OMEGA / c_ref[row] + 1.0
        center_ahead = ahead_ref[row] - OMEGA / c_ref[row + 1] + 1.0
        behind, ahead = behind_ref[row], ahead_ref[row + 1]
        for at, count, _ in cell_tiles(start, start + 2 * s.shape[1], block):
            z = at - (low + 1)
            here = u2[row - 1, z - 1 : z + count + 1]
            there = u2[row, z - 1 : z + count + 1]
            even, odd = paired(here + there)
            cells = slice(at - low, at - low + count)
            column = (at - start) // 2
            s[index, column : column + count // 2] = (
                pair_sums(g[row, cells] + g[row + 1, cells])
                + (even[:-1] + odd[1:])
                + behind * pair_sums(u2[row - 2, z : z + count])
                + center * pair_sums(here[1:-1])
                + center_ahead * pair_sums(there[1:-1])
                + ahead * pair_sums(u2[row + 1, z : z + count])
            )
        return carry

    return s.shape[0], restrict_row


def inner_kernel(
    local_rows, block, deep_ref, near_ref, far_ref, u_ref, s_ref,
    g, u1, u2, s, c_ref, ahead_ref, behind_ref, in_sems, out_sems,
):
    pairs, start = [], 0
    for ref in (deep_ref, near_ref, far_ref):
        pairs.append((ref, g.at[start : start + ref.shape[0]]))
        start += ref.shape[0]
    loads = started(pairs, in_sems)
    position, squares = place(), mode_squares(c_ref.shape[1:])
    upper = position[0] == 1
    row_weights(upper, local_rows, -DEEP, DEEP + local_rows, squares, c_ref, ahead_ref, behind_ref)
    weights = (c_ref, ahead_ref, behind_ref, -DEEP)
    finished(loads)
    smooth_columns(local_rows, block, [((0, block), g, u1, u2, s)], weights, None)
    pairs = [(u2.at[DEEP - 3 : DEEP - 1 + local_rows], u_ref), (s, s_ref)]
    finished(started(pairs, out_sems))


def outer_kernel(
    local_rows, block,
    deep_ref, near_ref, far_ref, left_ref, right_ref, inner_ref,
    u_left_ref, u_right_ref, head_ref, tail_ref,
    g_left, g_right, u1_left, u1_right, u2_left, u2_right, s_left, s_right, head, tail,
    c_ref, ahead_ref, behind_ref, in_sems, out_sems,
):
    wide = g_left.shape[1]
    own = wide - NEAR
    pairs, start = [], 0
    for ref in (deep_ref, near_ref, far_ref):
        span = slice(start, start + ref.shape[0])
        pairs.append((ref.at[:, :own], g_left.at[span, NEAR:]))
        pairs.append((ref.at[:, block - own :], g_right.at[span, :own]))
        start = span.stop
    pairs += [(left_ref, g_left.at[:, :NEAR]), (right_ref, g_right.at[:, own:])]
    inner = inner_ref.shape[1]
    pairs += [(inner_ref.at[:, : FAR - 1], head.at[:, 1:])]
    pairs += [(inner_ref.at[:, inner - FAR + 1 :], tail.at[:, : FAR - 1])]
    loads = started(pairs, in_sems)
    position, squares = place(), mode_squares(c_ref.shape[1:])
    upper = position[0] == 1
    row_weights(upper, local_rows, -DEEP, DEEP + local_rows, squares, c_ref, ahead_ref, behind_ref)
    masks = side_masks(position, squares.shape)
    weights = (c_ref, ahead_ref, behind_ref, -DEEP)
    finished(loads)
    rows = slice(DEEP - 3, DEEP - 1 + local_rows)
    strips = [
        ((-NEAR, own), g_left, u1_left, u2_left, s_left),
        ((block - own, block + NEAR), g_right, u1_right, u2_right, s_right),
    ]
    smooth_columns(local_rows, block, strips, weights, masks)
    head[:, 0] = s_left[:, 0]
    tail[:, FAR - 1] = s_right[:, 0]
    pairs = [(head, head_ref), (tail, tail_ref), (u2_left.at[rows, :NEAR], u_left_ref)]
    pairs.append((u2_right.at[rows, wide - 2 - NEAR :], u_right_ref))
    finished(started(pairs, out_sems))


def field_pairs(g_refs, g):
    pairs, start = [], 0
    local_rows, middle = g.shape[0] - 1, slice(1, g.shape[1] - 1)
    for ref in g_refs[:3]:
        rows = slice(DEEP - 1, DEEP) if start == 0 else slice(0, ref.shape[0])
        count = rows.stop - rows.start
        pairs.append((ref.at[rows], g.at[start : start + count, middle]))
        start += count
    rows = slice(DEEP - 1, DEEP + local_rows)
    pairs.append((g_refs[3].at[rows, NEAR - 1 : NEAR], g.at[:, 0:1]))
    pairs.append((g_refs[4].at[rows, 0:1], g.at[:, middle.stop : middle.stop + 1]))
    return pairs


def settle_kernel(
    local_rows, block, inner_ref, left_ref, right_ref, *refs
):
    g_refs = refs[:5]
    v_ref, u, g, v, c_ref, ahead_ref, behind_ref, in_sems, out_sems = refs[5:]
    rows = slice(0, local_rows + 2)
    pairs = [
        (left_ref, u.at[rows, :NEAR]),
        (inner_ref, u.at[rows, NEAR : NEAR + block - 2]),
        (right_ref, u.at[rows, NEAR + block - 2 :]),
    ]
    loads = started(pairs + field_pairs(g_refs, g), in_sems)
    position, squares = place(), mode_squares(c_ref.shape[1:])
    masks = side_masks(position, squares.shape)
    upper = position[0] == 1
    row_weights(upper, local_rows, -1, 1 + local_rows, squares, c_ref, ahead_ref, behind_ref)
    u[2 + local_rows] = jnp.zeros(u.shape[1:], jnp.float32)
    finished(loads)
    u_at, v_at, g_at = (u, -2, -2), (v, -1, -1), (g, -1, -1)
    weights = (c_ref, ahead_ref, behind_ref, -1)
    sweep((-1, local_rows), (-1, block + 1), block, u_at, g_at, v_at, weights, masks)
    finished(started([(v, v_ref)], out_sems))


def add_share(v, row, e, here, other, weights, masks, half):
    c, stay, cross = weights
    keep = 1.0 - OMEGA
    count = half // 2
    for first in (0, count):
        line = e[here, FAR + first - 1 : FAR + first + count + 1]
        common = (keep + c * stay + c) * line[1:-1] + (c * cross) * e[other, FAR + first : FAR + first + count]
        beside = c * line
        pairs = jnp.stack([common + beside[:-2], common + beside[2:]], axis=1)
        cells = slice(1 + 2 * first, 1 + 2 * (first + count))
        v[row, cells] = v[row, cells] + pairs.reshape(2 * count, *pairs.shape[2:])
    for near, beside, cell, mask in (
        (FAR - 1, FAR, 0, masks[0]), (FAR + half, FAR + half - 1, 2 * half + 1, masks[1]),
    ):
        c_side = c * mask
        v[row, cell] = v[row, cell] + (
            (keep + c_side * stay + c_side) * e[here, near]
            + (c_side * cross) * e[other, near]
            + c_side * e[here, beside]
        )


def finish_kernel(local_rows, block, tile_groups, *refs):
    (
        high_ref, low_ref, o_ref,
        s, e0, e1, v, g, w, o, t_high, t_low,
        c_ref, ahead_ref, behind_ref, cc_ref, cahead_ref, cbehind_ref, in_sems, out_sems,
    ) = refs[-20:]
    s_inner, s_head, s_tail, s_left, s_right, v_ref = refs[:6]
    position, squares = place(), mode_squares(c_ref.shape[1:])
    upper = position[0] == 1
    half_rows, half = local_rows // 2, block // 2
    pairs = [
        (s_inner, s.at[:, FAR + 1 : FAR + half - 1]),
        (s_head.at[:, 0:1], s.at[:, FAR : FAR + 1]),
        (s_tail.at[:, FAR - 1 : FAR], s.at[:, FAR + half - 1 : FAR + half]),
        (s_left, s.at[:, 0:FAR]),
        (s_right, s.at[:, FAR + half : FAR + half + FAR]),
    ]
    s_loads = started(pairs, in_sems)
    pairs = [(v_ref, v.at[: local_rows + 1])] + field_pairs(refs[6:11], g)
    pairs += [(high_ref, t_high), (low_ref, t_low)]
    loads = started(pairs, in_sems, len(s_loads))
    masks = side_masks(position, squares.shape)
    row_weights(upper, half_rows, -FAR, FAR + half_rows, squares, cc_ref, cahead_ref, cbehind_ref)
    row_weights(upper, local_rows, -1, 1 + local_rows, squares, c_ref, ahead_ref, behind_ref)
    coarse = (cc_ref, cahead_ref, cbehind_ref, -FAR)
    fine = (c_ref, ahead_ref, behind_ref, -1)
    for buffer in (e0, e1):
        buffer[FAR + half_rows] = jnp.zeros(buffer.shape[1:], jnp.float32)
    v[1 + local_rows] = jnp.zeros(v.shape[1:], jnp.float32)
    finished(s_loads)
    s_at = (s, -FAR, -FAR)
    here, there = (e0, -FAR, -FAR), (e1, -FAR, -FAR)
    first_sweep((-FAR, half_rows), (-FAR, half + FAR), half, s_at, here, coarse, masks)
    for step in range(1, COARSE):
        sweep(
            (step - FAR, half_rows), (step - FAR, half + FAR - step), half,
            here, s_at if step > 1 else None, there, coarse, masks,
        )
        here, there = there, here
    e = here[0]
    finished(loads)

    def add_rows(index, carry):
        row, at = 2 * index + 1, index + FAR
        even = (c_ref[row], ahead_ref[row], behind_ref[row])
        add_share(v, row, e, at, at - 1, even, masks, half)
        odd = (c_ref[row + 1], behind_ref[row + 1], ahead_ref[row + 1])
        add_share(v, row + 1, e, at, at + 1, odd, masks, half)
        return carry

    add_share(v, 0, e, FAR - 1, FAR, (c_ref[0], behind_ref[0], ahead_ref[0]), masks, half)
    lax.fori_loop(0, half_rows, add_rows, 0)
    v_at, g_at = (v, -1, -1), (g, -1, -1)
    group_rows = TILE // tile_groups
    turn = (position[1] & (group_rows - 1), group_rows)
    sweep((0, local_rows), (0, block), block, v_at, g_at, (w, 0, 0), fine, masks, turn)
    stores = []
    for n in range(local_rows // TILE):
        span = slice(n * tile_groups, (n + 1) * tile_groups)
        synthesis_tile(w.at[n * TILE : (n + 1) * TILE], t_high, t_low, o.at[:, span])
        stores += started([(o.at[:, span], o_ref.at[:, span])], out_sems, n)
    finished(stores)


def params(mebibytes, *order):
    return pltpu.CompilerParams(
        dimension_semantics=order or None, vmem_limit_bytes=mebibytes * 1024 * 1024
    )


def cell_body(density):
    local_phi, local_rows, vertical_cells = density.shape
    az_count = lax.axis_size("az")
    azimuths = local_phi * az_count
    block = vertical_cells // az_count
    rows = LANES // block
    tiles = local_rows // TILE
    groups = TILE // rows
    chunks = 2
    chunk_tiles = tiles // chunks
    chunk_rows = local_rows // chunks
    analysis, synthesis = mode_tables(azimuths)
    point = (azimuths // LANES, LANES)
    f32 = jnp.float32
    a_high, a_low = high_low(analysis)
    s_high, s_low = high_low(synthesis)
    order = block_order(az_count)
    product = 2 * 3 * azimuths * azimuths // 2
    lane_tiles = vertical_cells // LANES
    anywhere = pl.BlockSpec(memory_space=pl.ANY)
    in_hbm = pl.BlockSpec(memory_space=pltpu.HBM)

    def field(row_count, cell_count):
        return jax.ShapeDtypeStruct((row_count, cell_count) + point, f32)

    def scratch(row_count, *cell_count):
        return pltpu.VMEM((row_count,) + cell_count + point, f32)

    def semaphores(count):
        return pltpu.SemaphoreType.DMA((count,))

    def cost(mebibytes):
        return pl.CostEstimate(flops=0, bytes_accessed=mebibytes * 1024 * 1024, transcendentals=0)

    def pack(first_tile):
        return pl.pallas_call(
            lambda *refs: pack_kernel(block, order, first_tile, *refs),
            in_specs=[in_hbm],
            out_specs=in_hbm,
            out_shape=jax.ShapeDtypeStruct(
                (az_count, chunk_tiles * groups, local_phi, LANES), f32
            ),
            scratch_shapes=[
                pltpu.VMEM((chunk_tiles, lane_tiles, local_phi, TILE, LANES), f32),
                pltpu.VMEM((az_count, chunk_tiles * groups, local_phi, LANES), f32),
                pltpu.SemaphoreType.DMA((chunk_tiles * lane_tiles,)),
                pltpu.SemaphoreType.DMA((chunk_tiles,)),
            ],
            compiler_params=params(56),
            name="pack",
        )(density)

    half_rows, half = local_rows // 2, block // 2
    all_rows, coarse_rows = DEEP + local_rows, FAR + half_rows
    tables = [pltpu.VMEM((azimuths // 2, azimuths), jnp.bfloat16)] * 2

    def analyse(received, held):
        out_shape = [field(chunk_rows, block)]
        out_shape += [field(all_rows, NEAR)] * 2 if held else [field(DEEP, 2 * NEAR), field(DEEP, block)]
        return pl.pallas_call(
            lambda *refs: analysis_kernel(groups, len(held), *refs),
            in_specs=[in_hbm] * 3 + [anywhere] * len(held),
            out_specs=[anywhere] * len(out_shape),
            out_shape=out_shape,
            scratch_shapes=[
                pltpu.VMEM((az_count, chunk_tiles * groups, local_phi, LANES), f32),
                *tables,
                scratch(chunk_rows, block),
                scratch(all_rows, 2 * NEAR) if held else scratch(DEEP, block),
                semaphores(chunk_tiles),
                semaphores(2),
                semaphores(chunk_rows + 6),
            ],
            compiler_params=params(56),
            cost_estimate=cost(12),
            name="analysis",
        )(received, a_high, a_low, *held)

    def exchange(value):
        return lax.all_to_all(value, "az", split_axis=0, concat_axis=0, tiled=True)

    to_right = [(order[i], order[i + 1]) for i in range(az_count - 1)]
    to_left = [(b, a) for a, b in to_right]

    def from_sides(head, tail):
        return lax.ppermute(tail, "az", to_right), lax.ppermute(head, "az", to_left)

    first_received = exchange(pack(0))
    second_received = exchange(pack(chunk_tiles))
    near, edge_sides, edge = analyse(first_received, ())
    deep_sides = lax.ppermute(edge_sides, "rad", [(0, 1), (1, 0)])
    deep_sides, edge = lax.optimization_barrier((deep_sides, edge))
    deep = lax.ppermute(edge, "rad", [(0, 1), (1, 0)])
    far, head, tail = analyse(second_received, (deep_sides, near))
    fields = (deep, near, far, *from_sides(head, tail))

    wide = 2 * NEAR + 1
    weight_scratch = [scratch(all_rows)] * 3
    u_inner, s_inner = pl.pallas_call(
        lambda *refs: inner_kernel(local_rows, block, *refs),
        in_specs=[anywhere] * 3,
        out_specs=[anywhere] * 2,
        out_shape=[field(local_rows + 2, block - 2), field(coarse_rows, half - 2)],
        scratch_shapes=[
            scratch(all_rows, block),
            scratch(all_rows + 1, block),
            scratch(all_rows, block - 2),
            scratch(coarse_rows, half - 2),
            *weight_scratch,
            semaphores(3),
            semaphores(2),
        ],
        compiler_params=params(28),
        cost_estimate=cost(32),
        name="inner",
    )(*fields[:3])
    u_left, u_right, s_head, s_tail = pl.pallas_call(
        lambda *refs: outer_kernel(local_rows, block, *refs),
        in_specs=[anywhere] * 6,
        out_specs=[anywhere] * 4,
        out_shape=[field(local_rows + 2, NEAR)] * 2 + [field(coarse_rows, FAR)] * 2,
        scratch_shapes=[
            scratch(all_rows, wide),
            scratch(all_rows, wide),
            scratch(all_rows + 1, wide),
            scratch(all_rows + 1, wide),
            scratch(all_rows, wide - 2),
            scratch(all_rows, wide - 2),
            scratch(coarse_rows, 1),
            scratch(coarse_rows, 1),
            scratch(coarse_rows, FAR),
            scratch(coarse_rows, FAR),
            *weight_scratch,
            semaphores(10),
            semaphores(4),
        ],
        compiler_params=params(20),
        cost_estimate=cost(12),
        name="outer",
    )(*fields, s_inner)
    s_parts = (s_inner, s_head, s_tail, *from_sides(s_head, s_tail))

    settled = pl.pallas_call(
        lambda *refs: settle_kernel(local_rows, block, *refs),
        in_specs=[anywhere] * 8,
        out_specs=anywhere,
        out_shape=field(local_rows + 1, block + 2),
        scratch_shapes=[
            scratch(local_rows + 3, block + 4),
            scratch(local_rows + 1, block + 2),
            scratch(local_rows + 1, block + 2),
            *[scratch(local_rows + 1)] * 3,
            semaphores(8),
            semaphores(1),
        ],
        compiler_params=params(24),
        cost_estimate=cost(16),
        name="settle",
    )(u_inner, u_left, u_right, *fields)

    received_shape = (az_count, tiles * groups, local_phi, LANES)
    physical = pl.pallas_call(
        lambda *refs: finish_kernel(local_rows, block, groups, *refs),
        in_specs=[anywhere] * 11 + [in_hbm] * 2,
        out_specs=in_hbm,
        out_shape=jax.ShapeDtypeStruct(received_shape, f32),
        scratch_shapes=[
            scratch(coarse_rows, half + 2 * FAR),
            scratch(coarse_rows + 1, half + 2 * FAR),
            scratch(coarse_rows + 1, half + 2 * FAR),
            scratch(local_rows + 2, block + 2),
            scratch(local_rows + 1, block + 2),
            scratch(local_rows, block),
            pltpu.VMEM(received_shape, f32),
            *tables,
            scratch(local_rows + 1),
            scratch(local_rows + 1),
            scratch(local_rows + 1),
            scratch(coarse_rows),
            scratch(coarse_rows),
            scratch(coarse_rows),
            semaphores(13),
            semaphores(tiles),
        ],
        compiler_params=params(46),
        name="finish",
    )(*s_parts, settled, *fields, s_high, s_low)

    returned = exchange(physical)
    side = jnp.stack([lax.axis_index("rad"), lax.axis_index("az")]).astype(jnp.int32)
    return pl.pallas_call(
        lambda *refs: unpack_kernel(block, order, *refs),
        in_specs=[in_hbm, anywhere],
        out_specs=in_hbm,
        out_shape=jax.ShapeDtypeStruct(density.shape, f32),
        scratch_shapes=[
            pltpu.VMEM((az_count, tiles * groups, local_phi, LANES), f32),
            pltpu.VMEM((tiles, lane_tiles, local_phi, TILE, LANES), f32),
            pltpu.SemaphoreType.DMA((tiles,)),
            pltpu.SemaphoreType.DMA((tiles * lane_tiles,)),
        ],
        compiler_params=params(56),
        name="unpack",
    )(returned, side)


def block_order(az_count):
    return [i ^ 2 if (i // 4) % 2 else i for i in range(az_count)]


def fits_cells(density):
    local_phi, local_rows, vertical_cells = density.shape
    az_count, rad_count = lax.axis_size("az"), lax.axis_size("rad")
    block = vertical_cells // az_count
    return (
        rad_count == 2
        and vertical_cells % (az_count * 2) == 0
        and vertical_cells % LANES == 0
        and LANES // TILE <= block <= LANES
        and LANES % block == 0
        and block // 2 >= FAR
        and local_rows % (4 * TILE) == 0
        and local_rows // 2 >= DEEP
        and az_count % 4 == 0
        and local_phi % TILE == 0
        and (az_count * local_phi) % (2 * LANES) == 0
        and az_count * local_phi == TILE * LANES
    )


def body(density):
    return cell_body(density) if fits_cells(density) else general_body(density)


def solution(mesh):
    placed = (P("az", "rad", None),)
    return jax.shard_map(
        body, mesh=mesh, in_specs=placed, out_specs=P("az", "rad", None), check_vma=False
    )
```
